32 devices in a mesh: grp: 1, tm: 16 (over z, y, x), chan: 2 (over core).
Axes of the slice: x: 2, y: 2, z: 4, core: 2. Of those that a mesh axis runs over, the one named last changes fastest.
Arguments:
- signal: float32 [131072, 256], P(('grp', 'tm'), 'chan'), may hold values from -6 to 6
- kernel: float32 [131072, 256], P('tm', 'chan'), may hold values from -0.015625 to 0.015625
- skip_gain: float32 [256], replicated, may hold values from -4 to 4
- gate_input: float32 [131072, 256], P(('grp', 'tm', 'chan')), may hold values from -6 to 6
- tap_weight: float32 [256, 254], replicated, may hold values from -0.03125 to 0.03125
- norm_gain: float32 [256], replicated, may hold values from 0.5 to 2
- up_weight: float32 [256, 1024], replicated, may hold values from -0.375 to 0.375
- up_bias: float32 [1024], replicated, may hold values from -4 to 4
- down_weight: float32 [1024, 256], replicated, may hold values from -0.1875 to 0.1875
Outputs:
- block_output: float32 [131072, 256], P(('grp', 'tm', 'chan'))
The draws below stay inside these ranges and needn't reach their ends.
All inputs are finite; a program needn't handle non-finite values.
Results may differ from the reference program's by a relative error of at most 0.0003.
Values sent between devices are 32-bit elements; how exact they have to be, the bound alone decides.
No kernel may reach another device: no remote copies, remote signals or barrier semaphores. Data moves between devices by JAX's collectives and lax.ppermute only.
A program may use at most 256 MiB of HBM per device.

```python
import math
import jax
import jax.numpy as jnp
from jax import lax

WIDTH = 256
HIDDEN_SIZE = 1024
HEADS = 2
TAPS = 127
WINDOW = 131072


def block_levels(own_key, dims, split, low, largest):
    def one(dim, parts):
        draws = jax.random.uniform(jax.random.fold_in(jax.random.fold_in(own_key, 6), dim), (parts,), jnp.float32, low / len(split), largest / len(split))
        return jnp.repeat(jnp.exp(draws), dims[dim] // parts).reshape((-1,) + (1,) * (len(dims) - dim - 1))

    level = one(*split[0])
    for cut in split[1:]:
        level = level * one(*cut)
    return level


def noise(rng, shape, scale, most, cuts=(), kind=jnp.bfloat16):
    values = scale * jax.random.normal(rng, shape, jnp.float32)
    if cuts:
        values = values * block_levels(rng, shape, cuts, -0.22, 0.18)
    return jnp.clip(values, -most, most).astype(kind)


def setup_inputs(seed: int = 0, part: int = 0) -> dict:
    arg_keys = jax.random.split(jax.random.key(seed), 10)
    part_splits = jax.random.split(jax.random.fold_in(arg_keys[9], part), 10)
    return {
        "signal": noise(part_splits[0], (WINDOW, WIDTH), 1.0, 6.0, ((0, 16), (1, 2)), jnp.float32),
        "kernel": noise(arg_keys[1], (WINDOW, WIDTH), WINDOW ** -0.5, 0.015625, ((0, 16), (1, 2)), jnp.float32),
        "skip_gain": noise(arg_keys[2], (WIDTH,), 1.0, 4.0, (), jnp.float32),
        "gate_input": noise(part_splits[3], (WINDOW, WIDTH), 1.0, 6.0, ((0, 32),), jnp.float32),
        "tap_weight": noise(arg_keys[4], (WIDTH, HEADS * TAPS), (WIDTH * TAPS) ** -0.5, 0.03125, (), jnp.float32),
        "norm_gain": jnp.clip(jnp.exp(jax.random.uniform(arg_keys[5], (WIDTH,), jnp.float32, math.log(0.5), math.log(2.0))), 0.5, 2.0),
        "up_weight": noise(arg_keys[6], (WIDTH, HIDDEN_SIZE), WIDTH ** -0.5, 0.375, (), jnp.float32),
        "up_bias": noise(arg_keys[7], (HIDDEN_SIZE,), 1.0, 4.0, (), jnp.float32),
        "down_weight": noise(arg_keys[8], (HIDDEN_SIZE, WIDTH), HIDDEN_SIZE ** -0.5, 0.1875, (), jnp.float32),
    }


HIGHEST = lax.Precision.HIGHEST
EPSILON = 1e-06

def causal_filter(signal, kernel, skip_gain):
    group_width = min(32, WIDTH)
    group_count = WIDTH // group_width
    signal_groups = signal.T.reshape(group_count, group_width, WINDOW)
    kernel_groups = kernel.T.reshape(group_count, group_width, WINDOW)

    def one_group(arrays):
        signal_part, kernel_part = arrays
        spectrum = jnp.fft.rfft(signal_part, n=2 * WINDOW, axis=1) * jnp.fft.rfft(kernel_part, n=2 * WINDOW, axis=1)
        return jnp.fft.irfft(spectrum, n=2 * WINDOW, axis=1)[:, :WINDOW]
    result = lax.map(one_group, (signal_groups, kernel_groups)).reshape(WIDTH, WINDOW).T
    return result + skip_gain * signal

def reference(signal, kernel, skip_gain, gate_input, tap_weight, norm_gain, up_weight, up_bias, down_weight):
    convolved = causal_filter(signal, kernel, skip_gain)
    gated = gate_input * convolved
    tap_values = jnp.dot(gated, tap_weight, precision=HIGHEST).reshape(WINDOW, HEADS, TAPS)
    padded = jnp.concatenate([jnp.zeros((TAPS - 1, WIDTH), gated.dtype), gated], axis=0)
    padded = padded.reshape(WINDOW + TAPS - 1, HEADS, WIDTH // HEADS)

    def add_tap(step, running):
        offset = (TAPS - 1 - step).astype(jnp.int32)
        shifted = lax.dynamic_slice_in_dim(padded, offset, WINDOW, 0)
        weights_now = lax.dynamic_index_in_dim(tap_values, step.astype(jnp.int32), 2, keepdims=False)
        return running + weights_now[:, :, None] * shifted
    initial = jnp.zeros((WINDOW, HEADS, WIDTH // HEADS), gated.dtype)
    local_mix = lax.fori_loop(0, TAPS, add_tap, initial).reshape(WINDOW, WIDTH)
    mean_square = lax.optimization_barrier(jnp.mean(local_mix * local_mix, axis=1, keepdims=True))
    normed = local_mix * lax.rsqrt(mean_square + EPSILON) * norm_gain
    hidden_units = jax.nn.gelu(jnp.dot(normed, up_weight, precision=HIGHEST) + up_bias)
    return local_mix + jnp.dot(hidden_units, down_weight, precision=HIGHEST)
```

```python
import functools
import math

import jax
import jax.numpy as jnp
import numpy as np
from jax import lax
from jax.experimental import pallas as pl
from jax.experimental.pallas import tpu as pltpu
from jax.sharding import PartitionSpec as P
import ml_dtypes

LANES = 512
RADIX = 4
SUB = LANES // RADIX
TAPS = 127
HEADS = 2
EPSILON = 1e-06
BF16 = jnp.bfloat16
F32 = jnp.float32
VMEM_LIMIT = 56 * 1024 * 1024


def table_split(table, axis, order):
    high = table.astype(ml_dtypes.bfloat16)
    low = (table - high.astype(np.float64)).astype(ml_dtypes.bfloat16)
    parts = {"h": high, "l": low}
    return np.concatenate([parts[name] for name in order], axis=axis)


@functools.lru_cache(maxsize=None)
def tables(rows):
    length = rows * LANES
    turn = 2.0 * math.pi
    n1 = np.arange(rows, dtype=np.float64)
    n2 = np.arange(LANES, dtype=np.float64)
    m = np.arange(SUB, dtype=np.float64)
    first = turn * np.outer(n1 + 0.25, n1) / rows
    enter = table_split(np.concatenate([np.cos(first), -np.sin(first)], axis=0), 1, "hhl")
    leave = table_split(
        np.concatenate([np.cos(first.T), -np.sin(first.T)], axis=1) / length, 1, "hhl"
    )
    twiddle = turn * np.outer(n1 + 0.25, n2) / length
    forward, backward = [], []
    for r in range(RADIX):
        phase = turn * np.outer(m, m / SUB + r / LANES)
        c, s = np.cos(phase), np.sin(phase)
        forward.append(table_split(np.block([[c, -s], [s, c]]), 0, "hhl"))
        c, s = c.T, s.T
        backward.append(table_split(np.block([[c, s], [-s, c]]), 0, "hhl"))
    return (
        enter,
        np.cos(twiddle).astype(np.float32),
        np.sin(twiddle).astype(np.float32),
        np.stack(forward),
        np.stack(backward),
        leave,
    )


def halves(value):
    high = value.astype(BF16)
    low = (value - high.astype(F32)).astype(BF16)
    return high, low


def split_cat(value, axis):
    high, low = halves(value)
    return jnp.concatenate([high, low, high], axis=axis)


def dot(left, right):
    return jnp.dot(left, right, preferred_element_type=F32)


def filter_kernel(
    skip_ref, signal_ref, kernel_ref, enter_ref, cos_ref, sin_ref, forward_ref, backward_ref,
    leave_ref, out_ref, spread_ref,
):
    rows = cos_ref.shape[0]
    for index, ref in enumerate((signal_ref, kernel_ref)):
        turned = dot(enter_ref[...], split_cat(ref[...].reshape(rows, LANES), 0))
        real_in, imag_in = turned[:rows], turned[rows:]
        real = real_in * cos_ref[...] + imag_in * sin_ref[...]
        imag = imag_in * cos_ref[...] - real_in * sin_ref[...]
        r0, r1, r2, r3 = (real[:, b * SUB : (b + 1) * SUB] for b in range(RADIX))
        i0, i1, i2, i3 = (imag[:, b * SUB : (b + 1) * SUB] for b in range(RADIX))
        er, ei, fr, fi = r0 + r2, i0 + i2, r0 - r2, i0 - i2
        gr, gi, hr, hi = r1 + r3, i1 + i3, r1 - r3, i1 - i3
        spread = ((er + gr, ei + gi), (fr + hi, fi - hr), (er - gr, ei - gi), (fr - hi, fi + hr))
        for r, pair in enumerate(spread):
            spread_ref[r, index * rows : (index + 1) * rows, :] = split_cat(
                jnp.concatenate(pair, axis=1), 1
            )
    back = []
    for r in range(RADIX):
        both = dot(spread_ref[r], forward_ref[r])
        sr, si = both[:rows, :SUB], both[:rows, SUB:]
        kr, ki = both[rows:, :SUB], both[rows:, SUB:]
        product = jnp.concatenate([sr * kr - si * ki, sr * ki + si * kr], axis=1)
        turned = dot(split_cat(product, 1), backward_ref[r])
        back.append((turned[:, :SUB], turned[:, SUB:]))
    (r0, i0), (r1, i1), (r2, i2), (r3, i3) = back
    er, ei, fr, fi = r0 + r2, i0 + i2, r0 - r2, i0 - i2
    gr, gi, hr, hi = r1 + r3, i1 + i3, r1 - r3, i1 - i3
    real = jnp.concatenate([er + gr, fr - hi, er - gr, fr + hi], axis=1)
    imag = jnp.concatenate([ei + gi, fi + hr, ei - gi, fi - hr], axis=1)
    turned = jnp.concatenate(
        [real * cos_ref[...] - imag * sin_ref[...], imag * cos_ref[...] + real * sin_ref[...]],
        axis=0,
    )
    result = dot(leave_ref[...], split_cat(turned, 0))
    skip = skip_ref[pl.program_id(0)]
    result = result + skip * signal_ref[...].reshape(rows, LANES)
    out_ref[...] = result.reshape(out_ref.shape)


def long_filter(signal, kernel, skip, out_groups):
    groups, channels, group_rows, _ = signal.shape
    rows = groups * group_rows
    straight = group_rows % 8 == 0 and (rows // out_groups) % 8 == 0
    in_block = (groups, 1, group_rows, LANES)
    out_shape = (out_groups, channels, rows // out_groups, LANES)
    if not straight:
        signal = signal.transpose(1, 0, 2, 3).reshape(1, channels, rows, LANES)
        kernel = kernel.transpose(1, 0, 2, 3).reshape(1, channels, rows, LANES)
        in_block = (1, 1, rows, LANES)
        out_shape = (1, channels, rows, LANES)
    out_block = (out_shape[0], 1) + out_shape[2:]

    def along(c):
        return (0, c, 0, 0)

    def whole(array):
        return pl.BlockSpec(array.shape, lambda c: (0,) * array.ndim)

    held = tables(rows)
    result = pl.pallas_call(
        filter_kernel,
        grid=(channels,),
        in_specs=[
            pl.BlockSpec(memory_space=pltpu.SMEM),
            pl.BlockSpec(in_block, along),
            pl.BlockSpec(in_block, along),
        ]
        + [whole(table) for table in held],
        out_specs=pl.BlockSpec(out_block, along),
        out_shape=jax.ShapeDtypeStruct(out_shape, F32),
        scratch_shapes=[pltpu.VMEM((RADIX, 2 * rows, 6 * SUB), BF16)],
        compiler_params=pltpu.CompilerParams(vmem_limit_bytes=VMEM_LIMIT),
        cost_estimate=pl.CostEstimate(
            flops=channels * rows * LANES * 2048 * 3 * 3,
            bytes_accessed=channels * rows * LANES * 12,
            transcendentals=0,
        ),
        name="long_filter",
    )(skip, signal, kernel, *held)
    if not straight:
        result = result.reshape(channels, out_groups, rows // out_groups, LANES)
        result = result.transpose(1, 0, 2, 3)
    return result


def mix_kernel(
    conv_ref, gate_ref, halo_ref, tap_ref, gain_ref, up_ref, bias_ref, down_ref, out_ref,
    window_ref, high_ref, low_ref, mix_ref,
):
    block = gate_ref.shape[0]
    width = gate_ref.shape[1]
    reach = TAPS + 1
    head_width = width // HEADS

    @pl.when(pl.program_id(0) == 0)
    def _():
        window_ref[:reach, :] = halo_ref[...]

    @pl.when(pl.program_id(0) > 0)
    def _():
        window_ref[:reach, :] = window_ref[block : block + reach, :]

    window_ref[reach:, :] = jnp.transpose(conv_ref[0], (1, 0)) * gate_ref[...]
    high, low = halves(window_ref[...])
    high_ref[...] = high
    low_ref[...] = low
    taps = dot(
        jnp.concatenate([high[reach:], low[reach:], high[reach:]], axis=1), tap_ref[...]
    )
    for b in range(block // reach):
        for h in range(HEADS):
            own = taps[b * reach : (b + 1) * reach, h * reach : (h + 1) * reach]
            band = jnp.concatenate([own, jnp.zeros_like(own)], axis=1)
            band = pltpu.roll(band, 1, 1, stride=1, stride_axis=0)
            near_rows = slice(b * reach, (b + 2) * reach)
            columns = slice(h * head_width, (h + 1) * head_width)
            near_high = high_ref[near_rows, columns]
            near_low = low_ref[near_rows, columns]
            mix_ref[b * reach : (b + 1) * reach, columns] = dot(
                split_cat(band, 1), jnp.concatenate([near_high, near_high, near_low], axis=0)
            )
    mixed = mix_ref[...]
    mean_square = jnp.mean(mixed * mixed, axis=1, keepdims=True)
    normed = mixed * lax.rsqrt(mean_square + EPSILON) * gain_ref[...]
    raised = dot(split_cat(normed, 1), up_ref[...]) + bias_ref[...]
    inner = math.sqrt(2.0 / math.pi) * (raised + 0.044715 * (raised * raised * raised))
    hidden = 0.5 * raised * (1.0 + jnp.tanh(inner))
    out_ref[...] = mixed + dot(split_cat(hidden, 1), down_ref[...])


def weight_split(weight):
    high = lax.reduce_precision(weight, 8, 7)
    low = weight - high
    return jnp.concatenate([high, high, low], axis=0).astype(BF16)


def tail(conv_blocks, gate_input, halo, tap_weight, norm_gain, up_weight, up_bias, down_weight):
    count, width, block = conv_blocks.shape
    reach = TAPS + 1
    taps = tap_weight.reshape(width, HEADS, TAPS)[:, :, ::-1]
    taps = jnp.pad(taps, ((0, 0), (0, 0), (1, 0))).reshape(width, HEADS * reach)
    fixed = (
        weight_split(taps),
        norm_gain.reshape(1, -1),
        weight_split(up_weight),
        up_bias.reshape(1, -1),
        weight_split(down_weight),
    )

    def whole(array):
        return pl.BlockSpec(array.shape, lambda r: (0,) * array.ndim)

    return pl.pallas_call(
        mix_kernel,
        grid=(count,),
        in_specs=[
            pl.BlockSpec((1, width, block), lambda r: (r, 0, 0)),
            pl.BlockSpec((block, width), lambda r: (r, 0)),
            whole(halo),
        ]
        + [whole(array) for array in fixed],
        out_specs=pl.BlockSpec((block, width), lambda r: (r, 0)),
        out_shape=jax.ShapeDtypeStruct(gate_input.shape, F32),
        scratch_shapes=[
            pltpu.VMEM((block + reach, width), F32),
            pltpu.VMEM((block + reach, width), BF16),
            pltpu.VMEM((block + reach, width), BF16),
            pltpu.VMEM((block, width), F32),
        ],
        compiler_params=pltpu.CompilerParams(vmem_limit_bytes=VMEM_LIMIT),
        cost_estimate=pl.CostEstimate(
            flops=count * block * 3 * 2 * (2 * width * up_weight.shape[1] + 3 * width * width),
            bytes_accessed=count * block * width * 12,
            transcendentals=count * block * up_weight.shape[1],
        ),
        name="mix_and_mlp",
    )(conv_blocks, gate_input, halo, *fixed)


def on_device(
    signal, kernel, skip_gain, gate_input, tap_weight, norm_gain, up_weight, up_bias, down_weight
):
    groups = lax.axis_size("tm")
    pair = lax.axis_size("chan")
    frames_here, channels_here = signal.shape
    owned = channels_here // groups
    width = gate_input.shape[1]
    first_channel = lax.axis_index("chan") * channels_here + lax.axis_index("tm") * owned
    skip_here = lax.dynamic_slice_in_dim(skip_gain, first_channel, owned)

    def enter(array):
        shaped = array.reshape(frames_here // LANES, LANES, groups, owned).transpose(2, 3, 0, 1)
        return lax.all_to_all(shaped, "tm", split_axis=0, concat_axis=0, tiled=True)

    filtered = long_filter(enter(signal), enter(kernel), skip_here, groups * pair)
    back = lax.all_to_all(filtered, ("tm", "chan"), split_axis=0, concat_axis=0, tiled=True)
    blocks = back.reshape(groups, pair, owned, -1, LANES).transpose(3, 1, 0, 2, 4)
    blocks = blocks.reshape(-1, width, LANES)
    reach = TAPS + 1
    last = blocks[-1, :, LANES - reach :].T * gate_input[-reach:]
    devices = groups * pair
    halo = lax.ppermute(last, ("tm", "chan"), [(i, i + 1) for i in range(devices - 1)])
    return tail(blocks, gate_input, halo, tap_weight, norm_gain, up_weight, up_bias, down_weight)


def solution(mesh):
    placed = (
        P(("grp", "tm"), "chan"),
        P("tm", "chan"),
        P(),
        P(("grp", "tm", "chan"), None),
        P(),
        P(),
        P(),
        P(),
        P(),
    )
    return jax.shard_map(
        on_device,
        mesh=mesh,
        in_specs=placed,
        out_specs=P(("grp", "tm", "chan"), None),
        check_vma=False,
    )
```

```python
import functools
import math

import jax
import jax.numpy as jnp
import numpy as np
from jax import lax
from jax.experimental import pallas as pl
from jax.experimental.pallas import tpu as pltpu
from jax.sharding import PartitionSpec as P
import ml_dtypes

LANES = 512
RADIX = 4
SUB = LANES // RADIX
TAPS = 127
HEADS = 2
EPSILON = 1e-06
BF16 = jnp.bfloat16
F32 = jnp.float32
VMEM_LIMIT = 56 * 1024 * 1024


def table_split(table, axis, order):
    high = table.astype(ml_dtypes.bfloat16)
    low = (table - high.astype(np.float64)).astype(ml_dtypes.bfloat16)
    parts = {"h": high, "l": low}
    return np.concatenate([parts[name] for name in order], axis=axis)


@functools.lru_cache(maxsize=None)
def tables(rows):
    length = rows * LANES
    turn = 2.0 * math.pi
    n1 = np.arange(rows, dtype=np.float64)
    n2 = np.arange(LANES, dtype=np.float64)
    m = np.arange(SUB, dtype=np.float64)
    first = turn * np.outer(n1 + 0.25, n1) / rows
    enter = table_split(np.concatenate([np.cos(first), -np.sin(first)], axis=0), 1, "hhl")
    leave = table_split(
        np.concatenate([np.cos(first.T), -np.sin(first.T)], axis=1) / length, 1, "hhl"
    )
    twiddle = turn * np.outer(n1 + 0.25, n2) / length
    forward, backward = [], []
    for r in range(RADIX):
        phase = turn * np.outer(m, m / SUB + r / LANES)
        c, s = np.cos(phase), np.sin(phase)
        forward.append(table_split(np.block([[c, -s], [s, c]]), 0, "hhl"))
        c, s = c.T, s.T
        backward.append(table_split(np.block([[c, s], [-s, c]]), 0, "hhl"))
    return (
        enter,
        np.cos(twiddle).astype(np.float32),
        np.sin(twiddle).astype(np.float32),
        np.stack(forward),
        np.stack(backward),
        leave,
    )


def halves(value):
    high = value.astype(BF16)
    low = (value - high.astype(F32)).astype(BF16)
    return high, low


def split_cat(value, axis):
    high, low = halves(value)
    return jnp.concatenate([high, low, high], axis=axis)


def dot(left, right):
    return jnp.dot(left, right, preferred_element_type=F32)


def filter_channel(signal, kernel, skip, enter_ref, cos_ref, sin_ref, forward_ref, backward_ref,
                   leave_ref, spread_ref):
    rows = cos_ref.shape[0]
    for index, value in enumerate((signal, kernel)):
        turned = dot(enter_ref[...], split_cat(value, 0))
        real_in, imag_in = turned[:rows], turned[rows:]
        real = real_in * cos_ref[...] + imag_in * sin_ref[...]
        imag = imag_in * cos_ref[...] - real_in * sin_ref[...]
        r0, r1, r2, r3 = (real[:, b * SUB : (b + 1) * SUB] for b in range(RADIX))
        i0, i1, i2, i3 = (imag[:, b * SUB : (b + 1) * SUB] for b in range(RADIX))
        er, ei, fr, fi = r0 + r2, i0 + i2, r0 - r2, i0 - i2
        gr, gi, hr, hi = r1 + r3, i1 + i3, r1 - r3, i1 - i3
        spread = ((er + gr, ei + gi), (fr + hi, fi - hr), (er - gr, ei - gi), (fr - hi, fi + hr))
        for r, pair in enumerate(spread):
            spread_ref[r, index * rows : (index + 1) * rows, :] = split_cat(
                jnp.concatenate(pair, axis=1), 1
            )
    back = []
    for r in range(RADIX):
        both = dot(spread_ref[r], forward_ref[r])
        sr, si = both[:rows, :SUB], both[:rows, SUB:]
        kr, ki = both[rows:, :SUB], both[rows:, SUB:]
        product = jnp.concatenate([sr * kr - si * ki, sr * ki + si * kr], axis=1)
        turned = dot(split_cat(product, 1), backward_ref[r])
        back.append((turned[:, :SUB], turned[:, SUB:]))
    (r0, i0), (r1, i1), (r2, i2), (r3, i3) = back
    er, ei, fr, fi = r0 + r2, i0 + i2, r0 - r2, i0 - i2
    gr, gi, hr, hi = r1 + r3, i1 + i3, r1 - r3, i1 - i3
    real = jnp.concatenate([er + gr, fr - hi, er - gr, fr + hi], axis=1)
    imag = jnp.concatenate([ei + gi, fi + hr, ei - gi, fi - hr], axis=1)
    turned = jnp.concatenate(
        [real * cos_ref[...] - imag * sin_ref[...], imag * cos_ref[...] + real * sin_ref[...]],
        axis=0,
    )
    return dot(leave_ref[...], split_cat(turned, 0)) + skip * signal


def filter_kernel(
    skip_ref, signal_ref, kernel_ref, enter_ref, cos_ref, sin_ref, forward_ref, backward_ref,
    leave_ref, out_ref, spread_ref,
):
    rows = cos_ref.shape[0]
    result = filter_channel(
        signal_ref[...].reshape(rows, LANES), kernel_ref[...].reshape(rows, LANES),
        skip_ref[pl.program_id(0)], enter_ref, cos_ref, sin_ref, forward_ref, backward_ref,
        leave_ref, spread_ref,
    )
    out_ref[...] = result.reshape(out_ref.shape)


def long_filter(signal, kernel, skip, out_groups):
    groups, channels, group_rows, _ = signal.shape
    rows = groups * group_rows
    straight = group_rows % 8 == 0 and (rows // out_groups) % 8 == 0
    in_block = (groups, 1, group_rows, LANES)
    out_shape = (out_groups, channels, rows // out_groups, LANES)
    if not straight:
        signal = signal.transpose(1, 0, 2, 3).reshape(1, channels, rows, LANES)
        kernel = kernel.transpose(1, 0, 2, 3).reshape(1, channels, rows, LANES)
        in_block = (1, 1, rows, LANES)
        out_shape = (1, channels, rows, LANES)
    out_block = (out_shape[0], 1) + out_shape[2:]

    def along(c):
        return (0, c, 0, 0)

    def whole(array):
        return pl.BlockSpec(array.shape, lambda c: (0,) * array.ndim)

    held = tables(rows)
    result = pl.pallas_call(
        filter_kernel,
        grid=(channels,),
        in_specs=[
            pl.BlockSpec(memory_space=pltpu.SMEM),
            pl.BlockSpec(in_block, along),
            pl.BlockSpec(in_block, along),
        ]
        + [whole(table) for table in held],
        out_specs=pl.BlockSpec(out_block, along),
        out_shape=jax.ShapeDtypeStruct(out_shape, F32),
        scratch_shapes=[pltpu.VMEM((RADIX, 2 * rows, 6 * SUB), BF16)],
        compiler_params=pltpu.CompilerParams(vmem_limit_bytes=VMEM_LIMIT),
        cost_estimate=pl.CostEstimate(
            flops=channels * rows * LANES * 2048 * 3 * 3,
            bytes_accessed=channels * rows * LANES * 12,
            transcendentals=0,
        ),
        name="long_filter",
    )(skip, signal, kernel, *held)
    if not straight:
        result = result.reshape(channels, out_groups, rows // out_groups, LANES)
        result = result.transpose(1, 0, 2, 3)
    return result


def mix_block(window_ref, tap_ref, gain_ref, up_ref, bias_ref, down_ref, out_ref, high_ref, low_ref,
              mix_ref):
    block, width = out_ref.shape
    reach = TAPS + 1
    head_width = width // HEADS
    high, low = halves(window_ref[...])
    high_ref[...] = high
    low_ref[...] = low
    taps = dot(
        jnp.concatenate([high[reach:], low[reach:], high[reach:]], axis=1), tap_ref[...]
    )
    for b in range(block // reach):
        for h in range(HEADS):
            own = taps[b * reach : (b + 1) * reach, h * reach : (h + 1) * reach]
            band = jnp.concatenate([own, jnp.zeros_like(own)], axis=1)
            band = pltpu.roll(band, 1, 1, stride=1, stride_axis=0)
            near_rows = slice(b * reach, (b + 2) * reach)
            columns = slice(h * head_width, (h + 1) * head_width)
            near_high = high_ref[near_rows, columns]
            near_low = low_ref[near_rows, columns]
            mix_ref[b * reach : (b + 1) * reach, columns] = dot(
                split_cat(band, 1), jnp.concatenate([near_high, near_high, near_low], axis=0)
            )
    mixed = mix_ref[...]
    mean_square = jnp.mean(mixed * mixed, axis=1, keepdims=True)
    normed = mixed * lax.rsqrt(mean_square + EPSILON) * gain_ref[...]
    raised = dot(split_cat(normed, 1), up_ref[...]) + bias_ref[...]
    inner = math.sqrt(2.0 / math.pi) * (raised + 0.044715 * (raised * raised * raised))
    hidden = 0.5 * raised * (1.0 + jnp.tanh(inner))
    out_ref[...] = mixed + dot(split_cat(hidden, 1), down_ref[...])


def mix_kernel(
    conv_ref, gate_ref, halo_ref, tap_ref, gain_ref, up_ref, bias_ref, down_ref, out_ref,
    window_ref, high_ref, low_ref, mix_ref,
):
    block = gate_ref.shape[0]
    reach = TAPS + 1

    @pl.when(pl.program_id(0) == 0)
    def _():
        window_ref[:reach, :] = halo_ref[...]

    @pl.when(pl.program_id(0) > 0)
    def _():
        window_ref[:reach, :] = window_ref[block : block + reach, :]

    window_ref[reach:, :] = jnp.transpose(conv_ref[0], (1, 0)) * gate_ref[...]
    mix_block(
        window_ref, tap_ref, gain_ref, up_ref, bias_ref, down_ref, out_ref, high_ref, low_ref, mix_ref
    )


def weight_split(weight):
    high = lax.reduce_precision(weight, 8, 7)
    low = weight - high
    return jnp.concatenate([high, high, low], axis=0).astype(BF16)


def fixed_operands(tap_weight, norm_gain, up_weight, up_bias, down_weight):
    width = tap_weight.shape[0]
    taps = tap_weight.reshape(width, HEADS, TAPS)[:, :, ::-1]
    taps = jnp.pad(taps, ((0, 0), (0, 0), (1, 0))).reshape(width, HEADS * (TAPS + 1))
    return (
        weight_split(taps),
        norm_gain.reshape(1, -1),
        weight_split(up_weight),
        up_bias.reshape(1, -1),
        weight_split(down_weight),
    )


def tail(conv_blocks, gate_input, halo, fixed):
    count, width, block = conv_blocks.shape
    reach = TAPS + 1
    hidden = fixed[3].shape[1]

    def whole(array):
        return pl.BlockSpec(array.shape, lambda r: (0,) * array.ndim)

    return pl.pallas_call(
        mix_kernel,
        grid=(count,),
        in_specs=[
            pl.BlockSpec((1, width, block), lambda r: (r, 0, 0)),
            pl.BlockSpec((block, width), lambda r: (r, 0)),
            whole(halo),
        ]
        + [whole(array) for array in fixed],
        out_specs=pl.BlockSpec((block, width), lambda r: (r, 0)),
        out_shape=jax.ShapeDtypeStruct(gate_input.shape, F32),
        scratch_shapes=[
            pltpu.VMEM((block + reach, width), F32),
            pltpu.VMEM((block + reach, width), BF16),
            pltpu.VMEM((block + reach, width), BF16),
            pltpu.VMEM((block, width), F32),
        ],
        compiler_params=pltpu.CompilerParams(vmem_limit_bytes=VMEM_LIMIT),
        cost_estimate=pl.CostEstimate(
            flops=count * block * 3 * 2 * (2 * width * hidden + 3 * width * width),
            bytes_accessed=count * block * width * 12,
            transcendentals=count * block * hidden,
        ),
        name="mix_and_mlp",
    )(conv_blocks, gate_input, halo, *fixed)


def turn_kernel(signal_ref, kernel_ref, *out_refs):
    chunk = signal_ref.shape[0]
    half = 8 // 2
    for tile in range(chunk // 128):
        span = slice(tile * 128, (tile + 1) * 128)
        s = jnp.transpose(signal_ref[span, :], (1, 0))
        k = jnp.transpose(kernel_ref[span, :], (1, 0))
        lower = lax.broadcasted_iota(jnp.int32, s.shape, 0) % 8 < half
        first = jnp.where(lower, s, pltpu.roll(k, half, 0))
        second = jnp.where(lower, pltpu.roll(s, s.shape[0] - half, 0), k)
        for ref, value in zip(out_refs, (first, second)):
            ref[:, tile] = value.reshape(ref.shape[0], 8, 128)


def turn(signal, kernel, groups):
    frames, width = signal.shape
    chunk = 1024
    tiles = chunk // 128
    block = pl.BlockSpec((chunk, width), lambda i: (i, 0))
    out_block = pl.BlockSpec((groups, tiles, 8, 128), lambda i: (0, i, 0, 0))
    shape = jax.ShapeDtypeStruct((groups, frames // 128, 8, 128), F32)
    return pl.pallas_call(
        turn_kernel,
        grid=(frames // chunk,),
        in_specs=[block, block],
        out_specs=[out_block, out_block],
        out_shape=[shape, shape],
        compiler_params=pltpu.CompilerParams(vmem_limit_bytes=VMEM_LIMIT),
        name="turn",
    )(signal, kernel)


def gather_channel(ref, slot, rows):
    tiles = LANES // 128
    return jnp.concatenate(
        [ref[pl.ds(8 * j + slot, rows, stride=8 * tiles), :] for j in range(tiles)], axis=1
    )


def scatter_channel(ref, slot, value):
    tiles = LANES // 128
    for j in range(tiles):
        ref[pl.ds(8 * j + slot, value.shape[0], stride=8 * tiles), :] = (
            value[:, j * 128 : (j + 1) * 128]
        )


def first_half_kernel(skip_ref, data_ref, *rest):
    *table_refs, out_ref, spread_ref = rest
    rows = table_refs[1].shape[0]
    c = pl.program_id(0)
    result = filter_channel(
        gather_channel(data_ref, c, rows), gather_channel(data_ref, c + 4, rows), skip_ref[c],
        *table_refs, spread_ref,
    )
    scatter_channel(out_ref, c, result)


def second_half_kernel(late, skip_ref, data_ref, *rest):
    *table_refs, before_ref, late_ref, early_ref, spread_ref, held_ref, sems = rest
    rows = table_refs[1].shape[0]
    c = pl.program_id(0)
    devices, tiles = late_ref.shape[0], late_ref.shape[1] + early_ref.shape[1]
    load = pltpu.make_async_copy(before_ref, held_ref, sems.at[0])

    @pl.when(c == 0)
    def _():
        load.start()

    result = filter_channel(
        gather_channel(data_ref, c, rows), gather_channel(data_ref, c + 4, rows),
        skip_ref[c + 4], *table_refs, spread_ref,
    )

    @pl.when(c == 0)
    def _():
        load.wait()

    scatter_channel(held_ref, c + 4, result)

    @pl.when(c == pl.num_programs(0) - 1)
    def _():
        shaped = held_ref.reshape(devices, tiles, 8, 128)
        copies = [
            pltpu.make_async_copy(
                shaped.at[:, late:tiles], late_ref.at[:, 0 : tiles - late], sems.at[1]
            ),
            pltpu.make_async_copy(
                shaped.at[:, late - 1 : late],
                late_ref.at[:, tiles - late : tiles - late + 1],
                sems.at[2],
            ),
            pltpu.make_async_copy(shaped.at[:, 0 : late - 1], early_ref, sems.at[3]),
        ]
        for copy in copies:
            copy.start()
        for copy in copies:
            copy.wait()


def filter_half(data, skip, before, devices, late):
    flat = data.reshape(-1, 128)
    rows = flat.shape[0] // (8 * (LANES // 128))
    tiles = flat.shape[0] // (8 * devices)
    held = tables(rows)

    def whole(array):
        return pl.BlockSpec(array.shape, lambda c: (0,) * array.ndim)

    in_specs = [pl.BlockSpec(memory_space=pltpu.SMEM), whole(flat)] + [whole(t) for t in held]
    spread = pltpu.VMEM((RADIX, 2 * rows, 6 * SUB), BF16)
    options = dict(
        grid=(4,),
        compiler_params=pltpu.CompilerParams(vmem_limit_bytes=VMEM_LIMIT),
        cost_estimate=pl.CostEstimate(
            flops=4 * rows * LANES * 2048 * 3 * 3,
            bytes_accessed=4 * rows * LANES * 12,
            transcendentals=0,
        ),
    )
    if before is None:
        return pl.pallas_call(
            first_half_kernel,
            in_specs=in_specs,
            out_specs=whole(flat),
            out_shape=jax.ShapeDtypeStruct(flat.shape, F32),
            scratch_shapes=[spread],
            name="filter_first",
            **options,
        )(skip, flat, *held)
    anywhere = pl.BlockSpec(memory_space=pl.ANY)
    return pl.pallas_call(
        functools.partial(second_half_kernel, late),
        in_specs=in_specs + [anywhere],
        out_specs=[anywhere, anywhere],
        out_shape=[
            jax.ShapeDtypeStruct((devices, tiles - late + 1, 8, 128), F32),
            jax.ShapeDtypeStruct((devices, late - 1, 8, 128), F32),
        ],
        scratch_shapes=[spread, pltpu.VMEM(flat.shape, F32), pltpu.SemaphoreType.DMA((4,))],
        name="filter_second",
        **options,
    )(skip, flat, *held, before)


def frames_by_channels(tile):
    paired = tile.reshape(tile.shape[0] // HEADS, HEADS, 8, 128)
    return jnp.concatenate(
        [jnp.transpose(paired[:, h].reshape(-1, 128), (1, 0)) for h in range(HEADS)], axis=1
    )


def late_kernel(conv_ref, edge_ref, gate_ref, edge_gate_ref, *rest):
    *fixed, out_ref, window_ref, high_ref, low_ref, mix_ref = rest
    block = gate_ref.shape[0]
    reach = TAPS + 1

    @pl.when(pl.program_id(0) == 0)
    def _():
        window_ref[:reach, :] = frames_by_channels(edge_ref[:, 0]) * edge_gate_ref[...]

    @pl.when(pl.program_id(0) > 0)
    def _():
        window_ref[:reach, :] = window_ref[block : block + reach, :]

    for j in range(block // reach):
        span = slice(j * reach, (j + 1) * reach)
        window_ref[reach + j * reach : 2 * reach + j * reach, :] = (
            frames_by_channels(conv_ref[:, j]) * gate_ref[span, :]
        )
    mix_block(window_ref, *fixed, out_ref, high_ref, low_ref, mix_ref)


def early_kernel(conv_ref, edge_ref, gate_ref, halo_ref, *rest):
    *fixed, _, out_ref, window_ref, high_ref, low_ref, mix_ref = rest
    block = gate_ref.shape[0]
    reach = TAPS + 1
    last = pl.program_id(0) == pl.num_programs(0) - 1

    @pl.when(pl.program_id(0) == 0)
    def _():
        window_ref[:reach, :] = halo_ref[...]

    @pl.when(pl.program_id(0) > 0)
    def _():
        window_ref[:reach, :] = window_ref[block : block + reach, :]

    count = block // reach
    for j in range(count):
        tile = conv_ref[:, j]
        if j == count - 1:
            tile = jnp.where(last, edge_ref[:, 0], tile)
        span = slice(j * reach, (j + 1) * reach)
        window_ref[reach + j * reach : 2 * reach + j * reach, :] = (
            frames_by_channels(tile) * gate_ref[span, :]
        )
    mix_block(window_ref, *fixed, out_ref, high_ref, low_ref, mix_ref)


def tail_part(conv, late, gate_input, halo, before, late_tiles, fixed):
    devices = conv.shape[0]
    frames, width = gate_input.shape
    reach = TAPS + 1
    block = 512
    per_block = block // 128
    edge = late.shape[1] - 1
    first = before is not None

    def whole(array):
        return pl.BlockSpec(array.shape, lambda r: (0,) * array.ndim)

    start = 0 if first else late_tiles // per_block
    count = (late_tiles if first else edge) // per_block
    in_specs = [
        pl.BlockSpec((devices, per_block, 8, 128), lambda r: (0, r, 0, 0)),
        pl.BlockSpec((devices, 1, 8, 128), lambda r: (0, edge, 0, 0)),
        pl.BlockSpec((block, width), lambda r: (r + start, 0)),
    ]
    operands = [conv, late, gate_input]
    if first:
        in_specs += [whole(halo)]
        operands += [halo]
    else:
        in_specs += [pl.BlockSpec((reach, width), lambda r: (late_tiles - 1, 0))]
        operands += [gate_input]
    in_specs += [whole(array) for array in fixed]
    operands += fixed
    aliases = {}
    if first:
        aliases = {len(operands): 0}
        in_specs += [pl.BlockSpec(memory_space=pl.ANY)]
        operands += [before]
    hidden = fixed[3].shape[1]
    return pl.pallas_call(
        early_kernel if first else late_kernel,
        grid=(count,),
        in_specs=in_specs,
        out_specs=pl.BlockSpec((block, width), lambda r: (r + start, 0)),
        out_shape=jax.ShapeDtypeStruct(gate_input.shape, F32),
        input_output_aliases=aliases,
        scratch_shapes=[
            pltpu.VMEM((block + reach, width), F32),
            pltpu.VMEM((block + reach, width), BF16),
            pltpu.VMEM((block + reach, width), BF16),
            pltpu.VMEM((block, width), F32),
        ],
        compiler_params=pltpu.CompilerParams(vmem_limit_bytes=VMEM_LIMIT),
        cost_estimate=pl.CostEstimate(
            flops=count * block * 3 * 2 * (2 * width * hidden + 3 * width * width),
            bytes_accessed=count * block * width * 12,
            transcendentals=count * block * hidden,
        ),
        name="mix_early" if first else "mix_late",
    )(*operands)


def owned_eight(signal, kernel, skip_here, gate_input, fixed):
    groups = lax.axis_size("tm")
    devices = groups * lax.axis_size("chan")
    reach = TAPS + 1
    late_tiles = 2 * (512 // 128)

    def enter(array):
        return lax.all_to_all(array, "tm", split_axis=0, concat_axis=0, tiled=True)

    def leave(array):
        return lax.all_to_all(array, ("tm", "chan"), split_axis=0, concat_axis=0, tiled=True)

    one, two = turn(signal, kernel, groups)
    before = filter_half(enter(one), skip_here, None, devices, late_tiles)
    late, early = filter_half(enter(two), skip_here, before, devices, late_tiles)
    late = leave(late)
    final = frames_by_channels(late[:, late.shape[1] - 2]) * gate_input[-reach:]
    halo = lax.ppermute(final, ("tm", "chan"), [(i, i + 1) for i in range(devices - 1)])
    early = leave(early)
    part = tail_part(late, late, gate_input, None, None, late_tiles, fixed)
    return tail_part(early, late, gate_input, halo, part, late_tiles, fixed)


def on_device(
    signal, kernel, skip_gain, gate_input, tap_weight, norm_gain, up_weight, up_bias, down_weight
):
    groups = lax.axis_size("tm")
    pair = lax.axis_size("chan")
    frames_here, channels_here = signal.shape
    owned = channels_here // groups
    width = gate_input.shape[1]
    first_channel = lax.axis_index("chan") * channels_here + lax.axis_index("tm") * owned
    skip_here = lax.dynamic_slice_in_dim(skip_gain, first_channel, owned)
    fixed = fixed_operands(tap_weight, norm_gain, up_weight, up_bias, down_weight)
    window = frames_here * groups
    if owned == 8 and channels_here == 128 and pair == HEADS and window == 256 * LANES:
        if gate_input.shape[0] % 512 == 0 and gate_input.shape[0] >= 2048:
            return owned_eight(signal, kernel, skip_here, gate_input, fixed)

    def enter(array):
        shaped = array.reshape(frames_here // LANES, LANES, groups, owned).transpose(2, 3, 0, 1)
        return lax.all_to_all(shaped, "tm", split_axis=0, concat_axis=0, tiled=True)

    filtered = long_filter(enter(signal), enter(kernel), skip_here, groups * pair)
    back = lax.all_to_all(filtered, ("tm", "chan"), split_axis=0, concat_axis=0, tiled=True)
    blocks = back.reshape(groups, pair, owned, -1, LANES).transpose(3, 1, 0, 2, 4)
    blocks = blocks.reshape(-1, width, LANES)
    reach = TAPS + 1
    last = blocks[-1, :, LANES - reach :].T * gate_input[-reach:]
    devices = groups * pair
    halo = lax.ppermute(last, ("tm", "chan"), [(i, i + 1) for i in range(devices - 1)])
    return tail(blocks, gate_input, halo, fixed)


def solution(mesh):
    placed = (
        P(("grp", "tm"), "chan"),
        P("tm", "chan"),
        P(),
        P(("grp", "tm", "chan"), None),
        P(),
        P(),
        P(),
        P(),
        P(),
    )
    return jax.shard_map(
        on_device,
        mesh=mesh,
        in_specs=placed,
        out_specs=P(("grp", "tm", "chan"), None),
        check_vma=False,
    )
```

```python
import functools
import math

import jax
import jax.numpy as jnp
import numpy as np
from jax import lax
from jax.experimental import pallas as pl
from jax.experimental.pallas import tpu as pltpu
from jax.sharding import PartitionSpec as P
import ml_dtypes

LANES = 512
RADIX = 4
SUB = LANES // RADIX
TAPS = 127
HEADS = 2
EPSILON = 1e-06
BF16 = jnp.bfloat16
F32 = jnp.float32
VMEM_LIMIT = 56 * 1024 * 1024


def table_split(table, axis, order):
    high = table.astype(ml_dtypes.bfloat16)
    low = (table - high.astype(np.float64)).astype(ml_dtypes.bfloat16)
    parts = {"h": high, "l": low}
    return np.concatenate([parts[name] for name in order], axis=axis)


@functools.lru_cache(maxsize=None)
def tables(rows):
    length = rows * LANES
    turn = 2.0 * math.pi
    n1 = np.arange(rows, dtype=np.float64)
    n2 = np.arange(LANES, dtype=np.float64)
    m = np.arange(SUB, dtype=np.float64)
    first = turn * np.outer(n1 + 0.25, n1) / rows
    enter = table_split(np.concatenate([np.cos(first), -np.sin(first)], axis=0), 1, "hhl")
    leave = table_split(
        np.concatenate([np.cos(first.T), -np.sin(first.T)], axis=1) / length, 1, "hhl"
    )
    twiddle = turn * np.outer(n1 + 0.25, n2) / length
    forward, backward = [], []
    for r in range(RADIX):
        phase = turn * np.outer(m, m / SUB + r / LANES)
        c, s = np.cos(phase), np.sin(phase)
        forward.append(table_split(np.block([[c, -s], [s, c]]), 0, "hhl"))
        c, s = c.T, s.T
        backward.append(table_split(np.block([[c, s], [-s, c]]), 0, "hhl"))
    return (
        enter,
        np.cos(twiddle).astype(np.float32),
        np.sin(twiddle).astype(np.float32),
        np.stack(forward),
        np.stack(backward),
        leave,
    )


def halves(value):
    high = value.astype(BF16)
    low = (value - high.astype(F32)).astype(BF16)
    return high, low


def split_cat(value, axis):
    high, low = halves(value)
    return jnp.concatenate([high, low, high], axis=axis)


def dot(left, right):
    return jnp.dot(left, right, preferred_element_type=F32)


def filter_channel(signal, kernel, skip, enter_ref, cos_ref, sin_ref, forward_ref, backward_ref,
                   leave_ref, spread_ref):
    rows = cos_ref.shape[0]
    for index, value in enumerate((signal, kernel)):
        turned = dot(enter_ref[...], split_cat(value, 0))
        real_in, imag_in = turned[:rows], turned[rows:]
        real = real_in * cos_ref[...] + imag_in * sin_ref[...]
        imag = imag_in * cos_ref[...] - real_in * sin_ref[...]
        r0, r1, r2, r3 = (real[:, b * SUB : (b + 1) * SUB] for b in range(RADIX))
        i0, i1, i2, i3 = (imag[:, b * SUB : (b + 1) * SUB] for b in range(RADIX))
        er, ei, fr, fi = r0 + r2, i0 + i2, r0 - r2, i0 - i2
        gr, gi, hr, hi = r1 + r3, i1 + i3, r1 - r3, i1 - i3
        spread = ((er + gr, ei + gi), (fr + hi, fi - hr), (er - gr, ei - gi), (fr - hi, fi + hr))
        for r, pair in enumerate(spread):
            spread_ref[r, index * rows : (index + 1) * rows, :] = split_cat(
                jnp.concatenate(pair, axis=1), 1
            )
    back = []
    for r in range(RADIX):
        both = dot(spread_ref[r], forward_ref[r])
        sr, si = both[:rows, :SUB], both[:rows, SUB:]
        kr, ki = both[rows:, :SUB], both[rows:, SUB:]
        product = jnp.concatenate([sr * kr - si * ki, sr * ki + si * kr], axis=1)
        turned = dot(split_cat(product, 1), backward_ref[r])
        back.append((turned[:, :SUB], turned[:, SUB:]))
    (r0, i0), (r1, i1), (r2, i2), (r3, i3) = back
    er, ei, fr, fi = r0 + r2, i0 + i2, r0 - r2, i0 - i2
    gr, gi, hr, hi = r1 + r3, i1 + i3, r1 - r3, i1 - i3
    real = jnp.concatenate([er + gr, fr - hi, er - gr, fr + hi], axis=1)
    imag = jnp.concatenate([ei + gi, fi + hr, ei - gi, fi - hr], axis=1)
    turned = jnp.concatenate(
        [real * cos_ref[...] - imag * sin_ref[...], imag * cos_ref[...] + real * sin_ref[...]],
        axis=0,
    )
    return dot(leave_ref[...], split_cat(turned, 0)) + skip * signal


def filter_kernel(
    skip_ref, signal_ref, kernel_ref, enter_ref, cos_ref, sin_ref, forward_ref, backward_ref,
    leave_ref, out_ref, spread_ref,
):
    rows = cos_ref.shape[0]
    result = filter_channel(
        signal_ref[...].reshape(rows, LANES), kernel_ref[...].reshape(rows, LANES),
        skip_ref[pl.program_id(0)], enter_ref, cos_ref, sin_ref, forward_ref, backward_ref,
        leave_ref, spread_ref,
    )
    out_ref[...] = result.reshape(out_ref.shape)


def long_filter(signal, kernel, skip, out_groups):
    groups, channels, group_rows, _ = signal.shape
    rows = groups * group_rows
    straight = group_rows % 8 == 0 and (rows // out_groups) % 8 == 0
    in_block = (groups, 1, group_rows, LANES)
    out_shape = (out_groups, channels, rows // out_groups, LANES)
    if not straight:
        signal = signal.transpose(1, 0, 2, 3).reshape(1, channels, rows, LANES)
        kernel = kernel.transpose(1, 0, 2, 3).reshape(1, channels, rows, LANES)
        in_block = (1, 1, rows, LANES)
        out_shape = (1, channels, rows, LANES)
    out_block = (out_shape[0], 1) + out_shape[2:]

    def along(c):
        return (0, c, 0, 0)

    def whole(array):
        return pl.BlockSpec(array.shape, lambda c: (0,) * array.ndim)

    held = tables(rows)
    result = pl.pallas_call(
        filter_kernel,
        grid=(channels,),
        in_specs=[
            pl.BlockSpec(memory_space=pltpu.SMEM),
            pl.BlockSpec(in_block, along),
            pl.BlockSpec(in_block, along),
        ]
        + [whole(table) for table in held],
        out_specs=pl.BlockSpec(out_block, along),
        out_shape=jax.ShapeDtypeStruct(out_shape, F32),
        scratch_shapes=[pltpu.VMEM((RADIX, 2 * rows, 6 * SUB), BF16)],
        compiler_params=pltpu.CompilerParams(vmem_limit_bytes=VMEM_LIMIT),
        cost_estimate=pl.CostEstimate(
            flops=channels * rows * LANES * 2048 * 3 * 3,
            bytes_accessed=channels * rows * LANES * 12,
            transcendentals=0,
        ),
        name="long_filter",
    )(skip, signal, kernel, *held)
    if not straight:
        result = result.reshape(channels, out_groups, rows // out_groups, LANES)
        result = result.transpose(1, 0, 2, 3)
    return result


def mix_block(window_ref, tap_ref, gain_ref, up_ref, bias_ref, down_ref, out_ref, high_ref, low_ref,
              mix_ref):
    block, width = out_ref.shape
    reach = TAPS + 1
    head_width = width // HEADS
    high, low = halves(window_ref[...])
    high_ref[...] = high
    low_ref[...] = low
    taps = dot(
        jnp.concatenate([high[reach:], low[reach:], high[reach:]], axis=1), tap_ref[...]
    )
    for b in range(block // reach):
        for h in range(HEADS):
            own = taps[b * reach : (b + 1) * reach, h * reach : (h + 1) * reach]
            band = jnp.concatenate([own, jnp.zeros_like(own)], axis=1)
            band = pltpu.roll(band, 1, 1, stride=1, stride_axis=0)
            near_rows = slice(b * reach, (b + 2) * reach)
            columns = slice(h * head_width, (h + 1) * head_width)
            near_high = high_ref[near_rows, columns]
            near_low = low_ref[near_rows, columns]
            mix_ref[b * reach : (b + 1) * reach, columns] = dot(
                split_cat(band, 1), jnp.concatenate([near_high, near_high, near_low], axis=0)
            )
    mixed = mix_ref[...]
    mean_square = jnp.mean(mixed * mixed, axis=1, keepdims=True)
    normed = mixed * lax.rsqrt(mean_square + EPSILON) * gain_ref[...]
    raised = dot(split_cat(normed, 1), up_ref[...]) + bias_ref[...]
    inner = math.sqrt(2.0 / math.pi) * (raised + 0.044715 * (raised * raised * raised))
    hidden = 0.5 * raised * (1.0 + jnp.tanh(inner))
    out_ref[...] = mixed + dot(split_cat(hidden, 1), down_ref[...])


def mix_kernel(
    conv_ref, gate_ref, halo_ref, tap_ref, gain_ref, up_ref, bias_ref, down_ref, out_ref,
    window_ref, high_ref, low_ref, mix_ref,
):
    block = gate_ref.shape[0]
    reach = TAPS + 1

    @pl.when(pl.program_id(0) == 0)
    def _():
        window_ref[:reach, :] = halo_ref[...]

    @pl.when(pl.program_id(0) > 0)
    def _():
        window_ref[:reach, :] = window_ref[block : block + reach, :]

    window_ref[reach:, :] = jnp.transpose(conv_ref[0], (1, 0)) * gate_ref[...]
    mix_block(
        window_ref, tap_ref, gain_ref, up_ref, bias_ref, down_ref, out_ref, high_ref, low_ref, mix_ref
    )


def weight_split(weight):
    high = lax.reduce_precision(weight, 8, 7)
    low = weight - high
    return jnp.concatenate([high, high, low], axis=0).astype(BF16)


def fixed_operands(tap_weight, norm_gain, up_weight, up_bias, down_weight):
    width = tap_weight.shape[0]
    taps = tap_weight.reshape(width, HEADS, TAPS)[:, :, ::-1]
    taps = jnp.pad(taps, ((0, 0), (0, 0), (1, 0))).reshape(width, HEADS * (TAPS + 1))
    return (
        weight_split(taps),
        norm_gain.reshape(1, -1),
        weight_split(up_weight),
        up_bias.reshape(1, -1),
        weight_split(down_weight),
    )


def tail(conv_blocks, gate_input, halo, fixed):
    count, width, block = conv_blocks.shape
    reach = TAPS + 1
    hidden = fixed[3].shape[1]

    def whole(array):
        return pl.BlockSpec(array.shape, lambda r: (0,) * array.ndim)

    return pl.pallas_call(
        mix_kernel,
        grid=(count,),
        in_specs=[
            pl.BlockSpec((1, width, block), lambda r: (r, 0, 0)),
            pl.BlockSpec((block, width), lambda r: (r, 0)),
            whole(halo),
        ]
        + [whole(array) for array in fixed],
        out_specs=pl.BlockSpec((block, width), lambda r: (r, 0)),
        out_shape=jax.ShapeDtypeStruct(gate_input.shape, F32),
        scratch_shapes=[
            pltpu.VMEM((block + reach, width), F32),
            pltpu.VMEM((block + reach, width), BF16),
            pltpu.VMEM((block + reach, width), BF16),
            pltpu.VMEM((block, width), F32),
        ],
        compiler_params=pltpu.CompilerParams(vmem_limit_bytes=VMEM_LIMIT),
        cost_estimate=pl.CostEstimate(
            flops=count * block * 3 * 2 * (2 * width * hidden + 3 * width * width),
            bytes_accessed=count * block * width * 12,
            transcendentals=count * block * hidden,
        ),
        name="mix_and_mlp",
    )(conv_blocks, gate_input, halo, *fixed)


FIRST_PAIRS = 3


def exchange(low, high, distance):
    count = low.shape[0]
    lower = lax.broadcasted_iota(jnp.int32, low.shape, 0) % (2 * distance) < distance
    return (
        jnp.where(lower, low, pltpu.roll(high, distance, 0)),
        jnp.where(lower, pltpu.roll(low, count - distance, 0), high),
    )


def turn_kernel(signal_ref, kernel_ref, first_ref, second_ref):
    groups, pairs = first_ref.shape[:2]
    for j in range(LANES // 128):
        parts = []
        for row in range(2):
            span = slice(row * LANES + j * 128, row * LANES + (j + 1) * 128)
            parts.append(jnp.transpose(signal_ref[span, :], (1, 0)))
            parts.append(jnp.transpose(kernel_ref[span, :], (1, 0)))
        a0, a2 = exchange(parts[0], parts[2], 4)
        a1, a3 = exchange(parts[1], parts[3], 4)
        for q, value in enumerate(exchange(a0, a1, 2) + exchange(a2, a3, 2)):
            value = value.reshape(groups, 8, 128)
            if q < pairs:
                first_ref[:, q, j, 0] = value
            else:
                second_ref[:, q - pairs, j, 0] = value


def turn(signal, kernel, groups):
    frames, width = signal.shape
    chunk = 2 * LANES
    steps = frames // chunk
    lane_tiles = LANES // 128
    block = pl.BlockSpec((chunk, width), lambda i: (i, 0))
    counts = (FIRST_PAIRS, 4 - FIRST_PAIRS)
    return pl.pallas_call(
        turn_kernel,
        grid=(steps,),
        in_specs=[block, block],
        out_specs=[
            pl.BlockSpec((groups, n, lane_tiles, 1, 8, 128), lambda i: (0, 0, 0, i, 0, 0))
            for n in counts
        ],
        out_shape=[
            jax.ShapeDtypeStruct((groups, n, lane_tiles, steps, 8, 128), F32) for n in counts
        ],
        compiler_params=pltpu.CompilerParams(vmem_limit_bytes=VMEM_LIMIT),
        name="turn",
    )(signal, kernel)


def gather_channel(ref, slot):
    groups, _, lane_tiles, depth, _ = ref.shape
    rows = depth // 4
    return jnp.concatenate(
        [
            jnp.concatenate(
                [ref[g, 0, j, pl.ds(slot, rows, stride=4), :] for g in range(groups)], axis=0
            )
            for j in range(lane_tiles)
        ],
        axis=1,
    )


def scatter_channel(ref, slot, value):
    tiles = LANES // 128
    for j in range(tiles):
        ref[pl.ds(8 * j + slot, value.shape[0], stride=8 * tiles), :] = (
            value[:, j * 128 : (j + 1) * 128]
        )


def first_channels_kernel(skip_ref, data_ref, *rest):
    *table_refs, out_ref, spread_ref = rest
    c = pl.program_id(0)
    result = filter_channel(
        gather_channel(data_ref, c % 2), gather_channel(data_ref, 2 + c % 2), skip_ref[c],
        *table_refs, spread_ref,
    )
    scatter_channel(out_ref, c, result)


def last_channels_kernel(late, skip_ref, data_ref, *rest):
    *table_refs, before_ref, _, _, _, _, late_ref, early_ref, spread_ref, held_ref, sems = rest
    c = pl.program_id(0)
    channel = c + 2 * FIRST_PAIRS
    devices, tiles = late_ref.shape[0], late_ref.shape[1] + early_ref.shape[1] - 1
    load = pltpu.make_async_copy(before_ref, held_ref, sems.at[0])

    @pl.when(c == 0)
    def _():
        load.start()

    result = filter_channel(
        gather_channel(data_ref, c % 2), gather_channel(data_ref, 2 + c % 2),
        skip_ref[channel], *table_refs, spread_ref,
    )

    @pl.when(c == 0)
    def _():
        load.wait()

    scatter_channel(held_ref, channel, result)

    @pl.when(c == pl.num_programs(0) - 1)
    def _():
        shaped = held_ref.reshape(devices, tiles, 8, 128)
        final = shaped.at[:, tiles - 1 : tiles]
        pairs = (
            (shaped.at[:, late:tiles], late_ref.at[:, 0 : tiles - late]),
            (shaped.at[:, late - 1 : late], late_ref.at[:, tiles - late : tiles - late + 1]),
            (shaped.at[:, 0 : late - 1], early_ref.at[:, 0 : late - 1]),
            (final.at[0 : devices - 1], early_ref.at[1:devices, late - 1 : late]),
            (final.at[devices - 1 : devices], early_ref.at[0:1, late - 1 : late]),
        )
        copies = [
            pltpu.make_async_copy(here, there, sems.at[1 + i])
            for i, (here, there) in enumerate(pairs)
        ]
        for copy in copies:
            copy.start()
        for copy in copies:
            copy.wait()


def filter_pairs(data, skip, before, devices, late, ready=()):
    groups, pairs, lane_tiles, row_pairs, _, _ = data.shape
    flat = data.reshape(groups, pairs, lane_tiles, row_pairs * 8, 128)
    rows = groups * row_pairs * 2
    tiles = rows * lane_tiles // devices
    held = tables(rows)
    held_shape = (rows * lane_tiles * 8, 128)

    def whole(array):
        return pl.BlockSpec(array.shape, lambda c: (0,) * array.ndim)

    in_specs = [
        pl.BlockSpec(memory_space=pltpu.SMEM),
        pl.BlockSpec(
            (groups, 1, lane_tiles, row_pairs * 8, 128), lambda c: (0, c // 2, 0, 0, 0)
        ),
    ] + [whole(t) for t in held]
    spread = pltpu.VMEM((RADIX, 2 * rows, 6 * SUB), BF16)
    options = dict(
        grid=(2 * pairs,),
        compiler_params=pltpu.CompilerParams(vmem_limit_bytes=VMEM_LIMIT),
        cost_estimate=pl.CostEstimate(
            flops=2 * pairs * rows * LANES * 2048 * 3 * 3,
            bytes_accessed=2 * pairs * rows * LANES * 12,
            transcendentals=0,
        ),
    )
    if before is None:
        return pl.pallas_call(
            first_channels_kernel,
            in_specs=in_specs,
            out_specs=pl.BlockSpec(held_shape, lambda c: (0, 0)),
            out_shape=jax.ShapeDtypeStruct(held_shape, F32),
            scratch_shapes=[spread],
            name="filter_first",
            **options,
        )(skip, flat, *held)
    anywhere = pl.BlockSpec(memory_space=pl.ANY)
    return pl.pallas_call(
        functools.partial(last_channels_kernel, late),
        in_specs=in_specs + [anywhere] * (1 + len(ready)),
        out_specs=[anywhere, anywhere],
        out_shape=[
            jax.ShapeDtypeStruct((devices, tiles - late + 1, 8, 128), F32),
            jax.ShapeDtypeStruct((devices, late, 8, 128), F32),
        ],
        scratch_shapes=[spread, pltpu.VMEM(held_shape, F32), pltpu.SemaphoreType.DMA((6,))],
        name="filter_last",
        **options,
    )(skip, flat, *held, before, *ready)


def frames_by_channels(tile):
    paired = tile.reshape(tile.shape[0] // HEADS, HEADS, 8, 128)
    return jnp.concatenate(
        [jnp.transpose(paired[:, h].reshape(-1, 128), (1, 0)) for h in range(HEADS)], axis=1
    )


def late_kernel(conv_ref, edge_ref, gate_ref, edge_gate_ref, *rest):
    *fixed, out_ref, window_ref, high_ref, low_ref, mix_ref = rest
    block = gate_ref.shape[0]
    reach = TAPS + 1

    @pl.when(pl.program_id(0) == 0)
    def _():
        window_ref[:reach, :] = frames_by_channels(edge_ref[:, 0]) * edge_gate_ref[...]

    @pl.when(pl.program_id(0) > 0)
    def _():
        window_ref[:reach, :] = window_ref[block : block + reach, :]

    for j in range(block // reach):
        span = slice(j * reach, (j + 1) * reach)
        window_ref[reach + j * reach : 2 * reach + j * reach, :] = (
            frames_by_channels(conv_ref[:, j]) * gate_ref[span, :]
        )
    mix_block(window_ref, *fixed, out_ref, high_ref, low_ref, mix_ref)


def early_kernel(conv_ref, edge_ref, gate_ref, halo_ref, halo_gate_ref, *rest):
    *fixed, _, out_ref, window_ref, high_ref, low_ref, mix_ref = rest
    block = gate_ref.shape[0]
    reach = TAPS + 1
    last = pl.program_id(0) == pl.num_programs(0) - 1

    @pl.when(pl.program_id(0) == 0)
    def _():
        window_ref[:reach, :] = frames_by_channels(halo_ref[:, 0]) * halo_gate_ref[...]

    @pl.when(pl.program_id(0) > 0)
    def _():
        window_ref[:reach, :] = window_ref[block : block + reach, :]

    count = block // reach
    for j in range(count):
        tile = conv_ref[:, j]
        if j == count - 1:
            tile = jnp.where(last, edge_ref[:, 0], tile)
        span = slice(j * reach, (j + 1) * reach)
        window_ref[reach + j * reach : 2 * reach + j * reach, :] = (
            frames_by_channels(tile) * gate_ref[span, :]
        )
    mix_block(window_ref, *fixed, out_ref, high_ref, low_ref, mix_ref)


def tail_part(conv, late, gate_input, halo_gate, before, late_tiles, fixed):
    devices = conv.shape[0]
    frames, width = gate_input.shape
    reach = TAPS + 1
    block = 512
    per_block = block // 128
    edge = late.shape[1] - 1
    first = before is not None

    def whole(array):
        return pl.BlockSpec(array.shape, lambda r: (0,) * array.ndim)

    start = 0 if first else late_tiles // per_block
    count = (late_tiles if first else edge) // per_block
    in_specs = [
        pl.BlockSpec((devices, per_block, 8, 128), lambda r: (0, r, 0, 0)),
        pl.BlockSpec((devices, 1, 8, 128), lambda r: (0, edge, 0, 0)),
        pl.BlockSpec((block, width), lambda r: (r + start, 0)),
    ]
    operands = [conv, late, gate_input]
    if first:
        ahead = late_tiles - 1
        in_specs += [pl.BlockSpec((devices, 1, 8, 128), lambda r: (0, ahead, 0, 0)), whole(halo_gate)]
        operands += [conv, halo_gate]
    else:
        in_specs += [pl.BlockSpec((reach, width), lambda r: (late_tiles - 1, 0))]
        operands += [gate_input]
    in_specs += [whole(array) for array in fixed]
    operands += fixed
    aliases = {}
    if first:
        aliases = {len(operands): 0}
        in_specs += [pl.BlockSpec(memory_space=pl.ANY)]
        operands += [before]
    hidden = fixed[3].shape[1]
    return pl.pallas_call(
        early_kernel if first else late_kernel,
        grid=(count,),
        in_specs=in_specs,
        out_specs=pl.BlockSpec((block, width), lambda r: (r + start, 0)),
        out_shape=jax.ShapeDtypeStruct(gate_input.shape, F32),
        input_output_aliases=aliases,
        scratch_shapes=[
            pltpu.VMEM((block + reach, width), F32),
            pltpu.VMEM((block + reach, width), BF16),
            pltpu.VMEM((block + reach, width), BF16),
            pltpu.VMEM((block, width), F32),
        ],
        compiler_params=pltpu.CompilerParams(vmem_limit_bytes=VMEM_LIMIT),
        cost_estimate=pl.CostEstimate(
            flops=count * block * 3 * 2 * (2 * width * hidden + 3 * width * width),
            bytes_accessed=count * block * width * 12,
            transcendentals=count * block * hidden,
        ),
        name="mix_early" if first else "mix_late",
    )(*operands)


def owned_eight(signal, kernel, skip_here, gate_input, fixed):
    groups = lax.axis_size("tm")
    devices = groups * lax.axis_size("chan")
    reach = TAPS + 1
    late_tiles = 2 * (512 // 128)

    def enter(array):
        return lax.all_to_all(array, "tm", split_axis=0, concat_axis=0, tiled=True)

    def leave(array):
        return lax.all_to_all(array, ("tm", "chan"), split_axis=0, concat_axis=0, tiled=True)

    ring = [(i, i + 1) for i in range(devices - 1)]
    halo_gate = lax.ppermute(gate_input[-reach:], ("tm", "chan"), ring)
    one, two = turn(signal, kernel, groups)
    before = filter_pairs(enter(one), skip_here, None, devices, late_tiles)
    ready = (fixed[0], fixed[2], fixed[4], halo_gate)
    late, early = filter_pairs(enter(two), skip_here, before, devices, late_tiles, ready)
    late = leave(late)
    early = leave(early)
    part = tail_part(late, late, gate_input, None, None, late_tiles, fixed)
    return tail_part(early, late, gate_input, halo_gate, part, late_tiles, fixed)


def on_device(
    signal, kernel, skip_gain, gate_input, tap_weight, norm_gain, up_weight, up_bias, down_weight
):
    groups = lax.axis_size("tm")
    pair = lax.axis_size("chan")
    frames_here, channels_here = signal.shape
    owned = channels_here // groups
    width = gate_input.shape[1]
    first_channel = lax.axis_index("chan") * channels_here + lax.axis_index("tm") * owned
    skip_here = lax.dynamic_slice_in_dim(skip_gain, first_channel, owned)
    fixed = fixed_operands(tap_weight, norm_gain, up_weight, up_bias, down_weight)
    window = frames_here * groups
    if owned == 8 and channels_here == 128 and pair == HEADS and window == 256 * LANES:
        if gate_input.shape[0] % 512 == 0 and gate_input.shape[0] >= 2048:
            return owned_eight(signal, kernel, skip_here, gate_input, fixed)

    def enter(array):
        shaped = array.reshape(frames_here // LANES, LANES, groups, owned).transpose(2, 3, 0, 1)
        return lax.all_to_all(shaped, "tm", split_axis=0, concat_axis=0, tiled=True)

    filtered = long_filter(enter(signal), enter(kernel), skip_here, groups * pair)
    back = lax.all_to_all(filtered, ("tm", "chan"), split_axis=0, concat_axis=0, tiled=True)
    blocks = back.reshape(groups, pair, owned, -1, LANES).transpose(3, 1, 0, 2, 4)
    blocks = blocks.reshape(-1, width, LANES)
    reach = TAPS + 1
    last = blocks[-1, :, LANES - reach :].T * gate_input[-reach:]
    devices = groups * pair
    halo = lax.ppermute(last, ("tm", "chan"), [(i, i + 1) for i in range(devices - 1)])
    return tail(blocks, gate_input, halo, fixed)


def solution(mesh):
    placed = (
        P(("grp", "tm"), "chan"),
        P("tm", "chan"),
        P(),
        P(("grp", "tm", "chan"), None),
        P(),
        P(),
        P(),
        P(),
        P(),
    )
    return jax.shard_map(
        on_device,
        mesh=mesh,
        in_specs=placed,
        out_specs=P(("grp", "tm", "chan"), None),
        check_vma=False,
    )
```

```python
import functools
import math

import jax
import jax.numpy as jnp
import numpy as np
from jax import lax
from jax.experimental import pallas as pl
from jax.experimental.pallas import tpu as pltpu
from jax.sharding import PartitionSpec as P
import ml_dtypes

LANES = 512
RADIX = 4
SUB = LANES // RADIX
TAPS = 127
HEADS = 2
EPSILON = 1e-06
BF16 = jnp.bfloat16
F32 = jnp.float32
VMEM_LIMIT = 56 * 1024 * 1024


def table_split(table, axis, order):
    high = table.astype(ml_dtypes.bfloat16)
    low = (table - high.astype(np.float64)).astype(ml_dtypes.bfloat16)
    parts = {"h": high, "l": low}
    return np.concatenate([parts[name] for name in order], axis=axis)


@functools.lru_cache(maxsize=None)
def tables(rows):
    length = rows * LANES
    turn = 2.0 * math.pi
    n1 = np.arange(rows, dtype=np.float64)
    n2 = np.arange(LANES, dtype=np.float64)
    m = np.arange(SUB, dtype=np.float64)
    first = turn * np.outer(n1 + 0.25, n1) / rows
    enter = table_split(np.concatenate([np.cos(first), -np.sin(first)], axis=0), 1, "hhl")
    leave = table_split(
        np.concatenate([np.cos(first.T), -np.sin(first.T)], axis=1) / length, 1, "hhl"
    )
    twiddle = turn * np.outer(n1 + 0.25, n2) / length
    forward, backward = [], []
    for r in range(RADIX):
        phase = turn * np.outer(m, m / SUB + r / LANES)
        c, s = np.cos(phase), np.sin(phase)
        forward.append(table_split(np.block([[c, -s], [s, c]]), 0, "hhl"))
        c, s = c.T, s.T
        backward.append(table_split(np.block([[c, s], [-s, c]]), 0, "hhl"))
    return (
        enter,
        np.cos(twiddle).astype(np.float32),
        np.sin(twiddle).astype(np.float32),
        np.stack(forward),
        np.stack(backward),
        leave,
    )


def halves(value):
    high = value.astype(BF16)
    low = (value - high.astype(F32)).astype(BF16)
    return high, low


def split_cat(value, axis):
    high, low = halves(value)
    return jnp.concatenate([high, low, high], axis=axis)


def dot(left, right):
    return jnp.dot(left, right, preferred_element_type=F32)


def filter_channel(signal, kernel, skip, enter_ref, cos_ref, sin_ref, forward_ref, backward_ref,
                   leave_ref):
    rows = cos_ref.shape[0]
    entered = [dot(enter_ref[...], split_cat(value, 0)) for value in (signal, kernel)]
    spectra = []
    for turned in entered:
        real_in, imag_in = turned[:rows], turned[rows:]
        real = real_in * cos_ref[...] + imag_in * sin_ref[...]
        imag = imag_in * cos_ref[...] - real_in * sin_ref[...]
        r0, r1, r2, r3 = (real[:, b * SUB : (b + 1) * SUB] for b in range(RADIX))
        i0, i1, i2, i3 = (imag[:, b * SUB : (b + 1) * SUB] for b in range(RADIX))
        er, ei, fr, fi = r0 + r2, i0 + i2, r0 - r2, i0 - i2
        gr, gi, hr, hi = r1 + r3, i1 + i3, r1 - r3, i1 - i3
        spread = ((er + gr, ei + gi), (fr + hi, fi - hr), (er - gr, ei - gi), (fr - hi, fi + hr))
        spectra.append([
            dot(split_cat(jnp.concatenate(pair, axis=1), 1), forward_ref[r])
            for r, pair in enumerate(spread)
        ])
    products = []
    for s, k in zip(*spectra):
        sr, si = s[:, :SUB], s[:, SUB:]
        kr, ki = k[:, :SUB], k[:, SUB:]
        product = jnp.concatenate([sr * kr - si * ki, sr * ki + si * kr], axis=1)
        products.append(split_cat(product, 1))
    back = []
    for r in range(RADIX):
        turned = dot(products[r], backward_ref[r])
        back.append((turned[:, :SUB], turned[:, SUB:]))
    (r0, i0), (r1, i1), (r2, i2), (r3, i3) = back
    er, ei, fr, fi = r0 + r2, i0 + i2, r0 - r2, i0 - i2
    gr, gi, hr, hi = r1 + r3, i1 + i3, r1 - r3, i1 - i3
    real = jnp.concatenate([er + gr, fr - hi, er - gr, fr + hi], axis=1)
    imag = jnp.concatenate([ei + gi, fi + hr, ei - gi, fi - hr], axis=1)
    turned = jnp.concatenate(
        [real * cos_ref[...] - imag * sin_ref[...], imag * cos_ref[...] + real * sin_ref[...]],
        axis=0,
    )
    return dot(leave_ref[...], split_cat(turned, 0)) + skip * signal


def filter_kernel(
    skip_ref, signal_ref, kernel_ref, enter_ref, cos_ref, sin_ref, forward_ref, backward_ref,
    leave_ref, out_ref,
):
    rows = cos_ref.shape[0]
    result = filter_channel(
        signal_ref[...].reshape(rows, LANES), kernel_ref[...].reshape(rows, LANES),
        skip_ref[pl.program_id(0)], enter_ref, cos_ref, sin_ref, forward_ref, backward_ref,
        leave_ref,
    )
    out_ref[...] = result.reshape(out_ref.shape)


def long_filter(signal, kernel, skip, out_groups):
    groups, channels, group_rows, _ = signal.shape
    rows = groups * group_rows
    straight = group_rows % 8 == 0 and (rows // out_groups) % 8 == 0
    in_block = (groups, 1, group_rows, LANES)
    out_shape = (out_groups, channels, rows // out_groups, LANES)
    if not straight:
        signal = signal.transpose(1, 0, 2, 3).reshape(1, channels, rows, LANES)
        kernel = kernel.transpose(1, 0, 2, 3).reshape(1, channels, rows, LANES)
        in_block = (1, 1, rows, LANES)
        out_shape = (1, channels, rows, LANES)
    out_block = (out_shape[0], 1) + out_shape[2:]

    def along(c):
        return (0, c, 0, 0)

    def whole(array):
        return pl.BlockSpec(array.shape, lambda c: (0,) * array.ndim)

    held = tables(rows)
    result = pl.pallas_call(
        filter_kernel,
        grid=(channels,),
        in_specs=[
            pl.BlockSpec(memory_space=pltpu.SMEM),
            pl.BlockSpec(in_block, along),
            pl.BlockSpec(in_block, along),
        ]
        + [whole(table) for table in held],
        out_specs=pl.BlockSpec(out_block, along),
        out_shape=jax.ShapeDtypeStruct(out_shape, F32),
        compiler_params=pltpu.CompilerParams(vmem_limit_bytes=VMEM_LIMIT),
        cost_estimate=pl.CostEstimate(
            flops=channels * rows * LANES * 2048 * 3 * 3,
            bytes_accessed=channels * rows * LANES * 12,
            transcendentals=0,
        ),
        name="long_filter",
    )(skip, signal, kernel, *held)
    if not straight:
        result = result.reshape(channels, out_groups, rows // out_groups, LANES)
        result = result.transpose(1, 0, 2, 3)
    return result


def split_weights(tap_ref, up_ref, down_ref, taps_ref, ups_ref, downs_ref):
    def stacked(weight):
        high, low = halves(weight)
        return jnp.concatenate([high, high, low], axis=0)

    taps_ref[...] = stacked(tap_ref[...])
    chunks, _, chunk = ups_ref.shape
    for n in range(chunks):
        span = slice(n * chunk, (n + 1) * chunk)
        ups_ref[n] = stacked(up_ref[:, span])
        downs_ref[n] = stacked(down_ref[span, :])


def mix_block(window_ref, gain_ref, bias_ref, out_ref, high_ref, low_ref, mix_ref, taps_ref, ups_ref,
              downs_ref):
    block, width = out_ref.shape
    reach = TAPS + 1
    head_width = width // HEADS
    high, low = halves(window_ref[...])
    high_ref[...] = high
    low_ref[...] = low
    taps = dot(
        jnp.concatenate([high[reach:], low[reach:], high[reach:]], axis=1), taps_ref[...]
    )
    for b in range(block // reach):
        for h in range(HEADS):
            own = taps[b * reach : (b + 1) * reach, h * reach : (h + 1) * reach]
            band = jnp.concatenate([own, jnp.zeros_like(own)], axis=1)
            band = pltpu.roll(band, 1, 1, stride=1, stride_axis=0)
            near_rows = slice(b * reach, (b + 2) * reach)
            columns = slice(h * head_width, (h + 1) * head_width)
            near_high = high_ref[near_rows, columns]
            near_low = low_ref[near_rows, columns]
            mix_ref[b * reach : (b + 1) * reach, columns] = dot(
                split_cat(band, 1), jnp.concatenate([near_high, near_high, near_low], axis=0)
            )
    mixed = mix_ref[...]
    mean_square = jnp.mean(mixed * mixed, axis=1, keepdims=True)
    normed = split_cat(mixed * lax.rsqrt(mean_square + EPSILON) * gain_ref[...], 1)
    total = mixed
    chunks, _, chunk = ups_ref.shape
    scale = math.sqrt(2.0 / math.pi)
    for n in range(chunks):
        raised = dot(normed, ups_ref[n]) + bias_ref[:, n * chunk : (n + 1) * chunk]
        inner = raised * (scale + (scale * 0.044715) * (raised * raised))
        half = 0.5 * raised
        total = total + dot(split_cat(half + half * jnp.tanh(inner), 1), downs_ref[n])
    out_ref[...] = total


def mix_scratch(block, width, hidden):
    reach = TAPS + 1
    chunk = 256 if hidden % 256 == 0 else hidden
    return [
        pltpu.VMEM((block + reach, width), F32),
        pltpu.VMEM((block + reach, width), BF16),
        pltpu.VMEM((block + reach, width), BF16),
        pltpu.VMEM((block, width), F32),
        pltpu.VMEM((3 * width, HEADS * reach), BF16),
        pltpu.VMEM((hidden // chunk, 3 * width, chunk), BF16),
        pltpu.VMEM((hidden // chunk, 3 * chunk, width), BF16),
    ]


def mix_window(window_ref, fixed, scratch, out_ref):
    tap_ref, gain_ref, up_ref, bias_ref, down_ref = fixed
    weights = scratch[3:]

    @pl.when(pl.program_id(0) == 0)
    def _():
        split_weights(tap_ref, up_ref, down_ref, *weights)

    mix_block(window_ref, gain_ref, bias_ref, out_ref, *scratch)


def mix_kernel(conv_ref, gate_ref, halo_ref, *rest):
    fixed, out_ref, window_ref, scratch = rest[:5], rest[5], rest[6], rest[7:]
    block = gate_ref.shape[0]
    reach = TAPS + 1

    @pl.when(pl.program_id(0) == 0)
    def _():
        window_ref[:reach, :] = halo_ref[...]

    @pl.when(pl.program_id(0) > 0)
    def _():
        window_ref[:reach, :] = window_ref[block : block + reach, :]

    window_ref[reach:, :] = jnp.transpose(conv_ref[0], (1, 0)) * gate_ref[...]
    mix_window(window_ref, fixed, scratch, out_ref)


def fixed_operands(tap_weight, norm_gain, up_weight, up_bias, down_weight):
    width = tap_weight.shape[0]
    taps = tap_weight.reshape(width, HEADS, TAPS)[:, :, ::-1]
    taps = jnp.pad(taps, ((0, 0), (0, 0), (1, 0))).reshape(width, HEADS * (TAPS + 1))
    return (
        taps,
        norm_gain.reshape(1, -1),
        up_weight,
        up_bias.reshape(1, -1),
        down_weight,
    )


def tail(conv_blocks, gate_input, halo, fixed):
    count, width, block = conv_blocks.shape
    reach = TAPS + 1
    hidden = fixed[3].shape[1]

    def whole(array):
        return pl.BlockSpec(array.shape, lambda r: (0,) * array.ndim)

    return pl.pallas_call(
        mix_kernel,
        grid=(count,),
        in_specs=[
            pl.BlockSpec((1, width, block), lambda r: (r, 0, 0)),
            pl.BlockSpec((block, width), lambda r: (r, 0)),
            whole(halo),
        ]
        + [whole(array) for array in fixed],
        out_specs=pl.BlockSpec((block, width), lambda r: (r, 0)),
        out_shape=jax.ShapeDtypeStruct(gate_input.shape, F32),
        scratch_shapes=mix_scratch(block, width, hidden),
        compiler_params=pltpu.CompilerParams(vmem_limit_bytes=VMEM_LIMIT),
        cost_estimate=pl.CostEstimate(
            flops=count * block * 3 * 2 * (2 * width * hidden + 3 * width * width),
            bytes_accessed=count * block * width * 12,
            transcendentals=count * block * hidden,
        ),
        name="mix_and_mlp",
    )(conv_blocks, gate_input, halo, *fixed)


FIRST_CHANNELS = 7
TURN_ROWS = 4


def turn_kernel(signal_ref, kernel_ref, first_ref, second_ref):
    groups, early, rows = first_ref.shape[:3]
    late = second_ref.shape[1]
    stride = rows * 8
    first = first_ref.reshape(groups * early * stride, 128)
    second = second_ref.reshape(groups * late * stride, 128)
    for row in range(rows):
        for j in range(LANES // 128):
            span = slice(row * LANES + j * 128, row * LANES + (j + 1) * 128)
            for which, ref in enumerate((signal_ref, kernel_ref)):
                turned = jnp.transpose(ref[span, :], (1, 0))
                place = row * 8 + j * 2 + which
                for g in range(groups):
                    own = turned[g * 8 : (g + 1) * 8]
                    first[pl.ds(g * early * stride + place, early, stride=stride), :] = own[:early]
                    second[pl.ds(g * late * stride + place, late, stride=stride), :] = own[early:]


def turn(signal, kernel, groups):
    frames, width = signal.shape
    chunk = TURN_ROWS * LANES
    rows = frames // LANES
    block = pl.BlockSpec((chunk, width), lambda i: (i, 0))
    counts = (FIRST_CHANNELS, 8 - FIRST_CHANNELS)
    return pl.pallas_call(
        turn_kernel,
        grid=(frames // chunk,),
        in_specs=[block, block],
        out_specs=[
            pl.BlockSpec((groups, n, TURN_ROWS, 8, 128), lambda i: (0, 0, i, 0, 0)) for n in counts
        ],
        out_shape=[jax.ShapeDtypeStruct((groups, n, rows, 8, 128), F32) for n in counts],
        compiler_params=pltpu.CompilerParams(vmem_limit_bytes=VMEM_LIMIT),
        name="turn",
    )(signal, kernel)


def gather_channel(ref, which):
    groups, _, depth, _ = ref.shape
    tiles = LANES // 128
    flat = ref.reshape(groups * depth, 128)
    rows = groups * depth // 8
    return jnp.concatenate(
        [flat[pl.ds(2 * j + which, rows, stride=8), :] for j in range(tiles)], axis=1
    )


def scatter_channel(ref, slot, value):
    tiles = LANES // 128
    for j in range(tiles):
        ref[pl.ds(8 * j + slot, value.shape[0], stride=8 * tiles), :] = (
            value[:, j * 128 : (j + 1) * 128]
        )


def first_channels_kernel(skip_ref, data_ref, *rest):
    *table_refs, out_ref = rest
    c = pl.program_id(0)
    result = filter_channel(
        gather_channel(data_ref, 0), gather_channel(data_ref, 1), skip_ref[c],
        *table_refs,
    )
    scatter_channel(out_ref, c, result)


def last_channels_kernel(late, extra, skip_ref, data_ref, *rest):
    *table_refs, before_ref = rest[: len(rest) - 4 - extra]
    late_ref, early_ref, held_ref, sems = rest[-4:]
    c = pl.program_id(0)
    channel = c + FIRST_CHANNELS
    devices, tiles = late_ref.shape[0], late_ref.shape[1] + early_ref.shape[1] - 1
    load = pltpu.make_async_copy(before_ref, held_ref, sems.at[0])

    @pl.when(c == 0)
    def _():
        load.start()

    result = filter_channel(
        gather_channel(data_ref, 0), gather_channel(data_ref, 1),
        skip_ref[channel], *table_refs,
    )

    @pl.when(c == 0)
    def _():
        load.wait()

    scatter_channel(held_ref, channel, result)

    @pl.when(c == pl.num_programs(0) - 1)
    def _():
        shaped = held_ref.reshape(devices, tiles, 8, 128)
        final = shaped.at[:, tiles - 1 : tiles]
        pairs = (
            (shaped.at[:, late:tiles], late_ref.at[:, 0 : tiles - late]),
            (shaped.at[:, late - 1 : late], late_ref.at[:, tiles - late : tiles - late + 1]),
            (shaped.at[:, 0 : late - 1], early_ref.at[:, 0 : late - 1]),
            (final.at[0 : devices - 1], early_ref.at[1:devices, late - 1 : late]),
            (final.at[devices - 1 : devices], early_ref.at[0:1, late - 1 : late]),
        )
        copies = [
            pltpu.make_async_copy(here, there, sems.at[1 + i])
            for i, (here, there) in enumerate(pairs)
        ]
        for copy in copies:
            copy.start()
        for copy in copies:
            copy.wait()


def filter_channels(data, skip, before, devices, late, ready=()):
    groups, channels, group_rows, _, _ = data.shape
    flat = data.reshape(groups, channels, group_rows * 8, 128)
    rows = groups * group_rows
    lane_tiles = LANES // 128
    tiles = rows * lane_tiles // devices
    held = tables(rows)
    held_shape = (rows * lane_tiles * 8, 128)

    def whole(array):
        return pl.BlockSpec(array.shape, lambda c: (0,) * array.ndim)

    in_specs = [
        pl.BlockSpec(memory_space=pltpu.SMEM),
        pl.BlockSpec(
            (groups, 1, group_rows * 8, 128), lambda c: (0, c, 0, 0)
        ),
    ] + [whole(t) for t in held]
    options = dict(
        grid=(channels,),
        compiler_params=pltpu.CompilerParams(vmem_limit_bytes=VMEM_LIMIT),
        cost_estimate=pl.CostEstimate(
            flops=channels * rows * LANES * 2048 * 3 * 3,
            bytes_accessed=channels * rows * LANES * 12,
            transcendentals=0,
        ),
    )
    if before is None:
        return pl.pallas_call(
            first_channels_kernel,
            in_specs=in_specs,
            out_specs=pl.BlockSpec(held_shape, lambda c: (0, 0)),
            out_shape=jax.ShapeDtypeStruct(held_shape, F32),
            name="filter_first",
            **options,
        )(skip, flat, *held)
    anywhere = pl.BlockSpec(memory_space=pl.ANY)
    return pl.pallas_call(
        functools.partial(last_channels_kernel, late, len(ready)),
        in_specs=in_specs + [anywhere] * (1 + len(ready)),
        out_specs=[anywhere, anywhere],
        out_shape=[
            jax.ShapeDtypeStruct((devices, tiles - late + 1, 8, 128), F32),
            jax.ShapeDtypeStruct((devices, late, 8, 128), F32),
        ],
        scratch_shapes=[pltpu.VMEM(held_shape, F32), pltpu.SemaphoreType.DMA((6,))],
        name="filter_last",
        **options,
    )(skip, flat, *held, before, *ready)


def frames_by_channels(tile):
    paired = tile.reshape(tile.shape[0] // HEADS, HEADS, 8, 128)
    return jnp.concatenate(
        [jnp.transpose(paired[:, h].reshape(-1, 128), (1, 0)) for h in range(HEADS)], axis=1
    )


def late_kernel(conv_ref, edge_ref, gate_ref, edge_gate_ref, *rest):
    fixed, out_ref, window_ref, scratch = rest[:5], rest[5], rest[6], rest[7:]
    block = gate_ref.shape[0]
    reach = TAPS + 1

    @pl.when(pl.program_id(0) == 0)
    def _():
        window_ref[:reach, :] = frames_by_channels(edge_ref[:, 0]) * edge_gate_ref[...]

    @pl.when(pl.program_id(0) > 0)
    def _():
        window_ref[:reach, :] = window_ref[block : block + reach, :]

    for j in range(block // reach):
        span = slice(j * reach, (j + 1) * reach)
        window_ref[reach + j * reach : 2 * reach + j * reach, :] = (
            frames_by_channels(conv_ref[:, j]) * gate_ref[span, :]
        )
    mix_window(window_ref, fixed, scratch, out_ref)


def early_kernel(conv_ref, edge_ref, gate_ref, halo_ref, halo_gate_ref, *rest):
    fixed, out_ref, window_ref, scratch = rest[:5], rest[6], rest[7], rest[8:]
    block = gate_ref.shape[0]
    reach = TAPS + 1
    last = pl.program_id(0) == pl.num_programs(0) - 1

    @pl.when(pl.program_id(0) == 0)
    def _():
        window_ref[:reach, :] = frames_by_channels(halo_ref[:, 0]) * halo_gate_ref[...]

    @pl.when(pl.program_id(0) > 0)
    def _():
        window_ref[:reach, :] = window_ref[block : block + reach, :]

    count = block // reach
    for j in range(count):
        tile = conv_ref[:, j]
        if j == count - 1:
            tile = jnp.where(last, edge_ref[:, 0], tile)
        span = slice(j * reach, (j + 1) * reach)
        window_ref[reach + j * reach : 2 * reach + j * reach, :] = (
            frames_by_channels(tile) * gate_ref[span, :]
        )
    mix_window(window_ref, fixed, scratch, out_ref)


def tail_part(conv, late, gate_input, halo_gate, before, late_tiles, fixed):
    devices = conv.shape[0]
    frames, width = gate_input.shape
    reach = TAPS + 1
    block = 512
    per_block = block // 128
    edge = late.shape[1] - 1
    first = before is not None

    def whole(array):
        return pl.BlockSpec(array.shape, lambda r: (0,) * array.ndim)

    start = 0 if first else late_tiles // per_block
    count = (late_tiles if first else edge) // per_block
    in_specs = [
        pl.BlockSpec((devices, per_block, 8, 128), lambda r: (0, r, 0, 0)),
        pl.BlockSpec((devices, 1, 8, 128), lambda r: (0, edge, 0, 0)),
        pl.BlockSpec((block, width), lambda r: (r + start, 0)),
    ]
    operands = [conv, late, gate_input]
    if first:
        ahead = late_tiles - 1
        in_specs += [pl.BlockSpec((devices, 1, 8, 128), lambda r: (0, ahead, 0, 0)), whole(halo_gate)]
        operands += [conv, halo_gate]
    else:
        in_specs += [pl.BlockSpec((reach, width), lambda r: (late_tiles - 1, 0))]
        operands += [gate_input]
    in_specs += [whole(array) for array in fixed]
    operands += fixed
    aliases = {}
    if first:
        aliases = {len(operands): 0}
        in_specs += [pl.BlockSpec(memory_space=pl.ANY)]
        operands += [before]
    hidden = fixed[3].shape[1]
    return pl.pallas_call(
        early_kernel if first else late_kernel,
        grid=(count,),
        in_specs=in_specs,
        out_specs=pl.BlockSpec((block, width), lambda r: (r + start, 0)),
        out_shape=jax.ShapeDtypeStruct(gate_input.shape, F32),
        input_output_aliases=aliases,
        scratch_shapes=mix_scratch(block, width, hidden),
        compiler_params=pltpu.CompilerParams(vmem_limit_bytes=VMEM_LIMIT),
        cost_estimate=pl.CostEstimate(
            flops=count * block * 3 * 2 * (2 * width * hidden + 3 * width * width),
            bytes_accessed=count * block * width * 12,
            transcendentals=count * block * hidden,
        ),
        name="mix_early" if first else "mix_late",
    )(*operands)


def owned_eight(signal, kernel, skip_here, gate_input, fixed):
    groups = lax.axis_size("tm")
    devices = groups * lax.axis_size("chan")
    reach = TAPS + 1
    late_tiles = 2 * (512 // 128)

    def enter(array):
        return lax.all_to_all(array, "tm", split_axis=0, concat_axis=0, tiled=True)

    def leave(array):
        return lax.all_to_all(array, ("tm", "chan"), split_axis=0, concat_axis=0, tiled=True)

    ring = [(i, i + 1) for i in range(devices - 1)]
    halo_gate = lax.ppermute(gate_input[-reach:], ("tm", "chan"), ring)
    one, two = turn(signal, kernel, groups)
    before = filter_channels(enter(one), skip_here, None, devices, late_tiles)
    ready = (fixed[0], halo_gate)
    late, early = filter_channels(enter(two), skip_here, before, devices, late_tiles, ready)
    late = leave(late)
    early = leave(early)
    part = tail_part(late, late, gate_input, None, None, late_tiles, fixed)
    return tail_part(early, late, gate_input, halo_gate, part, late_tiles, fixed)


def on_device(
    signal, kernel, skip_gain, gate_input, tap_weight, norm_gain, up_weight, up_bias, down_weight
):
    groups = lax.axis_size("tm")
    pair = lax.axis_size("chan")
    frames_here, channels_here = signal.shape
    owned = channels_here // groups
    width = gate_input.shape[1]
    first_channel = lax.axis_index("chan") * channels_here + lax.axis_index("tm") * owned
    skip_here = lax.dynamic_slice_in_dim(skip_gain, first_channel, owned)
    fixed = fixed_operands(tap_weight, norm_gain, up_weight, up_bias, down_weight)
    window = frames_here * groups
    if owned == 8 and channels_here == 128 and pair == HEADS and window == 256 * LANES:
        if gate_input.shape[0] % 512 == 0 and gate_input.shape[0] >= 2048:
            return owned_eight(signal, kernel, skip_here, gate_input, fixed)

    def enter(array):
        shaped = array.reshape(frames_here // LANES, LANES, groups, owned).transpose(2, 3, 0, 1)
        return lax.all_to_all(shaped, "tm", split_axis=0, concat_axis=0, tiled=True)

    filtered = long_filter(enter(signal), enter(kernel), skip_here, groups * pair)
    back = lax.all_to_all(filtered, ("tm", "chan"), split_axis=0, concat_axis=0, tiled=True)
    blocks = back.reshape(groups, pair, owned, -1, LANES).transpose(3, 1, 0, 2, 4)
    blocks = blocks.reshape(-1, width, LANES)
    reach = TAPS + 1
    last = blocks[-1, :, LANES - reach :].T * gate_input[-reach:]
    devices = groups * pair
    halo = lax.ppermute(last, ("tm", "chan"), [(i, i + 1) for i in range(devices - 1)])
    return tail(blocks, gate_input, halo, fixed)


def solution(mesh):
    placed = (
        P(("grp", "tm"), "chan"),
        P("tm", "chan"),
        P(),
        P(("grp", "tm", "chan"), None),
        P(),
        P(),
        P(),
        P(),
        P(),
    )
    return jax.shard_map(
        on_device,
        mesh=mesh,
        in_specs=placed,
        out_specs=P(("grp", "tm", "chan"), None),
        check_vma=False,
    )
```

```python
import functools
import math

import jax
import jax.numpy as jnp
import numpy as np
from jax import lax
from jax.experimental import pallas as pl
from jax.experimental.pallas import tpu as pltpu
from jax.sharding import PartitionSpec as P
import ml_dtypes

LANES = 512
RADIX = 4
SUB = LANES // RADIX
TAPS = 127
HEADS = 2
EPSILON = 1e-06
BF16 = jnp.bfloat16
F32 = jnp.float32
VMEM_LIMIT = 56 * 1024 * 1024


def table_split(table, axis, order):
    high = table.astype(ml_dtypes.bfloat16)
    low = (table - high.astype(np.float64)).astype(ml_dtypes.bfloat16)
    parts = {"h": high, "l": low}
    return np.concatenate([parts[name] for name in order], axis=axis)


@functools.lru_cache(maxsize=None)
def tables(rows):
    length = rows * LANES
    turn = 2.0 * math.pi
    n1 = np.arange(rows, dtype=np.float64)
    n2 = np.arange(LANES, dtype=np.float64)
    m = np.arange(SUB, dtype=np.float64)
    first = turn * np.outer(n1 + 0.25, n1) / rows
    enter = table_split(np.concatenate([np.cos(first), -np.sin(first)], axis=0), 1, "hl")
    leave = table_split(
        np.concatenate([np.cos(first.T), -np.sin(first.T)], axis=1) / length, 1, "hl"
    )
    twiddle = turn * np.outer(n1 + 0.25, n2) / length
    forward, backward = [], []
    for r in range(RADIX):
        phase = turn * np.outer(m, m / SUB + r / LANES)
        c, s = np.cos(phase), np.sin(phase)
        forward.append(table_split(np.block([[c, -s], [s, c]]), 0, "hl"))
        c, s = c.T, s.T
        backward.append(table_split(np.block([[c, s], [-s, c]]), 0, "hl"))
    return (
        enter,
        np.cos(twiddle).astype(np.float32),
        np.sin(twiddle).astype(np.float32),
        np.stack(forward),
        np.stack(backward),
        leave,
    )


def halves(value):
    high = value.astype(BF16)
    low = (value - high.astype(F32)).astype(BF16)
    return high, low


def split_cat(value, axis):
    high, low = halves(value)
    return jnp.concatenate([high, low, high], axis=axis)


def high_high_low(table, axis):
    size = table.shape[axis] // 2
    high = lax.slice_in_dim(table, 0, size, axis=axis)
    low = lax.slice_in_dim(table, size, 2 * size, axis=axis)
    return jnp.concatenate([high, high, low], axis=axis)


def dot(left, right):
    return jnp.dot(left, right, preferred_element_type=F32)


def filter_channel(signal, kernel, skip, enter_ref, cos_ref, sin_ref, forward_ref, backward_ref,
                   leave_ref):
    rows = cos_ref.shape[0]
    enter = high_high_low(enter_ref[...], 1)
    entered = [dot(enter, split_cat(value, 0)) for value in (signal, kernel)]
    spectra = []
    for turned in entered:
        real_in, imag_in = turned[:rows], turned[rows:]
        real = real_in * cos_ref[...] + imag_in * sin_ref[...]
        imag = imag_in * cos_ref[...] - real_in * sin_ref[...]
        r0, r1, r2, r3 = (real[:, b * SUB : (b + 1) * SUB] for b in range(RADIX))
        i0, i1, i2, i3 = (imag[:, b * SUB : (b + 1) * SUB] for b in range(RADIX))
        er, ei, fr, fi = r0 + r2, i0 + i2, r0 - r2, i0 - i2
        gr, gi, hr, hi = r1 + r3, i1 + i3, r1 - r3, i1 - i3
        spread = ((er + gr, ei + gi), (fr + hi, fi - hr), (er - gr, ei - gi), (fr - hi, fi + hr))
        spectra.append([
            dot(split_cat(jnp.concatenate(pair, axis=1), 1), high_high_low(forward_ref[r], 0))
            for r, pair in enumerate(spread)
        ])
    products = []
    for s, k in zip(*spectra):
        sr, si = s[:, :SUB], s[:, SUB:]
        kr, ki = k[:, :SUB], k[:, SUB:]
        product = jnp.concatenate([sr * kr - si * ki, sr * ki + si * kr], axis=1)
        products.append(split_cat(product, 1))
    back = []
    for r in range(RADIX):
        turned = dot(products[r], high_high_low(backward_ref[r], 0))
        back.append((turned[:, :SUB], turned[:, SUB:]))
    (r0, i0), (r1, i1), (r2, i2), (r3, i3) = back
    er, ei, fr, fi = r0 + r2, i0 + i2, r0 - r2, i0 - i2
    gr, gi, hr, hi = r1 + r3, i1 + i3, r1 - r3, i1 - i3
    real = jnp.concatenate([er + gr, fr - hi, er - gr, fr + hi], axis=1)
    imag = jnp.concatenate([ei + gi, fi + hr, ei - gi, fi - hr], axis=1)
    turned = jnp.concatenate(
        [real * cos_ref[...] - imag * sin_ref[...], imag * cos_ref[...] + real * sin_ref[...]],
        axis=0,
    )
    return dot(high_high_low(leave_ref[...], 1), split_cat(turned, 0)) + skip * signal


def filter_kernel(
    skip_ref, signal_ref, kernel_ref, enter_ref, cos_ref, sin_ref, forward_ref, backward_ref,
    leave_ref, out_ref,
):
    rows = cos_ref.shape[0]
    result = filter_channel(
        signal_ref[...].reshape(rows, LANES), kernel_ref[...].reshape(rows, LANES),
        skip_ref[pl.program_id(0)], enter_ref, cos_ref, sin_ref, forward_ref, backward_ref,
        leave_ref,
    )
    out_ref[...] = result.reshape(out_ref.shape)


def long_filter(signal, kernel, skip, out_groups):
    groups, channels, group_rows, _ = signal.shape
    rows = groups * group_rows
    straight = group_rows % 8 == 0 and (rows // out_groups) % 8 == 0
    in_block = (groups, 1, group_rows, LANES)
    out_shape = (out_groups, channels, rows // out_groups, LANES)
    if not straight:
        signal = signal.transpose(1, 0, 2, 3).reshape(1, channels, rows, LANES)
        kernel = kernel.transpose(1, 0, 2, 3).reshape(1, channels, rows, LANES)
        in_block = (1, 1, rows, LANES)
        out_shape = (1, channels, rows, LANES)
    out_block = (out_shape[0], 1) + out_shape[2:]

    def along(c):
        return (0, c, 0, 0)

    def whole(array):
        return pl.BlockSpec(array.shape, lambda c: (0,) * array.ndim)

    held = tables(rows)
    result = pl.pallas_call(
        filter_kernel,
        grid=(channels,),
        in_specs=[
            pl.BlockSpec(memory_space=pltpu.SMEM),
            pl.BlockSpec(in_block, along),
            pl.BlockSpec(in_block, along),
        ]
        + [whole(table) for table in held],
        out_specs=pl.BlockSpec(out_block, along),
        out_shape=jax.ShapeDtypeStruct(out_shape, F32),
        compiler_params=pltpu.CompilerParams(vmem_limit_bytes=VMEM_LIMIT),
        cost_estimate=pl.CostEstimate(
            flops=channels * rows * LANES * 2048 * 3 * 3,
            bytes_accessed=channels * rows * LANES * 12,
            transcendentals=0,
        ),
        name="long_filter",
    )(skip, signal, kernel, *held)
    if not straight:
        result = result.reshape(channels, out_groups, rows // out_groups, LANES)
        result = result.transpose(1, 0, 2, 3)
    return result


def split_weights(tap_ref, up_ref, down_ref, taps_ref, ups_ref, downs_ref):
    def stacked(weight):
        high, low = halves(weight)
        return jnp.concatenate([high, high, low], axis=0)

    taps_ref[...] = stacked(tap_ref[...])
    chunks, _, chunk = ups_ref.shape
    for n in range(chunks):
        span = slice(n * chunk, (n + 1) * chunk)
        ups_ref[n] = stacked(up_ref[:, span])
        downs_ref[n] = stacked(down_ref[span, :])


def mix_block(window_ref, gain_ref, bias_ref, out_ref, high_ref, low_ref, mix_ref, taps_ref, ups_ref,
              downs_ref):
    block, width = out_ref.shape
    reach = TAPS + 1
    head_width = width // HEADS
    high, low = halves(window_ref[...])
    high_ref[...] = high
    low_ref[...] = low
    taps = dot(
        jnp.concatenate([high[reach:], low[reach:], high[reach:]], axis=1), taps_ref[...]
    )
    for b in range(block // reach):
        for h in range(HEADS):
            own = taps[b * reach : (b + 1) * reach, h * reach : (h + 1) * reach]
            band = jnp.concatenate([own, jnp.zeros_like(own)], axis=1)
            band = pltpu.roll(band, 1, 1, stride=1, stride_axis=0)
            near_rows = slice(b * reach, (b + 2) * reach)
            columns = slice(h * head_width, (h + 1) * head_width)
            near_high = high_ref[near_rows, columns]
            near_low = low_ref[near_rows, columns]
            mix_ref[b * reach : (b + 1) * reach, columns] = dot(
                split_cat(band, 1), jnp.concatenate([near_high, near_high, near_low], axis=0)
            )
    mixed = mix_ref[...]
    mean_square = jnp.mean(mixed * mixed, axis=1, keepdims=True)
    normed = split_cat(mixed * lax.rsqrt(mean_square + EPSILON) * gain_ref[...], 1)
    total = mixed
    chunks, _, chunk = ups_ref.shape
    scale = math.sqrt(2.0 / math.pi)
    for n in range(chunks):
        raised = dot(normed, ups_ref[n]) + bias_ref[:, n * chunk : (n + 1) * chunk]
        inner = raised * (scale + (scale * 0.044715) * (raised * raised))
        half = 0.5 * raised
        total = total + dot(split_cat(half + half * jnp.tanh(inner), 1), downs_ref[n])
    out_ref[...] = total


def mix_scratch(block, width, hidden):
    reach = TAPS + 1
    chunk = 256 if hidden % 256 == 0 else hidden
    return [
        pltpu.VMEM((block + reach, width), F32),
        pltpu.VMEM((block + reach, width), BF16),
        pltpu.VMEM((block + reach, width), BF16),
        pltpu.VMEM((block, width), F32),
        pltpu.VMEM((3 * width, HEADS * reach), BF16),
        pltpu.VMEM((hidden // chunk, 3 * width, chunk), BF16),
        pltpu.VMEM((hidden // chunk, 3 * chunk, width), BF16),
    ]


def mix_window(window_ref, fixed, scratch, out_ref):
    tap_ref, gain_ref, up_ref, bias_ref, down_ref = fixed
    weights = scratch[3:]

    @pl.when(pl.program_id(0) == 0)
    def _():
        split_weights(tap_ref, up_ref, down_ref, *weights)

    mix_block(window_ref, gain_ref, bias_ref, out_ref, *scratch)


def mix_kernel(conv_ref, gate_ref, halo_ref, *rest):
    fixed, out_ref, window_ref, scratch = rest[:5], rest[5], rest[6], rest[7:]
    block = gate_ref.shape[0]
    reach = TAPS + 1

    @pl.when(pl.program_id(0) == 0)
    def _():
        window_ref[:reach, :] = halo_ref[...]

    @pl.when(pl.program_id(0) > 0)
    def _():
        window_ref[:reach, :] = window_ref[block : block + reach, :]

    window_ref[reach:, :] = jnp.transpose(conv_ref[0], (1, 0)) * gate_ref[...]
    mix_window(window_ref, fixed, scratch, out_ref)


def fixed_operands(tap_weight, norm_gain, up_weight, up_bias, down_weight):
    width = tap_weight.shape[0]
    taps = tap_weight.reshape(width, HEADS, TAPS)[:, :, ::-1]
    taps = jnp.pad(taps, ((0, 0), (0, 0), (1, 0))).reshape(width, HEADS * (TAPS + 1))
    return (
        taps,
        norm_gain.reshape(1, -1),
        up_weight,
        up_bias.reshape(1, -1),
        down_weight,
    )


def tail(conv_blocks, gate_input, halo, fixed):
    count, width, block = conv_blocks.shape
    reach = TAPS + 1
    hidden = fixed[3].shape[1]

    def whole(array):
        return pl.BlockSpec(array.shape, lambda r: (0,) * array.ndim)

    return pl.pallas_call(
        mix_kernel,
        grid=(count,),
        in_specs=[
            pl.BlockSpec((1, width, block), lambda r: (r, 0, 0)),
            pl.BlockSpec((block, width), lambda r: (r, 0)),
            whole(halo),
        ]
        + [whole(array) for array in fixed],
        out_specs=pl.BlockSpec((block, width), lambda r: (r, 0)),
        out_shape=jax.ShapeDtypeStruct(gate_input.shape, F32),
        scratch_shapes=mix_scratch(block, width, hidden),
        compiler_params=pltpu.CompilerParams(vmem_limit_bytes=VMEM_LIMIT),
        cost_estimate=pl.CostEstimate(
            flops=count * block * 3 * 2 * (2 * width * hidden + 3 * width * width),
            bytes_accessed=count * block * width * 12,
            transcendentals=count * block * hidden,
        ),
        name="mix_and_mlp",
    )(conv_blocks, gate_input, halo, *fixed)


FIRST_CHANNELS = 6
TURN_ROWS = 8


def turn_kernel(signal_ref, kernel_ref, first_ref, second_ref, held_ref, sems):
    groups, early = first_ref.shape[:2]
    rows = signal_ref.shape[0] // LANES
    step, steps = pl.program_id(0), pl.num_programs(0)
    slot = step % 2

    def copies(at, slot):
        shaped = held_ref.at[slot].reshape(groups, 8, rows + 1, 8, 128)
        there = pl.ds(at * rows, rows)
        return (
            pltpu.make_async_copy(
                shaped.at[:, :early, :rows], first_ref.at[:, :, there], sems.at[slot, 0]
            ),
            pltpu.make_async_copy(
                shaped.at[:, early:, :rows], second_ref.at[:, :, there], sems.at[slot, 1]
            ),
        )

    @pl.when(step >= 2)
    def _():
        for copy in copies(step - 2, slot):
            copy.wait()

    for row in range(rows):
        for j in range(LANES // 128):
            span = slice(row * LANES + j * 128, row * LANES + (j + 1) * 128)
            for which, ref in enumerate((signal_ref, kernel_ref)):
                turned = jnp.transpose(ref[span, :], (1, 0))
                place = row * 8 + j * 2 + which
                held_ref[slot, pl.ds(place, turned.shape[0], stride=(rows + 1) * 8), :] = turned
    for copy in copies(step, slot):
        copy.start()

    @pl.when(step == steps - 1)
    def _():
        for copy in copies(step, slot):
            copy.wait()

    @pl.when((step == steps - 1) & (step >= 1))
    def _():
        for copy in copies(step - 1, 1 - slot):
            copy.wait()


def turn(signal, kernel, groups):
    frames, width = signal.shape
    chunk = TURN_ROWS * LANES
    rows = frames // LANES
    block = pl.BlockSpec((chunk, width), lambda i: (i, 0))
    counts = (FIRST_CHANNELS, 8 - FIRST_CHANNELS)
    return pl.pallas_call(
        turn_kernel,
        grid=(frames // chunk,),
        in_specs=[block, block],
        out_specs=[pl.BlockSpec(memory_space=pl.ANY)] * 2,
        out_shape=[jax.ShapeDtypeStruct((groups, n, rows, 8, 128), F32) for n in counts],
        scratch_shapes=[
            pltpu.VMEM((2, width * (TURN_ROWS + 1) * 8, 128), F32),
            pltpu.SemaphoreType.DMA((2, 2)),
        ],
        compiler_params=pltpu.CompilerParams(vmem_limit_bytes=VMEM_LIMIT),
        name="turn",
    )(signal, kernel)


def gather_channel(ref, which):
    groups, _, depth, _ = ref.shape
    tiles = LANES // 128
    flat = ref.reshape(groups * depth, 128)
    rows = groups * depth // 8
    return jnp.concatenate(
        [flat[pl.ds(2 * j + which, rows, stride=8), :] for j in range(tiles)], axis=1
    )


def scatter_channel(ref, slot, value):
    tiles = LANES // 128
    for j in range(tiles):
        ref[pl.ds(8 * j + slot, value.shape[0], stride=8 * tiles), :] = (
            value[:, j * 128 : (j + 1) * 128]
        )


def first_channels_kernel(skip_ref, data_ref, *rest):
    *table_refs, out_ref = rest
    c = pl.program_id(0)
    result = filter_channel(
        gather_channel(data_ref, 0), gather_channel(data_ref, 1), skip_ref[c],
        *table_refs,
    )
    scatter_channel(out_ref, c, result)


def last_channels_kernel(late, extra, skip_ref, data_ref, *rest):
    *table_refs, before_ref = rest[: len(rest) - 4 - extra]
    late_ref, early_ref, held_ref, sems = rest[-4:]
    c = pl.program_id(0)
    channel = c + FIRST_CHANNELS
    devices, tiles = late_ref.shape[0], late_ref.shape[1] + early_ref.shape[1] - 1
    load = pltpu.make_async_copy(before_ref, held_ref, sems.at[0])

    @pl.when(c == 0)
    def _():
        load.start()

    result = filter_channel(
        gather_channel(data_ref, 0), gather_channel(data_ref, 1),
        skip_ref[channel], *table_refs,
    )

    @pl.when(c == 0)
    def _():
        load.wait()

    scatter_channel(held_ref, channel, result)

    @pl.when(c == pl.num_programs(0) - 1)
    def _():
        shaped = held_ref.reshape(devices, tiles, 8, 128)
        final = shaped.at[:, tiles - 1 : tiles]
        pairs = (
            (shaped.at[:, late:tiles], late_ref.at[:, 0 : tiles - late]),
            (shaped.at[:, late - 1 : late], late_ref.at[:, tiles - late : tiles - late + 1]),
            (shaped.at[:, 0 : late - 1], early_ref.at[:, 0 : late - 1]),
            (final.at[0 : devices - 1], early_ref.at[1:devices, late - 1 : late]),
            (final.at[devices - 1 : devices], early_ref.at[0:1, late - 1 : late]),
        )
        copies = [
            pltpu.make_async_copy(here, there, sems.at[1 + i])
            for i, (here, there) in enumerate(pairs)
        ]
        for copy in copies:
            copy.start()
        for copy in copies:
            copy.wait()


def filter_channels(data, skip, before, devices, late, ready=()):
    groups, channels, group_rows, _, _ = data.shape
    flat = data.reshape(groups, channels, group_rows * 8, 128)
    rows = groups * group_rows
    lane_tiles = LANES // 128
    tiles = rows * lane_tiles // devices
    held = tables(rows)
    held_shape = (rows * lane_tiles * 8, 128)

    def whole(array):
        return pl.BlockSpec(array.shape, lambda c: (0,) * array.ndim)

    in_specs = [
        pl.BlockSpec(memory_space=pltpu.SMEM),
        pl.BlockSpec(
            (groups, 1, group_rows * 8, 128), lambda c: (0, c, 0, 0)
        ),
    ] + [whole(t) for t in held]
    options = dict(
        grid=(channels,),
        compiler_params=pltpu.CompilerParams(vmem_limit_bytes=VMEM_LIMIT),
        cost_estimate=pl.CostEstimate(
            flops=channels * rows * LANES * 2048 * 3 * 3,
            bytes_accessed=channels * rows * LANES * 12,
            transcendentals=0,
        ),
    )
    if before is None:
        return pl.pallas_call(
            first_channels_kernel,
            in_specs=in_specs,
            out_specs=pl.BlockSpec(held_shape, lambda c: (0, 0)),
            out_shape=jax.ShapeDtypeStruct(held_shape, F32),
            name="filter_first",
            **options,
        )(skip, flat, *held)
    anywhere = pl.BlockSpec(memory_space=pl.ANY)
    return pl.pallas_call(
        functools.partial(last_channels_kernel, late, len(ready)),
        in_specs=in_specs + [anywhere] * (1 + len(ready)),
        out_specs=[anywhere, anywhere],
        out_shape=[
            jax.ShapeDtypeStruct((devices, tiles - late + 1, 8, 128), F32),
            jax.ShapeDtypeStruct((devices, late, 8, 128), F32),
        ],
        scratch_shapes=[pltpu.VMEM(held_shape, F32), pltpu.SemaphoreType.DMA((6,))],
        name="filter_last",
        **options,
    )(skip, flat, *held, before, *ready)


def frames_by_channels(tile):
    paired = tile.reshape(tile.shape[0] // HEADS, HEADS, 8, 128)
    return jnp.concatenate(
        [jnp.transpose(paired[:, h].reshape(-1, 128), (1, 0)) for h in range(HEADS)], axis=1
    )


def late_kernel(conv_ref, edge_ref, gate_ref, edge_gate_ref, *rest):
    fixed, out_ref, window_ref, scratch = rest[:5], rest[5], rest[6], rest[7:]
    block = gate_ref.shape[0]
    reach = TAPS + 1

    @pl.when(pl.program_id(0) == 0)
    def _():
        window_ref[:reach, :] = frames_by_channels(edge_ref[:, 0]) * edge_gate_ref[...]

    @pl.when(pl.program_id(0) > 0)
    def _():
        window_ref[:reach, :] = window_ref[block : block + reach, :]

    for j in range(block // reach):
        span = slice(j * reach, (j + 1) * reach)
        window_ref[reach + j * reach : 2 * reach + j * reach, :] = (
            frames_by_channels(conv_ref[:, j]) * gate_ref[span, :]
        )
    mix_window(window_ref, fixed, scratch, out_ref)


def early_kernel(conv_ref, edge_ref, gate_ref, halo_ref, halo_gate_ref, *rest):
    fixed, out_ref, window_ref, scratch = rest[:5], rest[6], rest[7], rest[8:]
    block = gate_ref.shape[0]
    reach = TAPS + 1
    last = pl.program_id(0) == pl.num_programs(0) - 1

    @pl.when(pl.program_id(0) == 0)
    def _():
        window_ref[:reach, :] = frames_by_channels(halo_ref[:, 0]) * halo_gate_ref[...]

    @pl.when(pl.program_id(0) > 0)
    def _():
        window_ref[:reach, :] = window_ref[block : block + reach, :]

    count = block // reach
    for j in range(count):
        tile = conv_ref[:, j]
        if j == count - 1:
            tile = jnp.where(last, edge_ref[:, 0], tile)
        span = slice(j * reach, (j + 1) * reach)
        window_ref[reach + j * reach : 2 * reach + j * reach, :] = (
            frames_by_channels(tile) * gate_ref[span, :]
        )
    mix_window(window_ref, fixed, scratch, out_ref)


def tail_part(conv, late, gate_input, halo_gate, before, late_tiles, fixed):
    devices = conv.shape[0]
    frames, width = gate_input.shape
    reach = TAPS + 1
    block = 512
    per_block = block // 128
    edge = late.shape[1] - 1
    first = before is not None

    def whole(array):
        return pl.BlockSpec(array.shape, lambda r: (0,) * array.ndim)

    start = 0 if first else late_tiles // per_block
    count = (late_tiles if first else edge) // per_block
    in_specs = [
        pl.BlockSpec((devices, per_block, 8, 128), lambda r: (0, r, 0, 0)),
        pl.BlockSpec((devices, 1, 8, 128), lambda r: (0, edge, 0, 0)),
        pl.BlockSpec((block, width), lambda r: (r + start, 0)),
    ]
    operands = [conv, late, gate_input]
    if first:
        ahead = late_tiles - 1
        in_specs += [pl.BlockSpec((devices, 1, 8, 128), lambda r: (0, ahead, 0, 0)), whole(halo_gate)]
        operands += [conv, halo_gate]
    else:
        in_specs += [pl.BlockSpec((reach, width), lambda r: (late_tiles - 1, 0))]
        operands += [gate_input]
    in_specs += [whole(array) for array in fixed]
    operands += fixed
    aliases = {}
    if first:
        aliases = {len(operands): 0}
        in_specs += [pl.BlockSpec(memory_space=pl.ANY)]
        operands += [before]
    hidden = fixed[3].shape[1]
    return pl.pallas_call(
        early_kernel if first else late_kernel,
        grid=(count,),
        in_specs=in_specs,
        out_specs=pl.BlockSpec((block, width), lambda r: (r + start, 0)),
        out_shape=jax.ShapeDtypeStruct(gate_input.shape, F32),
        input_output_aliases=aliases,
        scratch_shapes=mix_scratch(block, width, hidden),
        compiler_params=pltpu.CompilerParams(vmem_limit_bytes=VMEM_LIMIT),
        cost_estimate=pl.CostEstimate(
            flops=count * block * 3 * 2 * (2 * width * hidden + 3 * width * width),
            bytes_accessed=count * block * width * 12,
            transcendentals=count * block * hidden,
        ),
        name="mix_early" if first else "mix_late",
    )(*operands)


def owned_eight(signal, kernel, skip_here, gate_input, fixed):
    groups = lax.axis_size("tm")
    devices = groups * lax.axis_size("chan")
    reach = TAPS + 1
    late_tiles = 2 * (512 // 128)

    def enter(array):
        return lax.all_to_all(array, "tm", split_axis=0, concat_axis=0, tiled=True)

    def leave(array):
        return lax.all_to_all(array, ("tm", "chan"), split_axis=0, concat_axis=0, tiled=True)

    ring = [(i, i + 1) for i in range(devices - 1)]
    halo_gate = lax.ppermute(gate_input[-reach:], ("tm", "chan"), ring)
    one, two = turn(signal, kernel, groups)
    before = filter_channels(enter(one), skip_here, None, devices, late_tiles)
    ready = (fixed[0], halo_gate)
    late, early = filter_channels(enter(two), skip_here, before, devices, late_tiles, ready)
    late = leave(late)
    early = leave(early)
    part = tail_part(late, late, gate_input, None, None, late_tiles, fixed)
    return tail_part(early, late, gate_input, halo_gate, part, late_tiles, fixed)


def on_device(
    signal, kernel, skip_gain, gate_input, tap_weight, norm_gain, up_weight, up_bias, down_weight
):
    groups = lax.axis_size("tm")
    pair = lax.axis_size("chan")
    frames_here, channels_here = signal.shape
    owned = channels_here // groups
    width = gate_input.shape[1]
    first_channel = lax.axis_index("chan") * channels_here + lax.axis_index("tm") * owned
    skip_here = lax.dynamic_slice_in_dim(skip_gain, first_channel, owned)
    fixed = fixed_operands(tap_weight, norm_gain, up_weight, up_bias, down_weight)
    window = frames_here * groups
    if owned == 8 and channels_here == 128 and pair == HEADS and window == 256 * LANES:
        if gate_input.shape[0] % 512 == 0 and gate_input.shape[0] >= 2048:
            return owned_eight(signal, kernel, skip_here, gate_input, fixed)

    def enter(array):
        shaped = array.reshape(frames_here // LANES, LANES, groups, owned).transpose(2, 3, 0, 1)
        return lax.all_to_all(shaped, "tm", split_axis=0, concat_axis=0, tiled=True)

    filtered = long_filter(enter(signal), enter(kernel), skip_here, groups * pair)
    back = lax.all_to_all(filtered, ("tm", "chan"), split_axis=0, concat_axis=0, tiled=True)
    blocks = back.reshape(groups, pair, owned, -1, LANES).transpose(3, 1, 0, 2, 4)
    blocks = blocks.reshape(-1, width, LANES)
    reach = TAPS + 1
    last = blocks[-1, :, LANES - reach :].T * gate_input[-reach:]
    devices = groups * pair
    halo = lax.ppermute(last, ("tm", "chan"), [(i, i + 1) for i in range(devices - 1)])
    return tail(blocks, gate_input, halo, fixed)


def solution(mesh):
    placed = (
        P(("grp", "tm"), "chan"),
        P("tm", "chan"),
        P(),
        P(("grp", "tm", "chan"), None),
        P(),
        P(),
        P(),
        P(),
        P(),
    )
    return jax.shard_map(
        on_device,
        mesh=mesh,
        in_specs=placed,
        out_specs=P(("grp", "tm", "chan"), None),
        check_vma=False,
    )
```

```python
import functools
import math

import jax
import jax.numpy as jnp
import numpy as np
from jax import lax
from jax.experimental import pallas as pl
from jax.experimental.pallas import tpu as pltpu
from jax.sharding import PartitionSpec as P
import ml_dtypes

LANES = 512
RADIX = 4
SUB = LANES // RADIX
TAPS = 127
HEADS = 2
EPSILON = 1e-06
BF16 = jnp.bfloat16
F32 = jnp.float32
VMEM_LIMIT = 63 * 1024 * 1024


def table_split(table, axis, order):
    high = table.astype(ml_dtypes.bfloat16)
    low = (table - high.astype(np.float64)).astype(ml_dtypes.bfloat16)
    parts = {"h": high, "l": low}
    return np.concatenate([parts[name] for name in order], axis=axis)


@functools.lru_cache(maxsize=None)
def tables(rows):
    length = rows * LANES
    turn = 2.0 * math.pi
    n1 = np.arange(rows, dtype=np.float64)
    n2 = np.arange(LANES, dtype=np.float64)
    m = np.arange(SUB, dtype=np.float64)
    first = turn * np.outer(n1 + 0.25, n1) / rows
    enter = table_split(np.concatenate([np.cos(first), -np.sin(first)], axis=0), 1, "hl")
    leave = table_split(
        np.concatenate([np.cos(first.T), -np.sin(first.T)], axis=1) / length, 1, "hl"
    )
    twiddle = turn * np.outer(n1 + 0.25, n2) / length
    forward, backward = [], []
    for r in range(RADIX):
        phase = turn * np.outer(m, m / SUB + r / LANES)
        c, s = np.cos(phase), np.sin(phase)
        forward.append(table_split(np.block([[c, -s], [s, c]]), 0, "hl"))
        c, s = c.T, s.T
        backward.append(table_split(np.block([[c, s], [-s, c]]), 0, "hl"))
    return (
        enter,
        np.cos(twiddle).astype(np.float32),
        np.sin(twiddle).astype(np.float32),
        np.stack(forward),
        np.stack(backward),
        leave,
    )


def halves(value):
    high = value.astype(BF16)
    low = (value - high.astype(F32)).astype(BF16)
    return high, low


def split_cat(value, axis):
    high, low = halves(value)
    return jnp.concatenate([high, low, high], axis=axis)


def high_high_low(table, axis):
    size = table.shape[axis] // 2
    high = lax.slice_in_dim(table, 0, size, axis=axis)
    low = lax.slice_in_dim(table, size, 2 * size, axis=axis)
    return jnp.concatenate([high, high, low], axis=axis)


def dot(left, right):
    return jnp.dot(left, right, preferred_element_type=F32)


def filter_channel(signal, kernel, skip, enter_ref, cos_ref, sin_ref, forward_ref, backward_ref,
                   leave_ref):
    rows = cos_ref.shape[0]
    enter = high_high_low(enter_ref[...], 1)
    entered = [dot(enter, split_cat(value, 0)) for value in (signal, kernel)]
    spectra = []
    for turned in entered:
        real_in, imag_in = turned[:rows], turned[rows:]
        real = real_in * cos_ref[...] + imag_in * sin_ref[...]
        imag = imag_in * cos_ref[...] - real_in * sin_ref[...]
        r0, r1, r2, r3 = (real[:, b * SUB : (b + 1) * SUB] for b in range(RADIX))
        i0, i1, i2, i3 = (imag[:, b * SUB : (b + 1) * SUB] for b in range(RADIX))
        er, ei, fr, fi = r0 + r2, i0 + i2, r0 - r2, i0 - i2
        gr, gi, hr, hi = r1 + r3, i1 + i3, r1 - r3, i1 - i3
        spread = ((er + gr, ei + gi), (fr + hi, fi - hr), (er - gr, ei - gi), (fr - hi, fi + hr))
        spectra.append([
            dot(split_cat(jnp.concatenate(pair, axis=1), 1), high_high_low(forward_ref[r], 0))
            for r, pair in enumerate(spread)
        ])
    products = []
    for s, k in zip(*spectra):
        sr, si = s[:, :SUB], s[:, SUB:]
        kr, ki = k[:, :SUB], k[:, SUB:]
        product = jnp.concatenate([sr * kr - si * ki, sr * ki + si * kr], axis=1)
        products.append(split_cat(product, 1))
    back = []
    for r in range(RADIX):
        turned = dot(products[r], high_high_low(backward_ref[r], 0))
        back.append((turned[:, :SUB], turned[:, SUB:]))
    (r0, i0), (r1, i1), (r2, i2), (r3, i3) = back
    er, ei, fr, fi = r0 + r2, i0 + i2, r0 - r2, i0 - i2
    gr, gi, hr, hi = r1 + r3, i1 + i3, r1 - r3, i1 - i3
    real = jnp.concatenate([er + gr, fr - hi, er - gr, fr + hi], axis=1)
    imag = jnp.concatenate([ei + gi, fi + hr, ei - gi, fi - hr], axis=1)
    turned = jnp.concatenate(
        [real * cos_ref[...] - imag * sin_ref[...], imag * cos_ref[...] + real * sin_ref[...]],
        axis=0,
    )
    return dot(high_high_low(leave_ref[...], 1), split_cat(turned, 0)) + skip * signal


def filter_kernel(
    skip_ref, signal_ref, kernel_ref, enter_ref, cos_ref, sin_ref, forward_ref, backward_ref,
    leave_ref, out_ref,
):
    rows = cos_ref.shape[0]
    result = filter_channel(
        signal_ref[...].reshape(rows, LANES), kernel_ref[...].reshape(rows, LANES),
        skip_ref[pl.program_id(0)], enter_ref, cos_ref, sin_ref, forward_ref, backward_ref,
        leave_ref,
    )
    out_ref[...] = result.reshape(out_ref.shape)


def long_filter(signal, kernel, skip, out_groups):
    groups, channels, group_rows, _ = signal.shape
    rows = groups * group_rows
    straight = group_rows % 8 == 0 and (rows // out_groups) % 8 == 0
    in_block = (groups, 1, group_rows, LANES)
    out_shape = (out_groups, channels, rows // out_groups, LANES)
    if not straight:
        signal = signal.transpose(1, 0, 2, 3).reshape(1, channels, rows, LANES)
        kernel = kernel.transpose(1, 0, 2, 3).reshape(1, channels, rows, LANES)
        in_block = (1, 1, rows, LANES)
        out_shape = (1, channels, rows, LANES)
    out_block = (out_shape[0], 1) + out_shape[2:]

    def along(c):
        return (0, c, 0, 0)

    def whole(array):
        return pl.BlockSpec(array.shape, lambda c: (0,) * array.ndim)

    held = tables(rows)
    result = pl.pallas_call(
        filter_kernel,
        grid=(channels,),
        in_specs=[
            pl.BlockSpec(memory_space=pltpu.SMEM),
            pl.BlockSpec(in_block, along),
            pl.BlockSpec(in_block, along),
        ]
        + [whole(table) for table in held],
        out_specs=pl.BlockSpec(out_block, along),
        out_shape=jax.ShapeDtypeStruct(out_shape, F32),
        compiler_params=pltpu.CompilerParams(vmem_limit_bytes=VMEM_LIMIT),
        cost_estimate=pl.CostEstimate(
            flops=channels * rows * LANES * 2048 * 3 * 3,
            bytes_accessed=channels * rows * LANES * 12,
            transcendentals=0,
        ),
        name="long_filter",
    )(skip, signal, kernel, *held)
    if not straight:
        result = result.reshape(channels, out_groups, rows // out_groups, LANES)
        result = result.transpose(1, 0, 2, 3)
    return result


def split_weights(tap_ref, up_ref, down_ref, taps_ref, ups_ref, downs_ref):
    def stacked(weight):
        high, low = halves(weight)
        return jnp.concatenate([high, high, low], axis=0)

    taps_ref[...] = stacked(tap_ref[...])
    chunks, _, chunk = ups_ref.shape
    for n in range(chunks):
        span = slice(n * chunk, (n + 1) * chunk)
        ups_ref[n] = stacked(up_ref[:, span])
        downs_ref[n] = stacked(down_ref[span, :])


def mix_block(window_ref, gain_ref, bias_ref, out_ref, high_ref, low_ref, mix_ref, taps_ref, ups_ref,
              downs_ref):
    block, width = out_ref.shape
    reach = TAPS + 1
    head_width = width // HEADS
    high, low = halves(window_ref[...])
    high_ref[...] = high
    low_ref[...] = low
    taps = dot(
        jnp.concatenate([high[reach:], low[reach:], high[reach:]], axis=1), taps_ref[...]
    )
    for b in range(block // reach):
        for h in range(HEADS):
            own = taps[b * reach : (b + 1) * reach, h * reach : (h + 1) * reach]
            band = jnp.concatenate([own, jnp.zeros_like(own)], axis=1)
            band = pltpu.roll(band, 1, 1, stride=1, stride_axis=0)
            near_rows = slice(b * reach, (b + 2) * reach)
            columns = slice(h * head_width, (h + 1) * head_width)
            near_high = high_ref[near_rows, columns]
            near_low = low_ref[near_rows, columns]
            mix_ref[b * reach : (b + 1) * reach, columns] = dot(
                split_cat(band, 1), jnp.concatenate([near_high, near_high, near_low], axis=0)
            )
    mixed = mix_ref[...]
    mean_square = jnp.mean(mixed * mixed, axis=1, keepdims=True)
    normed = split_cat(mixed * lax.rsqrt(mean_square + EPSILON) * gain_ref[...], 1)
    total = mixed
    chunks, _, chunk = ups_ref.shape
    scale = math.sqrt(2.0 / math.pi)
    for n in range(chunks):
        raised = dot(normed, ups_ref[n]) + bias_ref[:, n * chunk : (n + 1) * chunk]
        inner = raised * (scale + (scale * 0.044715) * (raised * raised))
        half = 0.5 * raised
        total = total + dot(split_cat(half + half * jnp.tanh(inner), 1), downs_ref[n])
    out_ref[...] = total


def mix_scratch(block, width, hidden):
    reach = TAPS + 1
    chunk = 256 if hidden % 256 == 0 else hidden
    return [
        pltpu.VMEM((block + reach, width), F32),
        pltpu.VMEM((block + reach, width), BF16),
        pltpu.VMEM((block + reach, width), BF16),
        pltpu.VMEM((block, width), F32),
        pltpu.VMEM((3 * width, HEADS * reach), BF16),
        pltpu.VMEM((hidden // chunk, 3 * width, chunk), BF16),
        pltpu.VMEM((hidden // chunk, 3 * chunk, width), BF16),
    ]


def mix_window(window_ref, fixed, scratch, out_ref):
    tap_ref, gain_ref, up_ref, bias_ref, down_ref = fixed
    weights = scratch[3:]

    @pl.when(pl.program_id(0) == 0)
    def _():
        split_weights(tap_ref, up_ref, down_ref, *weights)

    mix_block(window_ref, gain_ref, bias_ref, out_ref, *scratch)


def mix_kernel(conv_ref, gate_ref, halo_ref, *rest):
    fixed, out_ref, window_ref, scratch = rest[:5], rest[5], rest[6], rest[7:]
    block = gate_ref.shape[0]
    reach = TAPS + 1

    @pl.when(pl.program_id(0) == 0)
    def _():
        window_ref[:reach, :] = halo_ref[...]

    @pl.when(pl.program_id(0) > 0)
    def _():
        window_ref[:reach, :] = window_ref[block : block + reach, :]

    window_ref[reach:, :] = jnp.transpose(conv_ref[0], (1, 0)) * gate_ref[...]
    mix_window(window_ref, fixed, scratch, out_ref)


def fixed_operands(tap_weight, norm_gain, up_weight, up_bias, down_weight):
    width = tap_weight.shape[0]
    taps = tap_weight.reshape(width, HEADS, TAPS)[:, :, ::-1]
    taps = jnp.pad(taps, ((0, 0), (0, 0), (1, 0))).reshape(width, HEADS * (TAPS + 1))
    return (
        taps,
        norm_gain.reshape(1, -1),
        up_weight,
        up_bias.reshape(1, -1),
        down_weight,
    )


def tail(conv_blocks, gate_input, halo, fixed):
    count, width, block = conv_blocks.shape
    reach = TAPS + 1
    hidden = fixed[3].shape[1]

    def whole(array):
        return pl.BlockSpec(array.shape, lambda r: (0,) * array.ndim)

    return pl.pallas_call(
        mix_kernel,
        grid=(count,),
        in_specs=[
            pl.BlockSpec((1, width, block), lambda r: (r, 0, 0)),
            pl.BlockSpec((block, width), lambda r: (r, 0)),
            whole(halo),
        ]
        + [whole(array) for array in fixed],
        out_specs=pl.BlockSpec((block, width), lambda r: (r, 0)),
        out_shape=jax.ShapeDtypeStruct(gate_input.shape, F32),
        scratch_shapes=mix_scratch(block, width, hidden),
        compiler_params=pltpu.CompilerParams(vmem_limit_bytes=VMEM_LIMIT),
        cost_estimate=pl.CostEstimate(
            flops=count * block * 3 * 2 * (2 * width * hidden + 3 * width * width),
            bytes_accessed=count * block * width * 12,
            transcendentals=count * block * hidden,
        ),
        name="mix_and_mlp",
    )(conv_blocks, gate_input, halo, *fixed)


FIRST_CHANNELS = 6
TURN_ROWS = 8


def turn_kernel(signal_ref, kernel_ref, first_ref, second_ref, held_ref, sems):
    groups, early = first_ref.shape[:2]
    rows = signal_ref.shape[0] // LANES
    step, steps = pl.program_id(0), pl.num_programs(0)
    slot = step % 2

    def copies(at, slot):
        shaped = held_ref.at[slot].reshape(groups, 8, rows + 1, 8, 128)
        there = pl.ds(at * rows, rows)
        return (
            pltpu.make_async_copy(
                shaped.at[:, :early, :rows], first_ref.at[:, :, there], sems.at[slot, 0]
            ),
            pltpu.make_async_copy(
                shaped.at[:, early:, :rows], second_ref.at[:, :, there], sems.at[slot, 1]
            ),
        )

    @pl.when(step >= 2)
    def _():
        for copy in copies(step - 2, slot):
            copy.wait()

    for row in range(rows):
        for j in range(LANES // 128):
            span = slice(row * LANES + j * 128, row * LANES + (j + 1) * 128)
            for which, ref in enumerate((signal_ref, kernel_ref)):
                turned = jnp.transpose(ref[span, :], (1, 0))
                place = row * 8 + j * 2 + which
                held_ref[slot, pl.ds(place, turned.shape[0], stride=(rows + 1) * 8), :] = turned
    for copy in copies(step, slot):
        copy.start()

    @pl.when(step == steps - 1)
    def _():
        for copy in copies(step, slot):
            copy.wait()

    @pl.when((step == steps - 1) & (step >= 1))
    def _():
        for copy in copies(step - 1, 1 - slot):
            copy.wait()


def turn(signal, kernel, groups):
    frames, width = signal.shape
    chunk = TURN_ROWS * LANES
    rows = frames // LANES
    block = pl.BlockSpec((chunk, width), lambda i: (i, 0))
    counts = (FIRST_CHANNELS, 8 - FIRST_CHANNELS)
    return pl.pallas_call(
        turn_kernel,
        grid=(frames // chunk,),
        in_specs=[block, block],
        out_specs=[pl.BlockSpec(memory_space=pl.ANY)] * 2,
        out_shape=[jax.ShapeDtypeStruct((groups, n, rows, 8, 128), F32) for n in counts],
        scratch_shapes=[
            pltpu.VMEM((2, width * (TURN_ROWS + 1) * 8, 128), F32),
            pltpu.SemaphoreType.DMA((2, 2)),
        ],
        compiler_params=pltpu.CompilerParams(vmem_limit_bytes=VMEM_LIMIT),
        name="turn",
    )(signal, kernel)


def gather_channel(ref, which):
    groups, _, depth, _ = ref.shape
    tiles = LANES // 128
    flat = ref.reshape(groups * depth, 128)
    rows = groups * depth // 8
    return jnp.concatenate(
        [flat[pl.ds(2 * j + which, rows, stride=8), :] for j in range(tiles)], axis=1
    )


def scatter_channel(ref, slot, value, spare=0):
    tiles = LANES // 128
    for j in range(tiles):
        ref[pl.ds(8 * j + slot, value.shape[0], stride=8 * (tiles + spare)), :] = (
            value[:, j * 128 : (j + 1) * 128]
        )


def first_channels_kernel(skip_ref, data_ref, *rest):
    *table_refs, out_ref = rest
    c = pl.program_id(0)
    result = filter_channel(
        gather_channel(data_ref, 0), gather_channel(data_ref, 1), skip_ref[c],
        *table_refs,
    )
    scatter_channel(out_ref, c, result)


def last_channels_kernel(late, extra, skip_ref, data_ref, *rest):
    *table_refs, before_ref = rest[: len(rest) - 4 - extra]
    late_ref, early_ref, held_ref, sems = rest[-4:]
    c = pl.program_id(0)
    channel = c + FIRST_CHANNELS
    devices, tiles = late_ref.shape[0], late_ref.shape[1] + early_ref.shape[1] - 1
    per_row = LANES // 128
    rows = tiles // per_row
    shaped = held_ref.reshape(devices, rows, per_row + 1, 8, 128)
    load = pltpu.make_async_copy(before_ref, shaped.at[:, :, :per_row], sems.at[0])

    @pl.when(c == 0)
    def _():
        load.start()

    result = filter_channel(
        gather_channel(data_ref, 0), gather_channel(data_ref, 1),
        skip_ref[channel], *table_refs,
    )

    @pl.when(c == 0)
    def _():
        load.wait()

    scatter_channel(held_ref, channel, result, spare=1)

    @pl.when(c == pl.num_programs(0) - 1)
    def _():
        pairs = []
        for row in range(late // per_row, rows):
            at = row * per_row - late
            pairs.append((shaped.at[:, row, :per_row], late_ref.at[:, at : at + per_row]))
        for row in range(late // per_row):
            at = row * per_row
            count = min(per_row, late - 1 - at)
            pairs.append((shaped.at[:, row, :count], early_ref.at[:, at : at + count]))
        edge = shaped.at[:, late // per_row - 1, per_row - 1 : per_row]
        pairs.append((edge, late_ref.at[:, tiles - late : tiles - late + 1]))
        final = shaped.at[:, rows - 1, per_row - 1 : per_row]
        pairs.append((final.at[0 : devices - 1], early_ref.at[1:devices, late - 1 : late]))
        pairs.append((final.at[devices - 1 : devices], early_ref.at[0:1, late - 1 : late]))
        copies = [
            pltpu.make_async_copy(here, there, sems.at[1 + i])
            for i, (here, there) in enumerate(pairs)
        ]
        for copy in copies:
            copy.start()
        for copy in copies:
            copy.wait()


def filter_channels(data, skip, before, devices, late, ready=()):
    groups, channels, group_rows, _, _ = data.shape
    flat = data.reshape(groups, channels, group_rows * 8, 128)
    rows = groups * group_rows
    lane_tiles = LANES // 128
    tiles = rows * lane_tiles // devices
    held = tables(rows)
    held_shape = (rows * lane_tiles * 8, 128)

    def whole(array):
        return pl.BlockSpec(array.shape, lambda c: (0,) * array.ndim)

    in_specs = [
        pl.BlockSpec(memory_space=pltpu.SMEM),
        pl.BlockSpec(
            (groups, 1, group_rows * 8, 128), lambda c: (0, c, 0, 0)
        ),
    ] + [whole(t) for t in held]
    options = dict(
        grid=(channels,),
        compiler_params=pltpu.CompilerParams(vmem_limit_bytes=VMEM_LIMIT),
        cost_estimate=pl.CostEstimate(
            flops=channels * rows * LANES * 2048 * 3 * 3,
            bytes_accessed=channels * rows * LANES * 12,
            transcendentals=0,
        ),
    )
    if before is None:
        return pl.pallas_call(
            first_channels_kernel,
            in_specs=in_specs,
            out_specs=pl.BlockSpec(held_shape, lambda c: (0, 0)),
            out_shape=jax.ShapeDtypeStruct(held_shape, F32),
            name="filter_first",
            **options,
        )(skip, flat, *held)
    anywhere = pl.BlockSpec(memory_space=pl.ANY)
    return pl.pallas_call(
        functools.partial(last_channels_kernel, late, len(ready)),
        in_specs=in_specs + [anywhere] * (1 + len(ready)),
        out_specs=[anywhere, anywhere],
        out_shape=[
            jax.ShapeDtypeStruct((devices, tiles - late + 1, 8, 128), F32),
            jax.ShapeDtypeStruct((devices, late, 8, 128), F32),
        ],
        scratch_shapes=[
            pltpu.VMEM((rows * (lane_tiles + 1) * 8, 128), F32),
            pltpu.SemaphoreType.DMA((4 + tiles // lane_tiles,)),
        ],
        name="filter_last",
        **options,
    )(skip, flat, *held, before.reshape(devices, -1, lane_tiles, 8, 128), *ready)


def frames_by_channels(tile):
    paired = tile.reshape(tile.shape[0] // HEADS, HEADS, 8, 128)
    return jnp.concatenate(
        [jnp.transpose(paired[:, h].reshape(-1, 128), (1, 0)) for h in range(HEADS)], axis=1
    )


def late_kernel(conv_ref, edge_ref, gate_ref, edge_gate_ref, *rest):
    fixed, out_ref, window_ref, scratch = rest[:5], rest[5], rest[6], rest[7:]
    block = gate_ref.shape[0]
    reach = TAPS + 1

    @pl.when(pl.program_id(0) == 0)
    def _():
        window_ref[:reach, :] = frames_by_channels(edge_ref[:, 0]) * edge_gate_ref[...]

    @pl.when(pl.program_id(0) > 0)
    def _():
        window_ref[:reach, :] = window_ref[block : block + reach, :]

    for j in range(block // reach):
        span = slice(j * reach, (j + 1) * reach)
        window_ref[reach + j * reach : 2 * reach + j * reach, :] = (
            frames_by_channels(conv_ref[:, j]) * gate_ref[span, :]
        )
    mix_window(window_ref, fixed, scratch, out_ref)


def early_kernel(conv_ref, edge_ref, gate_ref, halo_ref, halo_gate_ref, *rest):
    fixed, out_ref, window_ref, scratch = rest[:5], rest[6], rest[7], rest[8:]
    block = gate_ref.shape[0]
    reach = TAPS + 1
    last = pl.program_id(0) == pl.num_programs(0) - 1

    @pl.when(pl.program_id(0) == 0)
    def _():
        window_ref[:reach, :] = frames_by_channels(halo_ref[:, 0]) * halo_gate_ref[...]

    @pl.when(pl.program_id(0) > 0)
    def _():
        window_ref[:reach, :] = window_ref[block : block + reach, :]

    count = block // reach
    for j in range(count):
        tile = conv_ref[:, j]
        if j == count - 1:
            tile = jnp.where(last, edge_ref[:, 0], tile)
        span = slice(j * reach, (j + 1) * reach)
        window_ref[reach + j * reach : 2 * reach + j * reach, :] = (
            frames_by_channels(tile) * gate_ref[span, :]
        )
    mix_window(window_ref, fixed, scratch, out_ref)


def tail_part(conv, late, gate_input, halo_gate, before, late_tiles, fixed):
    devices = conv.shape[0]
    frames, width = gate_input.shape
    reach = TAPS + 1
    block = 512
    per_block = block // 128
    edge = late.shape[1] - 1
    first = before is not None

    def whole(array):
        return pl.BlockSpec(array.shape, lambda r: (0,) * array.ndim)

    start = 0 if first else late_tiles // per_block
    count = (late_tiles if first else edge) // per_block
    in_specs = [
        pl.BlockSpec((devices, per_block, 8, 128), lambda r: (0, r, 0, 0)),
        pl.BlockSpec((devices, 1, 8, 128), lambda r: (0, edge, 0, 0)),
        pl.BlockSpec((block, width), lambda r: (r + start, 0)),
    ]
    operands = [conv, late, gate_input]
    if first:
        ahead = late_tiles - 1
        in_specs += [pl.BlockSpec((devices, 1, 8, 128), lambda r: (0, ahead, 0, 0)), whole(halo_gate)]
        operands += [conv, halo_gate]
    else:
        in_specs += [pl.BlockSpec((reach, width), lambda r: (late_tiles - 1, 0))]
        operands += [gate_input]
    in_specs += [whole(array) for array in fixed]
    operands += fixed
    aliases = {}
    if first:
        aliases = {len(operands): 0}
        in_specs += [pl.BlockSpec(memory_space=pl.ANY)]
        operands += [before]
    hidden = fixed[3].shape[1]
    return pl.pallas_call(
        early_kernel if first else late_kernel,
        grid=(count,),
        in_specs=in_specs,
        out_specs=pl.BlockSpec((block, width), lambda r: (r + start, 0)),
        out_shape=jax.ShapeDtypeStruct(gate_input.shape, F32),
        input_output_aliases=aliases,
        scratch_shapes=mix_scratch(block, width, hidden),
        compiler_params=pltpu.CompilerParams(vmem_limit_bytes=VMEM_LIMIT),
        cost_estimate=pl.CostEstimate(
            flops=count * block * 3 * 2 * (2 * width * hidden + 3 * width * width),
            bytes_accessed=count * block * width * 12,
            transcendentals=count * block * hidden,
        ),
        name="mix_early" if first else "mix_late",
    )(*operands)


def owned_eight(signal, kernel, skip_here, gate_input, fixed):
    groups = lax.axis_size("tm")
    devices = groups * lax.axis_size("chan")
    reach = TAPS + 1
    late_tiles = 2 * (512 // 128)

    def enter(array):
        return lax.all_to_all(array, "tm", split_axis=0, concat_axis=0, tiled=True)

    def leave(array):
        return lax.all_to_all(array, ("tm", "chan"), split_axis=0, concat_axis=0, tiled=True)

    ring = [(i, i + 1) for i in range(devices - 1)]
    halo_gate = lax.ppermute(gate_input[-reach:], ("tm", "chan"), ring)
    one, two = turn(signal, kernel, groups)
    before = filter_channels(enter(one), skip_here, None, devices, late_tiles)
    ready = (fixed[0], halo_gate)
    late, early = filter_channels(enter(two), skip_here, before, devices, late_tiles, ready)
    late = leave(late)
    early = leave(early)
    part = tail_part(late, late, gate_input, None, None, late_tiles, fixed)
    return tail_part(early, late, gate_input, halo_gate, part, late_tiles, fixed)


def on_device(
    signal, kernel, skip_gain, gate_input, tap_weight, norm_gain, up_weight, up_bias, down_weight
):
    groups = lax.axis_size("tm")
    pair = lax.axis_size("chan")
    frames_here, channels_here = signal.shape
    owned = channels_here // groups
    width = gate_input.shape[1]
    first_channel = lax.axis_index("chan") * channels_here + lax.axis_index("tm") * owned
    skip_here = lax.dynamic_slice_in_dim(skip_gain, first_channel, owned)
    fixed = fixed_operands(tap_weight, norm_gain, up_weight, up_bias, down_weight)
    window = frames_here * groups
    if owned == 8 and channels_here == 128 and pair == HEADS and window == 256 * LANES:
        if gate_input.shape[0] % 512 == 0 and gate_input.shape[0] >= 2048:
            return owned_eight(signal, kernel, skip_here, gate_input, fixed)

    def enter(array):
        shaped = array.reshape(frames_here // LANES, LANES, groups, owned).transpose(2, 3, 0, 1)
        return lax.all_to_all(shaped, "tm", split_axis=0, concat_axis=0, tiled=True)

    filtered = long_filter(enter(signal), enter(kernel), skip_here, groups * pair)
    back = lax.all_to_all(filtered, ("tm", "chan"), split_axis=0, concat_axis=0, tiled=True)
    blocks = back.reshape(groups, pair, owned, -1, LANES).transpose(3, 1, 0, 2, 4)
    blocks = blocks.reshape(-1, width, LANES)
    reach = TAPS + 1
    last = blocks[-1, :, LANES - reach :].T * gate_input[-reach:]
    devices = groups * pair
    halo = lax.ppermute(last, ("tm", "chan"), [(i, i + 1) for i in range(devices - 1)])
    return tail(blocks, gate_input, halo, fixed)


def solution(mesh):
    placed = (
        P(("grp", "tm"), "chan"),
        P("tm", "chan"),
        P(),
        P(("grp", "tm", "chan"), None),
        P(),
        P(),
        P(),
        P(),
        P(),
    )
    return jax.shard_map(
        on_device,
        mesh=mesh,
        in_specs=placed,
        out_specs=P(("grp", "tm", "chan"), None),
        check_vma=False,
    )
```

```python
import functools
import math

import jax
import jax.numpy as jnp
import numpy as np
from jax import lax
from jax.experimental import pallas as pl
from jax.experimental.pallas import tpu as pltpu
from jax.sharding import PartitionSpec as P
import ml_dtypes

LANES = 512
RADIX = 4
SUB = LANES // RADIX
TAPS = 127
HEADS = 2
EPSILON = 1e-06
BF16 = jnp.bfloat16
F32 = jnp.float32
VMEM_LIMIT = 63 * 1024 * 1024


def table_split(table, axis, order):
    high = table.astype(ml_dtypes.bfloat16)
    low = (table - high.astype(np.float64)).astype(ml_dtypes.bfloat16)
    parts = {"h": high, "l": low}
    return np.concatenate([parts[name] for name in order], axis=axis)


@functools.lru_cache(maxsize=None)
def tables(rows):
    length = rows * LANES
    turn = 2.0 * math.pi
    n1 = np.arange(rows, dtype=np.float64)
    n2 = np.arange(LANES, dtype=np.float64)
    m = np.arange(SUB, dtype=np.float64)
    first = turn * np.outer(n1 + 0.25, n1) / rows
    enter = table_split(np.concatenate([np.cos(first), -np.sin(first)], axis=0), 1, "hl")
    leave = table_split(
        np.concatenate([np.cos(first.T), -np.sin(first.T)], axis=1) / length, 1, "hl"
    )
    twiddle = turn * np.outer(n1 + 0.25, n2) / length
    forward, backward = [], []
    for r in range(RADIX):
        phase = turn * np.outer(m, m / SUB + r / LANES)
        c, s = np.cos(phase), np.sin(phase)
        forward.append(table_split(np.block([[c, -s], [s, c]]), 0, "hl"))
        c, s = c.T, s.T
        backward.append(table_split(np.block([[c, s], [-s, c]]), 0, "hl"))
    return (
        enter,
        np.cos(twiddle).astype(np.float32),
        np.sin(twiddle).astype(np.float32),
        np.stack(forward),
        np.stack(backward),
        leave,
    )


def halves(value):
    high = value.astype(BF16)
    low = (value - high.astype(F32)).astype(BF16)
    return high, low


def split_cat(value, axis):
    high, low = halves(value)
    return jnp.concatenate([high, low, high], axis=axis)


def high_high_low(table, axis):
    size = table.shape[axis] // 2
    high = lax.slice_in_dim(table, 0, size, axis=axis)
    low = lax.slice_in_dim(table, size, 2 * size, axis=axis)
    return jnp.concatenate([high, high, low], axis=axis)


def dot(left, right):
    return jnp.dot(left, right, preferred_element_type=F32)


def filter_channel(signal, kernel, skip, enter_ref, cos_ref, sin_ref, forward_ref, backward_ref,
                   leave_ref):
    rows = cos_ref.shape[0]
    enter = high_high_low(enter_ref[...], 1)
    entered = [dot(enter, split_cat(value, 0)) for value in (signal, kernel)]
    spectra = []
    for turned in entered:
        real_in, imag_in = turned[:rows], turned[rows:]
        real = real_in * cos_ref[...] + imag_in * sin_ref[...]
        imag = imag_in * cos_ref[...] - real_in * sin_ref[...]
        r0, r1, r2, r3 = (real[:, b * SUB : (b + 1) * SUB] for b in range(RADIX))
        i0, i1, i2, i3 = (imag[:, b * SUB : (b + 1) * SUB] for b in range(RADIX))
        er, ei, fr, fi = r0 + r2, i0 + i2, r0 - r2, i0 - i2
        gr, gi, hr, hi = r1 + r3, i1 + i3, r1 - r3, i1 - i3
        spread = ((er + gr, ei + gi), (fr + hi, fi - hr), (er - gr, ei - gi), (fr - hi, fi + hr))
        spectra.append([
            dot(split_cat(jnp.concatenate(pair, axis=1), 1), high_high_low(forward_ref[r], 0))
            for r, pair in enumerate(spread)
        ])
    products = []
    for s, k in zip(*spectra):
        sr, si = s[:, :SUB], s[:, SUB:]
        kr, ki = k[:, :SUB], k[:, SUB:]
        product = jnp.concatenate([sr * kr - si * ki, sr * ki + si * kr], axis=1)
        products.append(split_cat(product, 1))
    back = []
    for r in range(RADIX):
        turned = dot(products[r], high_high_low(backward_ref[r], 0))
        back.append((turned[:, :SUB], turned[:, SUB:]))
    (r0, i0), (r1, i1), (r2, i2), (r3, i3) = back
    er, ei, fr, fi = r0 + r2, i0 + i2, r0 - r2, i0 - i2
    gr, gi, hr, hi = r1 + r3, i1 + i3, r1 - r3, i1 - i3
    real = jnp.concatenate([er + gr, fr - hi, er - gr, fr + hi], axis=1)
    imag = jnp.concatenate([ei + gi, fi + hr, ei - gi, fi - hr], axis=1)
    turned = jnp.concatenate(
        [real * cos_ref[...] - imag * sin_ref[...], imag * cos_ref[...] + real * sin_ref[...]],
        axis=0,
    )
    return dot(high_high_low(leave_ref[...], 1), split_cat(turned, 0)) + skip * signal


def filter_kernel(
    skip_ref, signal_ref, kernel_ref, enter_ref, cos_ref, sin_ref, forward_ref, backward_ref,
    leave_ref, out_ref,
):
    rows = cos_ref.shape[0]
    result = filter_channel(
        signal_ref[...].reshape(rows, LANES), kernel_ref[...].reshape(rows, LANES),
        skip_ref[pl.program_id(0)], enter_ref, cos_ref, sin_ref, forward_ref, backward_ref,
        leave_ref,
    )
    out_ref[...] = result.reshape(out_ref.shape)


def long_filter(signal, kernel, skip, out_groups):
    groups, channels, group_rows, _ = signal.shape
    rows = groups * group_rows
    straight = group_rows % 8 == 0 and (rows // out_groups) % 8 == 0
    in_block = (groups, 1, group_rows, LANES)
    out_shape = (out_groups, channels, rows // out_groups, LANES)
    if not straight:
        signal = signal.transpose(1, 0, 2, 3).reshape(1, channels, rows, LANES)
        kernel = kernel.transpose(1, 0, 2, 3).reshape(1, channels, rows, LANES)
        in_block = (1, 1, rows, LANES)
        out_shape = (1, channels, rows, LANES)
    out_block = (out_shape[0], 1) + out_shape[2:]

    def along(c):
        return (0, c, 0, 0)

    def whole(array):
        return pl.BlockSpec(array.shape, lambda c: (0,) * array.ndim)

    held = tables(rows)
    result = pl.pallas_call(
        filter_kernel,
        grid=(channels,),
        in_specs=[
            pl.BlockSpec(memory_space=pltpu.SMEM),
            pl.BlockSpec(in_block, along),
            pl.BlockSpec(in_block, along),
        ]
        + [whole(table) for table in held],
        out_specs=pl.BlockSpec(out_block, along),
        out_shape=jax.ShapeDtypeStruct(out_shape, F32),
        compiler_params=pltpu.CompilerParams(vmem_limit_bytes=VMEM_LIMIT),
        cost_estimate=pl.CostEstimate(
            flops=channels * rows * LANES * 2048 * 3 * 3,
            bytes_accessed=channels * rows * LANES * 12,
            transcendentals=0,
        ),
        name="long_filter",
    )(skip, signal, kernel, *held)
    if not straight:
        result = result.reshape(channels, out_groups, rows // out_groups, LANES)
        result = result.transpose(1, 0, 2, 3)
    return result


def split_weights(tap_ref, up_ref, down_ref, taps_ref, ups_ref, downs_ref):
    def stacked(weight):
        high, low = halves(weight)
        return jnp.concatenate([high, high, low], axis=0)

    taps_ref[...] = stacked(tap_ref[...])
    chunks, _, chunk = ups_ref.shape
    for n in range(chunks):
        span = slice(n * chunk, (n + 1) * chunk)
        ups_ref[n] = stacked(up_ref[:, span])
        downs_ref[n] = stacked(down_ref[span, :])


def mix_block(window_ref, gain_ref, bias_ref, out_ref, high_ref, low_ref, mix_ref, taps_ref, ups_ref,
              downs_ref):
    block, width = out_ref.shape
    reach = TAPS + 1
    head_width = width // HEADS
    high, low = halves(window_ref[...])
    high_ref[...] = high
    low_ref[...] = low
    taps = dot(
        jnp.concatenate([high[reach:], low[reach:], high[reach:]], axis=1), taps_ref[...]
    )
    for b in range(block // reach):
        for h in range(HEADS):
            own = taps[b * reach : (b + 1) * reach, h * reach : (h + 1) * reach]
            band = jnp.concatenate([own, jnp.zeros_like(own)], axis=1)
            band = pltpu.roll(band, 1, 1, stride=1, stride_axis=0)
            near_rows = slice(b * reach, (b + 2) * reach)
            columns = slice(h * head_width, (h + 1) * head_width)
            near_high = high_ref[near_rows, columns]
            near_low = low_ref[near_rows, columns]
            mix_ref[b * reach : (b + 1) * reach, columns] = dot(
                split_cat(band, 1), jnp.concatenate([near_high, near_high, near_low], axis=0)
            )
    mixed = mix_ref[...]
    mean_square = jnp.mean(mixed * mixed, axis=1, keepdims=True)
    normed = split_cat(mixed * lax.rsqrt(mean_square + EPSILON) * gain_ref[...], 1)
    total = mixed
    chunks, _, chunk = ups_ref.shape
    scale = math.sqrt(2.0 / math.pi)
    for n in range(chunks):
        raised = dot(normed, ups_ref[n]) + bias_ref[:, n * chunk : (n + 1) * chunk]
        inner = raised * (scale + (scale * 0.044715) * (raised * raised))
        half = 0.5 * raised
        total = total + dot(split_cat(half + half * jnp.tanh(inner), 1), downs_ref[n])
    out_ref[...] = total


def mix_scratch(block, width, hidden):
    reach = TAPS + 1
    chunk = 256 if hidden % 256 == 0 else hidden
    return [
        pltpu.VMEM((block + reach, width), F32),
        pltpu.VMEM((block + reach, width), BF16),
        pltpu.VMEM((block + reach, width), BF16),
        pltpu.VMEM((block, width), F32),
        pltpu.VMEM((3 * width, HEADS * reach), BF16),
        pltpu.VMEM((hidden // chunk, 3 * width, chunk), BF16),
        pltpu.VMEM((hidden // chunk, 3 * chunk, width), BF16),
    ]


def mix_window(window_ref, fixed, scratch, out_ref):
    tap_ref, gain_ref, up_ref, bias_ref, down_ref = fixed
    weights = scratch[3:]

    @pl.when(pl.program_id(0) == 0)
    def _():
        split_weights(tap_ref, up_ref, down_ref, *weights)

    mix_block(window_ref, gain_ref, bias_ref, out_ref, *scratch)


def mix_kernel(conv_ref, gate_ref, halo_ref, *rest):
    fixed, out_ref, window_ref, scratch = rest[:5], rest[5], rest[6], rest[7:]
    block = gate_ref.shape[0]
    reach = TAPS + 1

    @pl.when(pl.program_id(0) == 0)
    def _():
        window_ref[:reach, :] = halo_ref[...]

    @pl.when(pl.program_id(0) > 0)
    def _():
        window_ref[:reach, :] = window_ref[block : block + reach, :]

    window_ref[reach:, :] = jnp.transpose(conv_ref[0], (1, 0)) * gate_ref[...]
    mix_window(window_ref, fixed, scratch, out_ref)


def fixed_operands(tap_weight, norm_gain, up_weight, up_bias, down_weight):
    width = tap_weight.shape[0]
    taps = tap_weight.reshape(width, HEADS, TAPS)[:, :, ::-1]
    taps = jnp.pad(taps, ((0, 0), (0, 0), (1, 0))).reshape(width, HEADS * (TAPS + 1))
    return (
        taps,
        norm_gain.reshape(1, -1),
        up_weight,
        up_bias.reshape(1, -1),
        down_weight,
    )


def tail(conv_blocks, gate_input, halo, fixed):
    count, width, block = conv_blocks.shape
    reach = TAPS + 1
    hidden = fixed[3].shape[1]

    def whole(array):
        return pl.BlockSpec(array.shape, lambda r: (0,) * array.ndim)

    return pl.pallas_call(
        mix_kernel,
        grid=(count,),
        in_specs=[
            pl.BlockSpec((1, width, block), lambda r: (r, 0, 0)),
            pl.BlockSpec((block, width), lambda r: (r, 0)),
            whole(halo),
        ]
        + [whole(array) for array in fixed],
        out_specs=pl.BlockSpec((block, width), lambda r: (r, 0)),
        out_shape=jax.ShapeDtypeStruct(gate_input.shape, F32),
        scratch_shapes=mix_scratch(block, width, hidden),
        compiler_params=pltpu.CompilerParams(vmem_limit_bytes=VMEM_LIMIT),
        cost_estimate=pl.CostEstimate(
            flops=count * block * 3 * 2 * (2 * width * hidden + 3 * width * width),
            bytes_accessed=count * block * width * 12,
            transcendentals=count * block * hidden,
        ),
        name="mix_and_mlp",
    )(conv_blocks, gate_input, halo, *fixed)


FIRST_CHANNELS = 6
TURN_ROWS = 8


def turn_kernel(signal_ref, kernel_ref, first_ref, second_ref, held_ref, sems):
    groups, early = first_ref.shape[:2]
    rows = signal_ref.shape[0] // LANES
    step, steps = pl.program_id(0), pl.num_programs(0)
    slot = step % 2

    def copies(at, slot):
        shaped = held_ref.at[slot].reshape(groups, 8, rows + 1, 8, 128)
        there = pl.ds(at * rows, rows)
        return (
            pltpu.make_async_copy(
                shaped.at[:, :early, :rows], first_ref.at[:, :, there], sems.at[slot, 0]
            ),
            pltpu.make_async_copy(
                shaped.at[:, early:, :rows], second_ref.at[:, :, there], sems.at[slot, 1]
            ),
        )

    @pl.when(step >= 2)
    def _():
        for copy in copies(step - 2, slot):
            copy.wait()

    for row in range(rows):
        for j in range(LANES // 128):
            span = slice(row * LANES + j * 128, row * LANES + (j + 1) * 128)
            for which, ref in enumerate((signal_ref, kernel_ref)):
                turned = jnp.transpose(ref[span, :], (1, 0))
                place = row * 8 + j * 2 + which
                held_ref[slot, pl.ds(place, turned.shape[0], stride=(rows + 1) * 8), :] = turned
    for copy in copies(step, slot):
        copy.start()

    @pl.when(step == steps - 1)
    def _():
        for copy in copies(step, slot):
            copy.wait()

    @pl.when((step == steps - 1) & (step >= 1))
    def _():
        for copy in copies(step - 1, 1 - slot):
            copy.wait()


def turn(signal, kernel, groups):
    frames, width = signal.shape
    chunk = TURN_ROWS * LANES
    rows = frames // LANES
    block = pl.BlockSpec((chunk, width), lambda i: (i, 0))
    counts = (FIRST_CHANNELS, 8 - FIRST_CHANNELS)
    return pl.pallas_call(
        turn_kernel,
        grid=(frames // chunk,),
        in_specs=[block, block],
        out_specs=[pl.BlockSpec(memory_space=pl.ANY)] * 2,
        out_shape=[jax.ShapeDtypeStruct((groups, n, rows, 8, 128), F32) for n in counts],
        scratch_shapes=[
            pltpu.VMEM((2, width * (TURN_ROWS + 1) * 8, 128), F32),
            pltpu.SemaphoreType.DMA((2, 2)),
        ],
        compiler_params=pltpu.CompilerParams(vmem_limit_bytes=VMEM_LIMIT),
        name="turn",
    )(signal, kernel)


def gather_channel(ref, which):
    groups, _, depth, _ = ref.shape
    tiles = LANES // 128
    flat = ref.reshape(groups * depth, 128)
    rows = groups * depth // 8
    return jnp.concatenate(
        [flat[pl.ds(2 * j + which, rows, stride=8), :] for j in range(tiles)], axis=1
    )


def scatter_channel(ref, slot, value, spare=0):
    tiles = LANES // 128
    for j in range(tiles):
        ref[pl.ds(8 * j + slot, value.shape[0], stride=8 * (tiles + spare)), :] = (
            value[:, j * 128 : (j + 1) * 128]
        )


def first_channels_kernel(skip_ref, data_ref, *rest):
    *table_refs, out_ref = rest
    c = pl.program_id(0)
    result = filter_channel(
        gather_channel(data_ref, 0), gather_channel(data_ref, 1), skip_ref[c],
        *table_refs,
    )
    scatter_channel(out_ref, c, result)


def last_channels_kernel(late, extra, skip_ref, data_ref, *rest):
    *table_refs, before_ref = rest[: len(rest) - 4 - extra]
    late_ref, early_ref, held_ref, sems = rest[-4:]
    c = pl.program_id(0)
    channel = c + FIRST_CHANNELS
    devices, tiles = late_ref.shape[0], late_ref.shape[1] + early_ref.shape[1] - 1
    per_row = LANES // 128
    rows = tiles // per_row
    shaped = held_ref.reshape(devices, rows, per_row + 1, 8, 128)
    load = pltpu.make_async_copy(before_ref, shaped.at[:, :, :per_row], sems.at[0])

    @pl.when(c == 0)
    def _():
        load.start()

    result = filter_channel(
        gather_channel(data_ref, 0), gather_channel(data_ref, 1),
        skip_ref[channel], *table_refs,
    )

    @pl.when(c == 0)
    def _():
        load.wait()

    scatter_channel(held_ref, channel, result, spare=1)

    @pl.when(c == pl.num_programs(0) - 1)
    def _():
        pairs = []
        for row in range(late // per_row, rows):
            at = row * per_row - late
            pairs.append((shaped.at[:, row, :per_row], late_ref.at[:, at : at + per_row]))
        for row in range(late // per_row):
            at = row * per_row
            count = min(per_row, late - 1 - at)
            pairs.append((shaped.at[:, row, :count], early_ref.at[:, at : at + count]))
        edge = shaped.at[:, late // per_row - 1, per_row - 1 : per_row]
        pairs.append((edge, late_ref.at[:, tiles - late : tiles - late + 1]))
        final = shaped.at[:, rows - 1, per_row - 1 : per_row]
        pairs.append((final.at[0 : devices - 1], early_ref.at[1:devices, late - 1 : late]))
        pairs.append((final.at[devices - 1 : devices], early_ref.at[0:1, late - 1 : late]))
        copies = [
            pltpu.make_async_copy(here, there, sems.at[1 + i])
            for i, (here, there) in enumerate(pairs)
        ]
        for copy in copies:
            copy.start()
        for copy in copies:
            copy.wait()


def filter_channels(data, skip, before, devices, late, ready=()):
    groups, channels, group_rows, _, _ = data.shape
    flat = data.reshape(groups, channels, group_rows * 8, 128)
    rows = groups * group_rows
    lane_tiles = LANES // 128
    tiles = rows * lane_tiles // devices
    held = tables(rows)
    held_shape = (rows * lane_tiles * 8, 128)

    def whole(array):
        return pl.BlockSpec(array.shape, lambda c: (0,) * array.ndim)

    in_specs = [
        pl.BlockSpec(memory_space=pltpu.SMEM),
        pl.BlockSpec(
            (groups, 1, group_rows * 8, 128), lambda c: (0, c, 0, 0)
        ),
    ] + [whole(t) for t in held]
    options = dict(
        grid=(channels,),
        compiler_params=pltpu.CompilerParams(vmem_limit_bytes=VMEM_LIMIT),
        cost_estimate=pl.CostEstimate(
            flops=channels * rows * LANES * 2048 * 3 * 3,
            bytes_accessed=channels * rows * LANES * 12,
            transcendentals=0,
        ),
    )
    if before is None:
        return pl.pallas_call(
            first_channels_kernel,
            in_specs=in_specs,
            out_specs=pl.BlockSpec(held_shape, lambda c: (0, 0)),
            out_shape=jax.ShapeDtypeStruct(held_shape, F32),
            name="filter_first",
            **options,
        )(skip, flat, *held)
    anywhere = pl.BlockSpec(memory_space=pl.ANY)
    return pl.pallas_call(
        functools.partial(last_channels_kernel, late, len(ready)),
        in_specs=in_specs + [anywhere] * (1 + len(ready)),
        out_specs=[anywhere, anywhere],
        out_shape=[
            jax.ShapeDtypeStruct((devices, tiles - late + 1, 8, 128), F32),
            jax.ShapeDtypeStruct((devices, late, 8, 128), F32),
        ],
        scratch_shapes=[
            pltpu.VMEM((rows * (lane_tiles + 1) * 8, 128), F32),
            pltpu.SemaphoreType.DMA((4 + tiles // lane_tiles,)),
        ],
        name="filter_last",
        **options,
    )(skip, flat, *held, before.reshape(devices, -1, lane_tiles, 8, 128), *ready)


def frames_by_channels(tile):
    paired = tile.reshape(tile.shape[0] // HEADS, HEADS, 8, 128)
    return jnp.concatenate(
        [jnp.transpose(paired[:, h].reshape(-1, 128), (1, 0)) for h in range(HEADS)], axis=1
    )


def late_kernel(conv_ref, edge_ref, gate_ref, edge_gate_ref, *rest):
    fixed, out_ref, window_ref, scratch = rest[:5], rest[5], rest[6], rest[7:]
    block = gate_ref.shape[0]
    reach = TAPS + 1

    @pl.when(pl.program_id(0) == 0)
    def _():
        window_ref[:reach, :] = frames_by_channels(edge_ref[:, 0]) * edge_gate_ref[...]

    @pl.when(pl.program_id(0) > 0)
    def _():
        window_ref[:reach, :] = window_ref[block : block + reach, :]

    for j in range(block // reach):
        span = slice(j * reach, (j + 1) * reach)
        window_ref[reach + j * reach : 2 * reach + j * reach, :] = (
            frames_by_channels(conv_ref[:, j]) * gate_ref[span, :]
        )
    mix_window(window_ref, fixed, scratch, out_ref)


def early_kernel(conv_ref, edge_ref, gate_ref, halo_ref, halo_gate_ref, *rest):
    fixed, out_ref, window_ref, scratch = rest[:5], rest[6], rest[7], rest[8:]
    block = gate_ref.shape[0]
    reach = TAPS + 1
    last = pl.program_id(0) == pl.num_programs(0) - 1

    @pl.when(pl.program_id(0) == 0)
    def _():
        window_ref[:reach, :] = frames_by_channels(halo_ref[:, 0]) * halo_gate_ref[...]

    @pl.when(pl.program_id(0) > 0)
    def _():
        window_ref[:reach, :] = window_ref[block : block + reach, :]

    count = block // reach
    for j in range(count):
        tile = conv_ref[:, j]
        if j == count - 1:
            tile = jnp.where(last, edge_ref[:, 0], tile)
        span = slice(j * reach, (j + 1) * reach)
        window_ref[reach + j * reach : 2 * reach + j * reach, :] = (
            frames_by_channels(tile) * gate_ref[span, :]
        )
    mix_window(window_ref, fixed, scratch, out_ref)


def tail_part(conv, late, gate_input, halo_gate, before, late_tiles, fixed):
    devices = conv.shape[0]
    frames, width = gate_input.shape
    reach = TAPS + 1
    block = 1024
    per_block = block // 128
    edge = late.shape[1] - 1
    first = before is not None

    def whole(array):
        return pl.BlockSpec(array.shape, lambda r: (0,) * array.ndim)

    start = 0 if first else late_tiles // per_block
    count = (late_tiles if first else edge) // per_block
    in_specs = [
        pl.BlockSpec((devices, per_block, 8, 128), lambda r: (0, r, 0, 0)),
        pl.BlockSpec((devices, 1, 8, 128), lambda r: (0, edge, 0, 0)),
        pl.BlockSpec((block, width), lambda r: (r + start, 0)),
    ]
    operands = [conv, late, gate_input]
    if first:
        ahead = late_tiles - 1
        in_specs += [pl.BlockSpec((devices, 1, 8, 128), lambda r: (0, ahead, 0, 0)), whole(halo_gate)]
        operands += [conv, halo_gate]
    else:
        in_specs += [pl.BlockSpec((reach, width), lambda r: (late_tiles - 1, 0))]
        operands += [gate_input]
    in_specs += [whole(array) for array in fixed]
    operands += fixed
    aliases = {}
    if first:
        aliases = {len(operands): 0}
        in_specs += [pl.BlockSpec(memory_space=pl.ANY)]
        operands += [before]
    hidden = fixed[3].shape[1]
    return pl.pallas_call(
        early_kernel if first else late_kernel,
        grid=(count,),
        in_specs=in_specs,
        out_specs=pl.BlockSpec((block, width), lambda r: (r + start, 0)),
        out_shape=jax.ShapeDtypeStruct(gate_input.shape, F32),
        input_output_aliases=aliases,
        scratch_shapes=mix_scratch(block, width, hidden),
        compiler_params=pltpu.CompilerParams(vmem_limit_bytes=VMEM_LIMIT),
        cost_estimate=pl.CostEstimate(
            flops=count * block * 3 * 2 * (2 * width * hidden + 3 * width * width),
            bytes_accessed=count * block * width * 12,
            transcendentals=count * block * hidden,
        ),
        name="mix_early" if first else "mix_late",
    )(*operands)


def owned_eight(signal, kernel, skip_here, gate_input, fixed):
    groups = lax.axis_size("tm")
    devices = groups * lax.axis_size("chan")
    reach = TAPS + 1
    late_tiles = 2 * (512 // 128)

    def enter(array):
        return lax.all_to_all(array, "tm", split_axis=0, concat_axis=0, tiled=True)

    def leave(array):
        return lax.all_to_all(array, ("tm", "chan"), split_axis=0, concat_axis=0, tiled=True)

    ring = [(i, i + 1) for i in range(devices - 1)]
    halo_gate = lax.ppermute(gate_input[-reach:], ("tm", "chan"), ring)
    one, two = turn(signal, kernel, groups)
    before = filter_channels(enter(one), skip_here, None, devices, late_tiles)
    ready = (fixed[0], halo_gate)
    late, early = filter_channels(enter(two), skip_here, before, devices, late_tiles, ready)
    late = leave(late)
    early = leave(early)
    part = tail_part(late, late, gate_input, None, None, late_tiles, fixed)
    return tail_part(early, late, gate_input, halo_gate, part, late_tiles, fixed)


def on_device(
    signal, kernel, skip_gain, gate_input, tap_weight, norm_gain, up_weight, up_bias, down_weight
):
    groups = lax.axis_size("tm")
    pair = lax.axis_size("chan")
    frames_here, channels_here = signal.shape
    owned = channels_here // groups
    width = gate_input.shape[1]
    first_channel = lax.axis_index("chan") * channels_here + lax.axis_index("tm") * owned
    skip_here = lax.dynamic_slice_in_dim(skip_gain, first_channel, owned)
    fixed = fixed_operands(tap_weight, norm_gain, up_weight, up_bias, down_weight)
    window = frames_here * groups
    if owned == 8 and channels_here == 128 and pair == HEADS and window == 256 * LANES:
        if gate_input.shape[0] % 1024 == 0 and gate_input.shape[0] >= 2048:
            return owned_eight(signal, kernel, skip_here, gate_input, fixed)

    def enter(array):
        shaped = array.reshape(frames_here // LANES, LANES, groups, owned).transpose(2, 3, 0, 1)
        return lax.all_to_all(shaped, "tm", split_axis=0, concat_axis=0, tiled=True)

    filtered = long_filter(enter(signal), enter(kernel), skip_here, groups * pair)
    back = lax.all_to_all(filtered, ("tm", "chan"), split_axis=0, concat_axis=0, tiled=True)
    blocks = back.reshape(groups, pair, owned, -1, LANES).transpose(3, 1, 0, 2, 4)
    blocks = blocks.reshape(-1, width, LANES)
    reach = TAPS + 1
    last = blocks[-1, :, LANES - reach :].T * gate_input[-reach:]
    devices = groups * pair
    halo = lax.ppermute(last, ("tm", "chan"), [(i, i + 1) for i in range(devices - 1)])
    return tail(blocks, gate_input, halo, fixed)


def solution(mesh):
    placed = (
        P(("grp", "tm"), "chan"),
        P("tm", "chan"),
        P(),
        P(("grp", "tm", "chan"), None),
        P(),
        P(),
        P(),
        P(),
        P(),
    )
    return jax.shard_map(
        on_device,
        mesh=mesh,
        in_specs=placed,
        out_specs=P(("grp", "tm", "chan"), None),
        check_vma=False,
    )
```

```python
import functools
import math

import jax
import jax.numpy as jnp
import numpy as np
from jax import lax
from jax.experimental import pallas as pl
from jax.experimental.pallas import tpu as pltpu
from jax.sharding import PartitionSpec as P
import ml_dtypes

LANES = 512
RADIX = 4
SUB = LANES // RADIX
TAPS = 127
HEADS = 2
EPSILON = 1e-06
BF16 = jnp.bfloat16
F32 = jnp.float32
VMEM_LIMIT = 63 * 1024 * 1024


def table_split(table, axis, order):
    high = table.astype(ml_dtypes.bfloat16)
    low = (table - high.astype(np.float64)).astype(ml_dtypes.bfloat16)
    parts = {"h": high, "l": low}
    return np.concatenate([parts[name] for name in order], axis=axis)


@functools.lru_cache(maxsize=None)
def tables(rows):
    length = rows * LANES
    turn = 2.0 * math.pi
    n1 = np.arange(rows, dtype=np.float64)
    n2 = np.arange(LANES, dtype=np.float64)
    m = np.arange(SUB, dtype=np.float64)
    first = turn * np.outer(n1 + 0.25, n1) / rows
    enter = table_split(np.concatenate([np.cos(first), -np.sin(first)], axis=0), 1, "hl")
    leave = table_split(
        np.concatenate([np.cos(first.T), -np.sin(first.T)], axis=1) / length, 1, "hl"
    )
    twiddle = turn * np.outer(n1 + 0.25, n2) / length
    forward, backward = [], []
    for r in range(RADIX):
        phase = turn * np.outer(m, m / SUB + r / LANES)
        c, s = np.cos(phase), np.sin(phase)
        forward.append(table_split(np.block([[c, -s], [s, c]]), 0, "hl"))
        c, s = c.T, s.T
        backward.append(table_split(np.block([[c, s], [-s, c]]), 0, "hl"))
    return (
        enter,
        np.cos(twiddle).astype(np.float32),
        np.sin(twiddle).astype(np.float32),
        np.stack(forward),
        np.stack(backward),
        leave,
    )


def halves(value):
    high = value.astype(BF16)
    low = (value - high.astype(F32)).astype(BF16)
    return high, low


def split_cat(value, axis):
    high, low = halves(value)
    return jnp.concatenate([high, low, high], axis=axis)


def high_high_low(table, axis):
    size = table.shape[axis] // 2
    high = lax.slice_in_dim(table, 0, size, axis=axis)
    low = lax.slice_in_dim(table, size, 2 * size, axis=axis)
    return jnp.concatenate([high, high, low], axis=axis)


def dot(left, right):
    return jnp.dot(left, right, preferred_element_type=F32)


def filter_channel(signal, kernel, skip, enter_ref, cos_ref, sin_ref, forward_ref, backward_ref,
                   leave_ref):
    rows = cos_ref.shape[0]
    enter = high_high_low(enter_ref[...], 1)
    entered = [dot(enter, split_cat(value, 0)) for value in (signal, kernel)]
    spectra = []
    for turned in entered:
        real_in, imag_in = turned[:rows], turned[rows:]
        real = real_in * cos_ref[...] + imag_in * sin_ref[...]
        imag = imag_in * cos_ref[...] - real_in * sin_ref[...]
        r0, r1, r2, r3 = (real[:, b * SUB : (b + 1) * SUB] for b in range(RADIX))
        i0, i1, i2, i3 = (imag[:, b * SUB : (b + 1) * SUB] for b in range(RADIX))
        er, ei, fr, fi = r0 + r2, i0 + i2, r0 - r2, i0 - i2
        gr, gi, hr, hi = r1 + r3, i1 + i3, r1 - r3, i1 - i3
        spread = ((er + gr, ei + gi), (fr + hi, fi - hr), (er - gr, ei - gi), (fr - hi, fi + hr))
        spectra.append([
            dot(split_cat(jnp.concatenate(pair, axis=1), 1), high_high_low(forward_ref[r], 0))
            for r, pair in enumerate(spread)
        ])
    products = []
    for s, k in zip(*spectra):
        sr, si = s[:, :SUB], s[:, SUB:]
        kr, ki = k[:, :SUB], k[:, SUB:]
        product = jnp.concatenate([sr * kr - si * ki, sr * ki + si * kr], axis=1)
        products.append(split_cat(product, 1))
    back = []
    for r in range(RADIX):
        turned = dot(products[r], high_high_low(backward_ref[r], 0))
        back.append((turned[:, :SUB], turned[:, SUB:]))
    (r0, i0), (r1, i1), (r2, i2), (r3, i3) = back
    er, ei, fr, fi = r0 + r2, i0 + i2, r0 - r2, i0 - i2
    gr, gi, hr, hi = r1 + r3, i1 + i3, r1 - r3, i1 - i3
    real = jnp.concatenate([er + gr, fr - hi, er - gr, fr + hi], axis=1)
    imag = jnp.concatenate([ei + gi, fi + hr, ei - gi, fi - hr], axis=1)
    turned = jnp.concatenate(
        [real * cos_ref[...] - imag * sin_ref[...], imag * cos_ref[...] + real * sin_ref[...]],
        axis=0,
    )
    return dot(high_high_low(leave_ref[...], 1), split_cat(turned, 0)) + skip * signal


def filter_kernel(
    skip_ref, signal_ref, kernel_ref, enter_ref, cos_ref, sin_ref, forward_ref, backward_ref,
    leave_ref, out_ref,
):
    rows = cos_ref.shape[0]
    result = filter_channel(
        signal_ref[...].reshape(rows, LANES), kernel_ref[...].reshape(rows, LANES),
        skip_ref[pl.program_id(0)], enter_ref, cos_ref, sin_ref, forward_ref, backward_ref,
        leave_ref,
    )
    out_ref[...] = result.reshape(out_ref.shape)


def long_filter(signal, kernel, skip, out_groups):
    groups, channels, group_rows, _ = signal.shape
    rows = groups * group_rows
    straight = group_rows % 8 == 0 and (rows // out_groups) % 8 == 0
    in_block = (groups, 1, group_rows, LANES)
    out_shape = (out_groups, channels, rows // out_groups, LANES)
    if not straight:
        signal = signal.transpose(1, 0, 2, 3).reshape(1, channels, rows, LANES)
        kernel = kernel.transpose(1, 0, 2, 3).reshape(1, channels, rows, LANES)
        in_block = (1, 1, rows, LANES)
        out_shape = (1, channels, rows, LANES)
    out_block = (out_shape[0], 1) + out_shape[2:]

    def along(c):
        return (0, c, 0, 0)

    def whole(array):
        return pl.BlockSpec(array.shape, lambda c: (0,) * array.ndim)

    held = tables(rows)
    result = pl.pallas_call(
        filter_kernel,
        grid=(channels,),
        in_specs=[
            pl.BlockSpec(memory_space=pltpu.SMEM),
            pl.BlockSpec(in_block, along),
            pl.BlockSpec(in_block, along),
        ]
        + [whole(table) for table in held],
        out_specs=pl.BlockSpec(out_block, along),
        out_shape=jax.ShapeDtypeStruct(out_shape, F32),
        compiler_params=pltpu.CompilerParams(vmem_limit_bytes=VMEM_LIMIT),
        cost_estimate=pl.CostEstimate(
            flops=channels * rows * LANES * 2048 * 3 * 3,
            bytes_accessed=channels * rows * LANES * 12,
            transcendentals=0,
        ),
        name="long_filter",
    )(skip, signal, kernel, *held)
    if not straight:
        result = result.reshape(channels, out_groups, rows // out_groups, LANES)
        result = result.transpose(1, 0, 2, 3)
    return result


def split_weights(tap_ref, up_ref, down_ref, taps_ref, ups_ref, downs_ref):
    def stacked(weight):
        high, low = halves(weight)
        return jnp.concatenate([high, high, low], axis=0)

    taps_ref[...] = stacked(tap_ref[...])
    chunks, _, chunk = ups_ref.shape
    for n in range(chunks):
        span = slice(n * chunk, (n + 1) * chunk)
        ups_ref[n] = stacked(up_ref[:, span])
        downs_ref[n] = stacked(down_ref[span, :])


def mix_block(window_ref, gain_ref, bias_ref, out_ref, high_ref, low_ref, mix_ref, taps_ref, ups_ref,
              downs_ref):
    block, width = out_ref.shape
    reach = TAPS + 1
    head_width = width // HEADS
    high, low = halves(window_ref[...])
    high_ref[...] = high
    low_ref[...] = low
    taps = dot(
        jnp.concatenate([high[reach:], low[reach:], high[reach:]], axis=1), taps_ref[...]
    )
    for b in range(block // reach):
        for h in range(HEADS):
            own = taps[b * reach : (b + 1) * reach, h * reach : (h + 1) * reach]
            band = jnp.concatenate([own, jnp.zeros_like(own)], axis=1)
            band = pltpu.roll(band, 1, 1, stride=1, stride_axis=0)
            near_rows = slice(b * reach, (b + 2) * reach)
            columns = slice(h * head_width, (h + 1) * head_width)
            near_high = high_ref[near_rows, columns]
            near_low = low_ref[near_rows, columns]
            mix_ref[b * reach : (b + 1) * reach, columns] = dot(
                split_cat(band, 1), jnp.concatenate([near_high, near_high, near_low], axis=0)
            )
    mixed = mix_ref[...]
    mean_square = jnp.mean(mixed * mixed, axis=1, keepdims=True)
    normed = split_cat(mixed * lax.rsqrt(mean_square + EPSILON) * gain_ref[...], 1)
    total = mixed
    chunks, _, chunk = ups_ref.shape
    scale = math.sqrt(2.0 / math.pi)
    for n in range(chunks):
        raised = dot(normed, ups_ref[n]) + bias_ref[:, n * chunk : (n + 1) * chunk]
        inner = raised * (scale + (scale * 0.044715) * (raised * raised))
        half = 0.5 * raised
        total = total + dot(split_cat(half + half * jnp.tanh(inner), 1), downs_ref[n])
    out_ref[...] = total


def mix_scratch(block, width, hidden):
    reach = TAPS + 1
    chunk = 256 if hidden % 256 == 0 else hidden
    return [
        pltpu.VMEM((block + reach, width), F32),
        pltpu.VMEM((block + reach, width), BF16),
        pltpu.VMEM((block + reach, width), BF16),
        pltpu.VMEM((block, width), F32),
        pltpu.VMEM((3 * width, HEADS * reach), BF16),
        pltpu.VMEM((hidden // chunk, 3 * width, chunk), BF16),
        pltpu.VMEM((hidden // chunk, 3 * chunk, width), BF16),
    ]


def mix_window(window_ref, fixed, scratch, out_ref):
    tap_ref, gain_ref, up_ref, bias_ref, down_ref = fixed
    weights = scratch[3:]

    @pl.when(pl.program_id(0) == 0)
    def _():
        split_weights(tap_ref, up_ref, down_ref, *weights)

    mix_block(window_ref, gain_ref, bias_ref, out_ref, *scratch)


def mix_kernel(conv_ref, gate_ref, halo_ref, *rest):
    fixed, out_ref, window_ref, scratch = rest[:5], rest[5], rest[6], rest[7:]
    block = gate_ref.shape[0]
    reach = TAPS + 1

    @pl.when(pl.program_id(0) == 0)
    def _():
        window_ref[:reach, :] = halo_ref[...]

    @pl.when(pl.program_id(0) > 0)
    def _():
        window_ref[:reach, :] = window_ref[block : block + reach, :]

    window_ref[reach:, :] = jnp.transpose(conv_ref[0], (1, 0)) * gate_ref[...]
    mix_window(window_ref, fixed, scratch, out_ref)


def fixed_operands(tap_weight, norm_gain, up_weight, up_bias, down_weight):
    width = tap_weight.shape[0]
    taps = tap_weight.reshape(width, HEADS, TAPS)[:, :, ::-1]
    taps = jnp.pad(taps, ((0, 0), (0, 0), (1, 0))).reshape(width, HEADS * (TAPS + 1))
    return (
        taps,
        norm_gain.reshape(1, -1),
        up_weight,
        up_bias.reshape(1, -1),
        down_weight,
    )


def tail(conv_blocks, gate_input, halo, fixed):
    count, width, block = conv_blocks.shape
    reach = TAPS + 1
    hidden = fixed[3].shape[1]

    def whole(array):
        return pl.BlockSpec(array.shape, lambda r: (0,) * array.ndim)

    return pl.pallas_call(
        mix_kernel,
        grid=(count,),
        in_specs=[
            pl.BlockSpec((1, width, block), lambda r: (r, 0, 0)),
            pl.BlockSpec((block, width), lambda r: (r, 0)),
            whole(halo),
        ]
        + [whole(array) for array in fixed],
        out_specs=pl.BlockSpec((block, width), lambda r: (r, 0)),
        out_shape=jax.ShapeDtypeStruct(gate_input.shape, F32),
        scratch_shapes=mix_scratch(block, width, hidden),
        compiler_params=pltpu.CompilerParams(vmem_limit_bytes=VMEM_LIMIT),
        cost_estimate=pl.CostEstimate(
            flops=count * block * 3 * 2 * (2 * width * hidden + 3 * width * width),
            bytes_accessed=count * block * width * 12,
            transcendentals=count * block * hidden,
        ),
        name="mix_and_mlp",
    )(conv_blocks, gate_input, halo, *fixed)


FIRST_CHANNELS = 6
TURN_ROWS = 8


def turn_kernel(low, signal_ref, kernel_ref, out_ref, held_ref, sems):
    groups, channels = out_ref.shape[:2]
    rows = signal_ref.shape[0] // LANES
    step, steps = pl.program_id(0), pl.num_programs(0)
    slot = step % 2

    def copies(at, slot):
        shaped = held_ref.at[slot].reshape(groups, 8, rows + 1, 8, 128)
        there = pl.ds(at * rows, rows)
        return (
            pltpu.make_async_copy(
                shaped.at[:, low : low + channels, :rows], out_ref.at[:, :, there], sems.at[slot]
            ),
        )

    @pl.when(step >= 2)
    def _():
        for copy in copies(step - 2, slot):
            copy.wait()

    for row in range(rows):
        for j in range(LANES // 128):
            span = slice(row * LANES + j * 128, row * LANES + (j + 1) * 128)
            for which, ref in enumerate((signal_ref, kernel_ref)):
                turned = jnp.transpose(ref[span, :], (1, 0))
                place = row * 8 + j * 2 + which
                held_ref[slot, pl.ds(place, turned.shape[0], stride=(rows + 1) * 8), :] = turned
    for copy in copies(step, slot):
        copy.start()

    @pl.when(step == steps - 1)
    def _():
        for copy in copies(step, slot):
            copy.wait()

    @pl.when((step == steps - 1) & (step >= 1))
    def _():
        for copy in copies(step - 1, 1 - slot):
            copy.wait()


def turn(signal, kernel, groups, low, high):
    frames, width = signal.shape
    chunk = TURN_ROWS * LANES
    block = pl.BlockSpec((chunk, width), lambda i: (i, 0))
    return pl.pallas_call(
        functools.partial(turn_kernel, low),
        grid=(frames // chunk,),
        in_specs=[block, block],
        out_specs=pl.BlockSpec(memory_space=pl.ANY),
        out_shape=jax.ShapeDtypeStruct((groups, high - low, frames // LANES, 8, 128), F32),
        scratch_shapes=[
            pltpu.VMEM((2, width * (TURN_ROWS + 1) * 8, 128), F32),
            pltpu.SemaphoreType.DMA((2,)),
        ],
        compiler_params=pltpu.CompilerParams(vmem_limit_bytes=VMEM_LIMIT),
        cost_estimate=pl.CostEstimate(
            flops=0, bytes_accessed=frames * width * 12, transcendentals=0
        ),
        name="turn_first" if low == 0 else "turn_rest",
    )(signal, kernel)


def gather_channel(ref, which):
    groups, _, depth, _ = ref.shape
    tiles = LANES // 128
    flat = ref.reshape(groups * depth, 128)
    rows = groups * depth // 8
    return jnp.concatenate(
        [flat[pl.ds(2 * j + which, rows, stride=8), :] for j in range(tiles)], axis=1
    )


def scatter_channel(ref, slot, value, spare=0):
    tiles = LANES // 128
    for j in range(tiles):
        ref[pl.ds(8 * j + slot, value.shape[0], stride=8 * (tiles + spare)), :] = (
            value[:, j * 128 : (j + 1) * 128]
        )


def first_channels_kernel(skip_ref, data_ref, *rest):
    *table_refs, out_ref = rest
    c = pl.program_id(0)
    result = filter_channel(
        gather_channel(data_ref, 0), gather_channel(data_ref, 1), skip_ref[c],
        *table_refs,
    )
    scatter_channel(out_ref, c, result)


def last_channels_kernel(late, extra, skip_ref, data_ref, *rest):
    *table_refs, before_ref = rest[: len(rest) - 4 - extra]
    late_ref, early_ref, held_ref, sems = rest[-4:]
    c = pl.program_id(0)
    channel = c + FIRST_CHANNELS
    devices, tiles = late_ref.shape[0], late_ref.shape[1] + early_ref.shape[1] - 1
    per_row = LANES // 128
    rows = tiles // per_row
    shaped = held_ref.reshape(devices, rows, per_row + 1, 8, 128)
    load = pltpu.make_async_copy(before_ref, shaped.at[:, :, :per_row], sems.at[0])

    @pl.when(c == 0)
    def _():
        load.start()

    result = filter_channel(
        gather_channel(data_ref, 0), gather_channel(data_ref, 1),
        skip_ref[channel], *table_refs,
    )

    @pl.when(c == 0)
    def _():
        load.wait()

    scatter_channel(held_ref, channel, result, spare=1)

    @pl.when(c == pl.num_programs(0) - 1)
    def _():
        pairs = []
        for row in range(late // per_row, rows):
            at = row * per_row - late
            pairs.append((shaped.at[:, row, :per_row], late_ref.at[:, at : at + per_row]))
        for row in range(late // per_row):
            at = row * per_row
            count = min(per_row, late - 1 - at)
            pairs.append((shaped.at[:, row, :count], early_ref.at[:, at : at + count]))
        edge = shaped.at[:, late // per_row - 1, per_row - 1 : per_row]
        pairs.append((edge, late_ref.at[:, tiles - late : tiles - late + 1]))
        final = shaped.at[:, rows - 1, per_row - 1 : per_row]
        pairs.append((final.at[0 : devices - 1], early_ref.at[1:devices, late - 1 : late]))
        pairs.append((final.at[devices - 1 : devices], early_ref.at[0:1, late - 1 : late]))
        copies = [
            pltpu.make_async_copy(here, there, sems.at[1 + i])
            for i, (here, there) in enumerate(pairs)
        ]
        for copy in copies:
            copy.start()
        for copy in copies:
            copy.wait()


def filter_channels(data, skip, before, devices, late, ready=()):
    groups, channels, group_rows, _, _ = data.shape
    flat = data.reshape(groups, channels, group_rows * 8, 128)
    rows = groups * group_rows
    lane_tiles = LANES // 128
    tiles = rows * lane_tiles // devices
    held = tables(rows)
    held_shape = (rows * lane_tiles * 8, 128)

    def whole(array):
        return pl.BlockSpec(array.shape, lambda c: (0,) * array.ndim)

    in_specs = [
        pl.BlockSpec(memory_space=pltpu.SMEM),
        pl.BlockSpec(
            (groups, 1, group_rows * 8, 128), lambda c: (0, c, 0, 0)
        ),
    ] + [whole(t) for t in held]
    options = dict(
        grid=(channels,),
        compiler_params=pltpu.CompilerParams(vmem_limit_bytes=VMEM_LIMIT),
        cost_estimate=pl.CostEstimate(
            flops=channels * rows * LANES * 2048 * 3 * 3,
            bytes_accessed=channels * rows * LANES * 12,
            transcendentals=0,
        ),
    )
    if before is None:
        return pl.pallas_call(
            first_channels_kernel,
            in_specs=in_specs,
            out_specs=pl.BlockSpec(held_shape, lambda c: (0, 0)),
            out_shape=jax.ShapeDtypeStruct(held_shape, F32),
            name="filter_first",
            **options,
        )(skip, flat, *held)
    anywhere = pl.BlockSpec(memory_space=pl.ANY)
    return pl.pallas_call(
        functools.partial(last_channels_kernel, late, len(ready)),
        in_specs=in_specs + [anywhere] * (1 + len(ready)),
        out_specs=[anywhere, anywhere],
        out_shape=[
            jax.ShapeDtypeStruct((devices, tiles - late + 1, 8, 128), F32),
            jax.ShapeDtypeStruct((devices, late, 8, 128), F32),
        ],
        scratch_shapes=[
            pltpu.VMEM((rows * (lane_tiles + 1) * 8, 128), F32),
            pltpu.SemaphoreType.DMA((4 + tiles // lane_tiles,)),
        ],
        name="filter_last",
        **options,
    )(skip, flat, *held, before.reshape(devices, -1, lane_tiles, 8, 128), *ready)


def frames_by_channels(tile):
    paired = tile.reshape(tile.shape[0] // HEADS, HEADS, 8, 128)
    return jnp.concatenate(
        [jnp.transpose(paired[:, h].reshape(-1, 128), (1, 0)) for h in range(HEADS)], axis=1
    )


def late_kernel(conv_ref, edge_ref, gate_ref, edge_gate_ref, *rest):
    fixed, out_ref, window_ref, scratch = rest[:5], rest[5], rest[6], rest[7:]
    block = gate_ref.shape[0]
    reach = TAPS + 1

    @pl.when(pl.program_id(0) == 0)
    def _():
        window_ref[:reach, :] = frames_by_channels(edge_ref[:, 0]) * edge_gate_ref[...]

    @pl.when(pl.program_id(0) > 0)
    def _():
        window_ref[:reach, :] = window_ref[block : block + reach, :]

    for j in range(block // reach):
        span = slice(j * reach, (j + 1) * reach)
        window_ref[reach + j * reach : 2 * reach + j * reach, :] = (
            frames_by_channels(conv_ref[:, j]) * gate_ref[span, :]
        )
    mix_window(window_ref, fixed, scratch, out_ref)


def early_kernel(conv_ref, edge_ref, gate_ref, halo_ref, halo_gate_ref, *rest):
    fixed, out_ref, window_ref, scratch = rest[:5], rest[6], rest[7], rest[8:]
    block = gate_ref.shape[0]
    reach = TAPS + 1
    last = pl.program_id(0) == pl.num_programs(0) - 1

    @pl.when(pl.program_id(0) == 0)
    def _():
        window_ref[:reach, :] = frames_by_channels(halo_ref[:, 0]) * halo_gate_ref[...]

    @pl.when(pl.program_id(0) > 0)
    def _():
        window_ref[:reach, :] = window_ref[block : block + reach, :]

    count = block // reach
    for j in range(count):
        tile = conv_ref[:, j]
        if j == count - 1:
            tile = jnp.where(last, edge_ref[:, 0], tile)
        span = slice(j * reach, (j + 1) * reach)
        window_ref[reach + j * reach : 2 * reach + j * reach, :] = (
            frames_by_channels(tile) * gate_ref[span, :]
        )
    mix_window(window_ref, fixed, scratch, out_ref)


def tail_part(conv, late, gate_input, halo_gate, before, late_tiles, fixed):
    devices = conv.shape[0]
    frames, width = gate_input.shape
    reach = TAPS + 1
    block = 1024
    per_block = block // 128
    edge = late.shape[1] - 1
    first = before is not None

    def whole(array):
        return pl.BlockSpec(array.shape, lambda r: (0,) * array.ndim)

    start = 0 if first else late_tiles // per_block
    count = (late_tiles if first else edge) // per_block
    in_specs = [
        pl.BlockSpec((devices, per_block, 8, 128), lambda r: (0, r, 0, 0)),
        pl.BlockSpec((devices, 1, 8, 128), lambda r: (0, edge, 0, 0)),
        pl.BlockSpec((block, width), lambda r: (r + start, 0)),
    ]
    operands = [conv, late, gate_input]
    if first:
        ahead = late_tiles - 1
        in_specs += [pl.BlockSpec((devices, 1, 8, 128), lambda r: (0, ahead, 0, 0)), whole(halo_gate)]
        operands += [conv, halo_gate]
    else:
        in_specs += [pl.BlockSpec((reach, width), lambda r: (late_tiles - 1, 0))]
        operands += [gate_input]
    in_specs += [whole(array) for array in fixed]
    operands += fixed
    aliases = {}
    if first:
        aliases = {len(operands): 0}
        in_specs += [pl.BlockSpec(memory_space=pl.ANY)]
        operands += [before]
    hidden = fixed[3].shape[1]
    return pl.pallas_call(
        early_kernel if first else late_kernel,
        grid=(count,),
        in_specs=in_specs,
        out_specs=pl.BlockSpec((block, width), lambda r: (r + start, 0)),
        out_shape=jax.ShapeDtypeStruct(gate_input.shape, F32),
        input_output_aliases=aliases,
        scratch_shapes=mix_scratch(block, width, hidden),
        compiler_params=pltpu.CompilerParams(vmem_limit_bytes=VMEM_LIMIT),
        cost_estimate=pl.CostEstimate(
            flops=count * block * 3 * 2 * (2 * width * hidden + 3 * width * width),
            bytes_accessed=count * block * width * 12,
            transcendentals=count * block * hidden,
        ),
        name="mix_early" if first else "mix_late",
    )(*operands)


def owned_eight(signal, kernel, skip_here, gate_input, fixed):
    groups = lax.axis_size("tm")
    devices = groups * lax.axis_size("chan")
    reach = TAPS + 1
    late_tiles = 2 * (512 // 128)

    def enter(array):
        return lax.all_to_all(array, "tm", split_axis=0, concat_axis=0, tiled=True)

    def leave(array):
        return lax.all_to_all(array, ("tm", "chan"), split_axis=0, concat_axis=0, tiled=True)

    ring = [(i, i + 1) for i in range(devices - 1)]
    halo_gate = lax.ppermute(gate_input[-reach:], ("tm", "chan"), ring)
    one = turn(signal, kernel, groups, 0, FIRST_CHANNELS)
    two = turn(signal, kernel, groups, FIRST_CHANNELS, 8)
    before = filter_channels(enter(one), skip_here, None, devices, late_tiles)
    ready = (fixed[0], halo_gate)
    late, early = filter_channels(enter(two), skip_here, before, devices, late_tiles, ready)
    late = leave(late)
    early = leave(early)
    part = tail_part(late, late, gate_input, None, None, late_tiles, fixed)
    return tail_part(early, late, gate_input, halo_gate, part, late_tiles, fixed)


def on_device(
    signal, kernel, skip_gain, gate_input, tap_weight, norm_gain, up_weight, up_bias, down_weight
):
    groups = lax.axis_size("tm")
    pair = lax.axis_size("chan")
    frames_here, channels_here = signal.shape
    owned = channels_here // groups
    width = gate_input.shape[1]
    first_channel = lax.axis_index("chan") * channels_here + lax.axis_index("tm") * owned
    skip_here = lax.dynamic_slice_in_dim(skip_gain, first_channel, owned)
    fixed = fixed_operands(tap_weight, norm_gain, up_weight, up_bias, down_weight)
    window = frames_here * groups
    if owned == 8 and channels_here == 128 and pair == HEADS and window == 256 * LANES:
        if gate_input.shape[0] % 1024 == 0 and gate_input.shape[0] >= 2048:
            return owned_eight(signal, kernel, skip_here, gate_input, fixed)

    def enter(array):
        shaped = array.reshape(frames_here // LANES, LANES, groups, owned).transpose(2, 3, 0, 1)
        return lax.all_to_all(shaped, "tm", split_axis=0, concat_axis=0, tiled=True)

    filtered = long_filter(enter(signal), enter(kernel), skip_here, groups * pair)
    back = lax.all_to_all(filtered, ("tm", "chan"), split_axis=0, concat_axis=0, tiled=True)
    blocks = back.reshape(groups, pair, owned, -1, LANES).transpose(3, 1, 0, 2, 4)
    blocks = blocks.reshape(-1, width, LANES)
    reach = TAPS + 1
    last = blocks[-1, :, LANES - reach :].T * gate_input[-reach:]
    devices = groups * pair
    halo = lax.ppermute(last, ("tm", "chan"), [(i, i + 1) for i in range(devices - 1)])
    return tail(blocks, gate_input, halo, fixed)


def solution(mesh):
    placed = (
        P(("grp", "tm"), "chan"),
        P("tm", "chan"),
        P(),
        P(("grp", "tm", "chan"), None),
        P(),
        P(),
        P(),
        P(),
        P(),
    )
    return jax.shard_map(
        on_device,
        mesh=mesh,
        in_specs=placed,
        out_specs=P(("grp", "tm", "chan"), None),
        check_vma=False,
    )
```

```python
import functools
import math

import jax
import jax.numpy as jnp
import numpy as np
from jax import lax
from jax.experimental import pallas as pl
from jax.experimental.pallas import tpu as pltpu
from jax.sharding import PartitionSpec as P
import ml_dtypes

LANES = 512
RADIX = 4
SUB = LANES // RADIX
TAPS = 127
HEADS = 2
EPSILON = 1e-06
BF16 = jnp.bfloat16
F32 = jnp.float32
VMEM_LIMIT = 63 * 1024 * 1024


def table_split(table, axis, order):
    high = table.astype(ml_dtypes.bfloat16)
    low = (table - high.astype(np.float64)).astype(ml_dtypes.bfloat16)
    parts = {"h": high, "l": low}
    return np.concatenate([parts[name] for name in order], axis=axis)


@functools.lru_cache(maxsize=None)
def tables(rows):
    length = rows * LANES
    turn = 2.0 * math.pi
    n1 = np.arange(rows, dtype=np.float64)
    n2 = np.arange(LANES, dtype=np.float64)
    m = np.arange(SUB, dtype=np.float64)
    first = turn * np.outer(n1 + 0.25, n1) / rows
    enter = table_split(np.concatenate([np.cos(first), -np.sin(first)], axis=0), 1, "hl")
    leave = table_split(
        np.concatenate([np.cos(first.T), -np.sin(first.T)], axis=1) / length, 1, "hl"
    )
    twiddle = turn * np.outer(n1 + 0.25, n2) / length
    forward, backward = [], []
    for r in range(RADIX):
        phase = turn * np.outer(m, m / SUB + r / LANES)
        c, s = np.cos(phase), np.sin(phase)
        forward.append(table_split(np.block([[c, -s], [s, c]]), 0, "hl"))
        c, s = c.T, s.T
        backward.append(table_split(np.block([[c, s], [-s, c]]), 0, "hl"))
    return (
        enter,
        np.cos(twiddle).astype(np.float32),
        np.sin(twiddle).astype(np.float32),
        np.stack(forward),
        np.stack(backward),
        leave,
    )


def halves(value):
    high = value.astype(BF16)
    low = (value - high.astype(F32)).astype(BF16)
    return high, low


def split_cat(value, axis):
    high, low = halves(value)
    return jnp.concatenate([high, low, high], axis=axis)


def high_high_low(table, axis):
    size = table.shape[axis] // 2
    high = lax.slice_in_dim(table, 0, size, axis=axis)
    low = lax.slice_in_dim(table, size, 2 * size, axis=axis)
    return jnp.concatenate([high, high, low], axis=axis)


def dot(left, right):
    return jnp.dot(left, right, preferred_element_type=F32)


def filter_channel(signal, kernel, skip, enter_ref, cos_ref, sin_ref, forward_ref, backward_ref,
                   leave_ref):
    rows = cos_ref.shape[0]
    enter = high_high_low(enter_ref[...], 1)
    entered = [dot(enter, split_cat(value, 0)) for value in (signal, kernel)]
    spectra = []
    for turned in entered:
        real_in, imag_in = turned[:rows], turned[rows:]
        real = real_in * cos_ref[...] + imag_in * sin_ref[...]
        imag = imag_in * cos_ref[...] - real_in * sin_ref[...]
        r0, r1, r2, r3 = (real[:, b * SUB : (b + 1) * SUB] for b in range(RADIX))
        i0, i1, i2, i3 = (imag[:, b * SUB : (b + 1) * SUB] for b in range(RADIX))
        er, ei, fr, fi = r0 + r2, i0 + i2, r0 - r2, i0 - i2
        gr, gi, hr, hi = r1 + r3, i1 + i3, r1 - r3, i1 - i3
        spread = ((er + gr, ei + gi), (fr + hi, fi - hr), (er - gr, ei - gi), (fr - hi, fi + hr))
        spectra.append([
            dot(split_cat(jnp.concatenate(pair, axis=1), 1), high_high_low(forward_ref[r], 0))
            for r, pair in enumerate(spread)
        ])
    products = []
    for s, k in zip(*spectra):
        sr, si = s[:, :SUB], s[:, SUB:]
        kr, ki = k[:, :SUB], k[:, SUB:]
        product = jnp.concatenate([sr * kr - si * ki, sr * ki + si * kr], axis=1)
        products.append(split_cat(product, 1))
    back = []
    for r in range(RADIX):
        turned = dot(products[r], high_high_low(backward_ref[r], 0))
        back.append((turned[:, :SUB], turned[:, SUB:]))
    (r0, i0), (r1, i1), (r2, i2), (r3, i3) = back
    er, ei, fr, fi = r0 + r2, i0 + i2, r0 - r2, i0 - i2
    gr, gi, hr, hi = r1 + r3, i1 + i3, r1 - r3, i1 - i3
    real = jnp.concatenate([er + gr, fr - hi, er - gr, fr + hi], axis=1)
    imag = jnp.concatenate([ei + gi, fi + hr, ei - gi, fi - hr], axis=1)
    turned = jnp.concatenate(
        [real * cos_ref[...] - imag * sin_ref[...], imag * cos_ref[...] + real * sin_ref[...]],
        axis=0,
    )
    return dot(high_high_low(leave_ref[...], 1), split_cat(turned, 0)) + skip * signal


def filter_kernel(
    skip_ref, signal_ref, kernel_ref, enter_ref, cos_ref, sin_ref, forward_ref, backward_ref,
    leave_ref, out_ref,
):
    rows = cos_ref.shape[0]
    result = filter_channel(
        signal_ref[...].reshape(rows, LANES), kernel_ref[...].reshape(rows, LANES),
        skip_ref[pl.program_id(0)], enter_ref, cos_ref, sin_ref, forward_ref, backward_ref,
        leave_ref,
    )
    out_ref[...] = result.reshape(out_ref.shape)


def long_filter(signal, kernel, skip, out_groups):
    groups, channels, group_rows, _ = signal.shape
    rows = groups * group_rows
    straight = group_rows % 8 == 0 and (rows // out_groups) % 8 == 0
    in_block = (groups, 1, group_rows, LANES)
    out_shape = (out_groups, channels, rows // out_groups, LANES)
    if not straight:
        signal = signal.transpose(1, 0, 2, 3).reshape(1, channels, rows, LANES)
        kernel = kernel.transpose(1, 0, 2, 3).reshape(1, channels, rows, LANES)
        in_block = (1, 1, rows, LANES)
        out_shape = (1, channels, rows, LANES)
    out_block = (out_shape[0], 1) + out_shape[2:]

    def along(c):
        return (0, c, 0, 0)

    def whole(array):
        return pl.BlockSpec(array.shape, lambda c: (0,) * array.ndim)

    held = tables(rows)
    result = pl.pallas_call(
        filter_kernel,
        grid=(channels,),
        in_specs=[
            pl.BlockSpec(memory_space=pltpu.SMEM),
            pl.BlockSpec(in_block, along),
            pl.BlockSpec(in_block, along),
        ]
        + [whole(table) for table in held],
        out_specs=pl.BlockSpec(out_block, along),
        out_shape=jax.ShapeDtypeStruct(out_shape, F32),
        compiler_params=pltpu.CompilerParams(vmem_limit_bytes=VMEM_LIMIT),
        cost_estimate=pl.CostEstimate(
            flops=channels * rows * LANES * 2048 * 3 * 3,
            bytes_accessed=channels * rows * LANES * 12,
            transcendentals=0,
        ),
        name="long_filter",
    )(skip, signal, kernel, *held)
    if not straight:
        result = result.reshape(channels, out_groups, rows // out_groups, LANES)
        result = result.transpose(1, 0, 2, 3)
    return result


def split_weights(tap_ref, up_ref, down_ref, taps_ref, ups_ref, downs_ref):
    def stacked(weight):
        high, low = halves(weight)
        return jnp.concatenate([high, high, low], axis=0)

    taps_ref[...] = stacked(tap_ref[...])
    chunks, _, chunk = ups_ref.shape
    for n in range(chunks):
        span = slice(n * chunk, (n + 1) * chunk)
        ups_ref[n] = stacked(up_ref[:, span])
        downs_ref[n] = stacked(down_ref[span, :])


def mix_block(window_ref, gain_ref, bias_ref, out_ref, high_ref, low_ref, mix_ref, taps_ref, ups_ref,
              downs_ref):
    block, width = out_ref.shape
    reach = TAPS + 1
    head_width = width // HEADS
    high, low = halves(window_ref[...])
    high_ref[...] = high
    low_ref[...] = low
    taps = dot(
        jnp.concatenate([high[reach:], low[reach:], high[reach:]], axis=1), taps_ref[...]
    )
    for b in range(block // reach):
        for h in range(HEADS):
            own = taps[b * reach : (b + 1) * reach, h * reach : (h + 1) * reach]
            band = jnp.concatenate([own, jnp.zeros_like(own)], axis=1)
            band = pltpu.roll(band, 1, 1, stride=1, stride_axis=0)
            near_rows = slice(b * reach, (b + 2) * reach)
            columns = slice(h * head_width, (h + 1) * head_width)
            near_high = high_ref[near_rows, columns]
            near_low = low_ref[near_rows, columns]
            mix_ref[b * reach : (b + 1) * reach, columns] = dot(
                split_cat(band, 1), jnp.concatenate([near_high, near_high, near_low], axis=0)
            )
    mixed = mix_ref[...]
    mean_square = jnp.mean(mixed * mixed, axis=1, keepdims=True)
    normed = split_cat(mixed * lax.rsqrt(mean_square + EPSILON) * gain_ref[...], 1)
    total = mixed
    chunks, _, chunk = ups_ref.shape
    scale = math.sqrt(2.0 / math.pi)
    for n in range(chunks):
        raised = dot(normed, ups_ref[n]) + bias_ref[:, n * chunk : (n + 1) * chunk]
        inner = raised * (scale + (scale * 0.044715) * (raised * raised))
        half = 0.5 * raised
        total = total + dot(split_cat(half + half * jnp.tanh(inner), 1), downs_ref[n])
    out_ref[...] = total


def mix_scratch(block, width, hidden):
    reach = TAPS + 1
    chunk = 512 if hidden % 512 == 0 else hidden
    return [
        pltpu.VMEM((block + reach, width), F32),
        pltpu.VMEM((block + reach, width), BF16),
        pltpu.VMEM((block + reach, width), BF16),
        pltpu.VMEM((block, width), F32),
        pltpu.VMEM((3 * width, HEADS * reach), BF16),
        pltpu.VMEM((hidden // chunk, 3 * width, chunk), BF16),
        pltpu.VMEM((hidden // chunk, 3 * chunk, width), BF16),
    ]


def mix_window(window_ref, fixed, scratch, out_ref):
    tap_ref, gain_ref, up_ref, bias_ref, down_ref = fixed
    weights = scratch[3:]

    @pl.when(pl.program_id(0) == 0)
    def _():
        split_weights(tap_ref, up_ref, down_ref, *weights)

    mix_block(window_ref, gain_ref, bias_ref, out_ref, *scratch)


def mix_kernel(conv_ref, gate_ref, halo_ref, *rest):
    fixed, out_ref, window_ref, scratch = rest[:5], rest[5], rest[6], rest[7:]
    block = gate_ref.shape[0]
    reach = TAPS + 1

    @pl.when(pl.program_id(0) == 0)
    def _():
        window_ref[:reach, :] = halo_ref[...]

    @pl.when(pl.program_id(0) > 0)
    def _():
        window_ref[:reach, :] = window_ref[block : block + reach, :]

    window_ref[reach:, :] = jnp.transpose(conv_ref[0], (1, 0)) * gate_ref[...]
    mix_window(window_ref, fixed, scratch, out_ref)


def fixed_operands(tap_weight, norm_gain, up_weight, up_bias, down_weight):
    width = tap_weight.shape[0]
    taps = tap_weight.reshape(width, HEADS, TAPS)[:, :, ::-1]
    taps = jnp.pad(taps, ((0, 0), (0, 0), (1, 0))).reshape(width, HEADS * (TAPS + 1))
    return (
        taps,
        norm_gain.reshape(1, -1),
        up_weight,
        up_bias.reshape(1, -1),
        down_weight,
    )


def tail(conv_blocks, gate_input, halo, fixed):
    count, width, block = conv_blocks.shape
    reach = TAPS + 1
    hidden = fixed[3].shape[1]

    def whole(array):
        return pl.BlockSpec(array.shape, lambda r: (0,) * array.ndim)

    return pl.pallas_call(
        mix_kernel,
        grid=(count,),
        in_specs=[
            pl.BlockSpec((1, width, block), lambda r: (r, 0, 0)),
            pl.BlockSpec((block, width), lambda r: (r, 0)),
            whole(halo),
        ]
        + [whole(array) for array in fixed],
        out_specs=pl.BlockSpec((block, width), lambda r: (r, 0)),
        out_shape=jax.ShapeDtypeStruct(gate_input.shape, F32),
        scratch_shapes=mix_scratch(block, width, hidden),
        compiler_params=pltpu.CompilerParams(vmem_limit_bytes=VMEM_LIMIT),
        cost_estimate=pl.CostEstimate(
            flops=count * block * 3 * 2 * (2 * width * hidden + 3 * width * width),
            bytes_accessed=count * block * width * 12,
            transcendentals=count * block * hidden,
        ),
        name="mix_and_mlp",
    )(conv_blocks, gate_input, halo, *fixed)


FIRST_CHANNELS = 6
TURN_ROWS = 8


def turn_kernel(signal_ref, kernel_ref, first_ref, second_ref, held_ref, sems):
    groups, early = first_ref.shape[:2]
    rows = signal_ref.shape[0] // LANES
    step, steps = pl.program_id(0), pl.num_programs(0)
    slot = step % 2

    def copies(at, slot):
        shaped = held_ref.at[slot].reshape(groups, 8, rows + 1, 8, 128)
        there = pl.ds(at * rows, rows)
        return (
            pltpu.make_async_copy(
                shaped.at[:, :early, :rows], first_ref.at[:, :, there], sems.at[slot, 0]
            ),
            pltpu.make_async_copy(
                shaped.at[:, early:, :rows], second_ref.at[:, :, there], sems.at[slot, 1]
            ),
        )

    @pl.when(step >= 2)
    def _():
        for copy in copies(step - 2, slot):
            copy.wait()

    for row in range(rows):
        for j in range(LANES // 128):
            span = slice(row * LANES + j * 128, row * LANES + (j + 1) * 128)
            for which, ref in enumerate((signal_ref, kernel_ref)):
                turned = jnp.transpose(ref[span, :], (1, 0))
                place = row * 8 + j * 2 + which
                held_ref[slot, pl.ds(place, turned.shape[0], stride=(rows + 1) * 8), :] = turned
    for copy in copies(step, slot):
        copy.start()

    @pl.when(step == steps - 1)
    def _():
        for copy in copies(step, slot):
            copy.wait()

    @pl.when((step == steps - 1) & (step >= 1))
    def _():
        for copy in copies(step - 1, 1 - slot):
            copy.wait()


def turn(signal, kernel, groups):
    frames, width = signal.shape
    chunk = TURN_ROWS * LANES
    rows = frames // LANES
    block = pl.BlockSpec((chunk, width), lambda i: (i, 0))
    counts = (FIRST_CHANNELS, 8 - FIRST_CHANNELS)
    return pl.pallas_call(
        turn_kernel,
        grid=(frames // chunk,),
        in_specs=[block, block],
        out_specs=[pl.BlockSpec(memory_space=pl.ANY)] * 2,
        out_shape=[jax.ShapeDtypeStruct((groups, n, rows, 8, 128), F32) for n in counts],
        scratch_shapes=[
            pltpu.VMEM((2, width * (TURN_ROWS + 1) * 8, 128), F32),
            pltpu.SemaphoreType.DMA((2, 2)),
        ],
        compiler_params=pltpu.CompilerParams(vmem_limit_bytes=VMEM_LIMIT),
        name="turn",
    )(signal, kernel)


def gather_channel(ref, which):
    groups, _, depth, _ = ref.shape
    tiles = LANES // 128
    flat = ref.reshape(groups * depth, 128)
    rows = groups * depth // 8
    return jnp.concatenate(
        [flat[pl.ds(2 * j + which, rows, stride=8), :] for j in range(tiles)], axis=1
    )


def scatter_channel(ref, slot, value, spare=0):
    tiles = LANES // 128
    for j in range(tiles):
        ref[pl.ds(8 * j + slot, value.shape[0], stride=8 * (tiles + spare)), :] = (
            value[:, j * 128 : (j + 1) * 128]
        )


def first_channels_kernel(skip_ref, data_ref, *rest):
    *table_refs, out_ref = rest
    c = pl.program_id(0)
    result = filter_channel(
        gather_channel(data_ref, 0), gather_channel(data_ref, 1), skip_ref[c],
        *table_refs,
    )
    scatter_channel(out_ref, c, result)


def last_channels_kernel(late, extra, skip_ref, data_ref, *rest):
    *table_refs, before_ref = rest[: len(rest) - 4 - extra]
    late_ref, early_ref, held_ref, sems = rest[-4:]
    c = pl.program_id(0)
    channel = c + FIRST_CHANNELS
    devices, tiles = late_ref.shape[0], late_ref.shape[1] + early_ref.shape[1] - 1
    per_row = LANES // 128
    rows = tiles // per_row
    shaped = held_ref.reshape(devices, rows, per_row + 1, 8, 128)
    load = pltpu.make_async_copy(before_ref, shaped.at[:, :, :per_row], sems.at[0])

    @pl.when(c == 0)
    def _():
        load.start()

    result = filter_channel(
        gather_channel(data_ref, 0), gather_channel(data_ref, 1),
        skip_ref[channel], *table_refs,
    )

    @pl.when(c == 0)
    def _():
        load.wait()

    scatter_channel(held_ref, channel, result, spare=1)

    @pl.when(c == pl.num_programs(0) - 1)
    def _():
        pairs = []
        for row in range(late // per_row, rows):
            at = row * per_row - late
            pairs.append((shaped.at[:, row, :per_row], late_ref.at[:, at : at + per_row]))
        for row in range(late // per_row):
            at = row * per_row
            count = min(per_row, late - 1 - at)
            pairs.append((shaped.at[:, row, :count], early_ref.at[:, at : at + count]))
        edge = shaped.at[:, late // per_row - 1, per_row - 1 : per_row]
        pairs.append((edge, late_ref.at[:, tiles - late : tiles - late + 1]))
        final = shaped.at[:, rows - 1, per_row - 1 : per_row]
        pairs.append((final.at[0 : devices - 1], early_ref.at[1:devices, late - 1 : late]))
        pairs.append((final.at[devices - 1 : devices], early_ref.at[0:1, late - 1 : late]))
        copies = [
            pltpu.make_async_copy(here, there, sems.at[1 + i])
            for i, (here, there) in enumerate(pairs)
        ]
        for copy in copies:
            copy.start()
        for copy in copies:
            copy.wait()


def filter_channels(data, skip, before, devices, late, ready=()):
    groups, channels, group_rows, _, _ = data.shape
    flat = data.reshape(groups, channels, group_rows * 8, 128)
    rows = groups * group_rows
    lane_tiles = LANES // 128
    tiles = rows * lane_tiles // devices
    held = tables(rows)
    held_shape = (rows * lane_tiles * 8, 128)

    def whole(array):
        return pl.BlockSpec(array.shape, lambda c: (0,) * array.ndim)

    in_specs = [
        pl.BlockSpec(memory_space=pltpu.SMEM),
        pl.BlockSpec(
            (groups, 1, group_rows * 8, 128), lambda c: (0, c, 0, 0)
        ),
    ] + [whole(t) for t in held]
    options = dict(
        grid=(channels,),
        compiler_params=pltpu.CompilerParams(vmem_limit_bytes=VMEM_LIMIT),
        cost_estimate=pl.CostEstimate(
            flops=channels * rows * LANES * 2048 * 3 * 3,
            bytes_accessed=channels * rows * LANES * 12,
            transcendentals=0,
        ),
    )
    if before is None:
        return pl.pallas_call(
            first_channels_kernel,
            in_specs=in_specs,
            out_specs=pl.BlockSpec(held_shape, lambda c: (0, 0)),
            out_shape=jax.ShapeDtypeStruct(held_shape, F32),
            name="filter_first",
            **options,
        )(skip, flat, *held)
    anywhere = pl.BlockSpec(memory_space=pl.ANY)
    return pl.pallas_call(
        functools.partial(last_channels_kernel, late, len(ready)),
        in_specs=in_specs + [anywhere] * (1 + len(ready)),
        out_specs=[anywhere, anywhere],
        out_shape=[
            jax.ShapeDtypeStruct((devices, tiles - late + 1, 8, 128), F32),
            jax.ShapeDtypeStruct((devices, late, 8, 128), F32),
        ],
        scratch_shapes=[
            pltpu.VMEM((rows * (lane_tiles + 1) * 8, 128), F32),
            pltpu.SemaphoreType.DMA((4 + tiles // lane_tiles,)),
        ],
        name="filter_last",
        **options,
    )(skip, flat, *held, before.reshape(devices, -1, lane_tiles, 8, 128), *ready)


def frames_by_channels(tile):
    paired = tile.reshape(tile.shape[0] // HEADS, HEADS, 8, 128)
    return jnp.concatenate(
        [jnp.transpose(paired[:, h].reshape(-1, 128), (1, 0)) for h in range(HEADS)], axis=1
    )


def late_kernel(conv_ref, edge_ref, gate_ref, edge_gate_ref, *rest):
    fixed, out_ref, window_ref, scratch = rest[:5], rest[5], rest[6], rest[7:]
    block = gate_ref.shape[0]
    reach = TAPS + 1

    @pl.when(pl.program_id(0) == 0)
    def _():
        window_ref[:reach, :] = frames_by_channels(edge_ref[:, 0]) * edge_gate_ref[...]

    @pl.when(pl.program_id(0) > 0)
    def _():
        window_ref[:reach, :] = window_ref[block : block + reach, :]

    for j in range(block // reach):
        span = slice(j * reach, (j + 1) * reach)
        window_ref[reach + j * reach : 2 * reach + j * reach, :] = (
            frames_by_channels(conv_ref[:, j]) * gate_ref[span, :]
        )
    mix_window(window_ref, fixed, scratch, out_ref)


def early_kernel(conv_ref, edge_ref, gate_ref, halo_ref, halo_gate_ref, *rest):
    fixed, out_ref, window_ref, scratch = rest[:5], rest[6], rest[7], rest[8:]
    block = gate_ref.shape[0]
    reach = TAPS + 1
    last = pl.program_id(0) == pl.num_programs(0) - 1

    @pl.when(pl.program_id(0) == 0)
    def _():
        window_ref[:reach, :] = frames_by_channels(halo_ref[:, 0]) * halo_gate_ref[...]

    @pl.when(pl.program_id(0) > 0)
    def _():
        window_ref[:reach, :] = window_ref[block : block + reach, :]

    count = block // reach
    for j in range(count):
        tile = conv_ref[:, j]
        if j == count - 1:
            tile = jnp.where(last, edge_ref[:, 0], tile)
        span = slice(j * reach, (j + 1) * reach)
        window_ref[reach + j * reach : 2 * reach + j * reach, :] = (
            frames_by_channels(tile) * gate_ref[span, :]
        )
    mix_window(window_ref, fixed, scratch, out_ref)


def tail_part(conv, late, gate_input, halo_gate, before, late_tiles, fixed):
    devices = conv.shape[0]
    frames, width = gate_input.shape
    reach = TAPS + 1
    block = 1024
    per_block = block // 128
    edge = late.shape[1] - 1
    first = before is not None

    def whole(array):
        return pl.BlockSpec(array.shape, lambda r: (0,) * array.ndim)

    start = 0 if first else late_tiles // per_block
    count = (late_tiles if first else edge) // per_block
    in_specs = [
        pl.BlockSpec((devices, per_block, 8, 128), lambda r: (0, r, 0, 0)),
        pl.BlockSpec((devices, 1, 8, 128), lambda r: (0, edge, 0, 0)),
        pl.BlockSpec((block, width), lambda r: (r + start, 0)),
    ]
    operands = [conv, late, gate_input]
    if first:
        ahead = late_tiles - 1
        in_specs += [pl.BlockSpec((devices, 1, 8, 128), lambda r: (0, ahead, 0, 0)), whole(halo_gate)]
        operands += [conv, halo_gate]
    else:
        in_specs += [pl.BlockSpec((reach, width), lambda r: (late_tiles - 1, 0))]
        operands += [gate_input]
    in_specs += [whole(array) for array in fixed]
    operands += fixed
    aliases = {}
    if first:
        aliases = {len(operands): 0}
        in_specs += [pl.BlockSpec(memory_space=pl.ANY)]
        operands += [before]
    hidden = fixed[3].shape[1]
    return pl.pallas_call(
        early_kernel if first else late_kernel,
        grid=(count,),
        in_specs=in_specs,
        out_specs=pl.BlockSpec((block, width), lambda r: (r + start, 0)),
        out_shape=jax.ShapeDtypeStruct(gate_input.shape, F32),
        input_output_aliases=aliases,
        scratch_shapes=mix_scratch(block, width, hidden),
        compiler_params=pltpu.CompilerParams(vmem_limit_bytes=VMEM_LIMIT),
        cost_estimate=pl.CostEstimate(
            flops=count * block * 3 * 2 * (2 * width * hidden + 3 * width * width),
            bytes_accessed=count * block * width * 12,
            transcendentals=count * block * hidden,
        ),
        name="mix_early" if first else "mix_late",
    )(*operands)


def owned_eight(signal, kernel, skip_here, gate_input, fixed):
    groups = lax.axis_size("tm")
    devices = groups * lax.axis_size("chan")
    reach = TAPS + 1
    late_tiles = 2 * (512 // 128)

    def enter(array):
        return lax.all_to_all(array, "tm", split_axis=0, concat_axis=0, tiled=True)

    def leave(array):
        return lax.all_to_all(array, ("tm", "chan"), split_axis=0, concat_axis=0, tiled=True)

    ring = [(i, i + 1) for i in range(devices - 1)]
    halo_gate = lax.ppermute(gate_input[-reach:], ("tm", "chan"), ring)
    one, two = turn(signal, kernel, groups)
    before = filter_channels(enter(one), skip_here, None, devices, late_tiles)
    ready = (fixed[0], halo_gate)
    late, early = filter_channels(enter(two), skip_here, before, devices, late_tiles, ready)
    late = leave(late)
    early = leave(early)
    part = tail_part(late, late, gate_input, None, None, late_tiles, fixed)
    return tail_part(early, late, gate_input, halo_gate, part, late_tiles, fixed)


def on_device(
    signal, kernel, skip_gain, gate_input, tap_weight, norm_gain, up_weight, up_bias, down_weight
):
    groups = lax.axis_size("tm")
    pair = lax.axis_size("chan")
    frames_here, channels_here = signal.shape
    owned = channels_here // groups
    width = gate_input.shape[1]
    first_channel = lax.axis_index("chan") * channels_here + lax.axis_index("tm") * owned
    skip_here = lax.dynamic_slice_in_dim(skip_gain, first_channel, owned)
    fixed = fixed_operands(tap_weight, norm_gain, up_weight, up_bias, down_weight)
    window = frames_here * groups
    if owned == 8 and channels_here == 128 and pair == HEADS and window == 256 * LANES:
        if gate_input.shape[0] % 1024 == 0 and gate_input.shape[0] >= 2048:
            return owned_eight(signal, kernel, skip_here, gate_input, fixed)

    def enter(array):
        shaped = array.reshape(frames_here // LANES, LANES, groups, owned).transpose(2, 3, 0, 1)
        return lax.all_to_all(shaped, "tm", split_axis=0, concat_axis=0, tiled=True)

    filtered = long_filter(enter(signal), enter(kernel), skip_here, groups * pair)
    back = lax.all_to_all(filtered, ("tm", "chan"), split_axis=0, concat_axis=0, tiled=True)
    blocks = back.reshape(groups, pair, owned, -1, LANES).transpose(3, 1, 0, 2, 4)
    blocks = blocks.reshape(-1, width, LANES)
    reach = TAPS + 1
    last = blocks[-1, :, LANES - reach :].T * gate_input[-reach:]
    devices = groups * pair
    halo = lax.ppermute(last, ("tm", "chan"), [(i, i + 1) for i in range(devices - 1)])
    return tail(blocks, gate_input, halo, fixed)


def solution(mesh):
    placed = (
        P(("grp", "tm"), "chan"),
        P("tm", "chan"),
        P(),
        P(("grp", "tm", "chan"), None),
        P(),
        P(),
        P(),
        P(),
        P(),
    )
    return jax.shard_map(
        on_device,
        mesh=mesh,
        in_specs=placed,
        out_specs=P(("grp", "tm", "chan"), None),
        check_vma=False,
    )
```
